256 devices in a mesh: bucket: 64 (over y, z, core), nbr: 4 (over x).
Axes of the slice: x: 4, y: 4, z: 8, core: 2. Of those that a mesh axis runs over, the one named last changes fastest.
Arguments:
- embeddings: bfloat16 [1024, 64, 1152], P('bucket'), may hold values from -6 to 6
- prior_scores: bfloat16 [1024, 64, 128], P('bucket'), may hold values from -6 to 6
- frame_valid: int32 [1024, 64], P('bucket'), may hold values 0 or 1
- neighbour_ids: int32 [1024, 32], P('bucket', 'nbr'), may hold values from 0 to 1023, as said below
- neighbour_count: int32 [1024], P('bucket'), may hold values from 1 to 32, as said below
- block_home: int32 [1024], replicated, may hold values from 0 to 1023, as said below
Outputs:
- spread_scores: bfloat16 [1024, 64, 128], P(('bucket', 'nbr'))
The draws below stay inside these ranges and needn't reach their ends.
Inputs may be any that keep to these rules, and one draw needn't show every extreme that they name: block_home is a permutation of 0 to 1023; the block stored at position q lies in bucket q // 16. `neighbour_ids`: over the 16 rows of one bucket and the 8 columns of one index of nbr, at most 2 entries name blocks stored in any one bucket, and one bucket is named exactly 2 times by every such group. No entry names its own row's block; entries may repeat. `neighbour_count`: some block has all 32 entries.
All inputs are finite; a program needn't handle non-finite values. No bound on the sum of `frame_valid` on one device may be relied on, other than what follows from the above.
Results may differ from the reference program's by a relative error of at most 0.011.
Values may be sent and summed in bfloat16 or wider, within the bound.
No kernel may reach another device: no remote copies, remote signals or barrier semaphores. Data moves between devices by JAX's collectives and lax.ppermute only.
A program may use at most 320 MiB of HBM per device.

```python
import math
import jax
import jax.numpy as jnp
from jax import lax

D = 1152
SCORES = 128
FRAMES = 64
BLK_DEV = 16
NBR_DEV = 8
BUCKETS = 64
BLOCKS = 1024
NBR = 32
REQS = 128
CAP = 2


def home_table(key):
    return jax.random.permutation(jax.random.fold_in(key, 11), BLOCKS).astype(jnp.int32)


def draw_block_home(key, part):
    return home_table(key)


def draw_neighbour_ids(key, part):
    stored = home_table(key)
    key = jax.random.fold_in(key, 2)
    logical = jnp.argsort(stored).astype(jnp.int32)
    groups = NBR // NBR_DEV
    hottest = jax.random.randint(jax.random.fold_in(key, 5), (), 0, BUCKETS).astype(jnp.int32)
    tickets = jnp.arange((BUCKETS - 1) * CAP, dtype=jnp.int32) // CAP
    tickets = jnp.where(tickets >= hottest, tickets + 1, tickets)

    def one_group(subkey, bucket):
        key_pick, second, key_slot = jax.random.split(subkey, 3)
        picked = jax.random.permutation(key_pick, tickets)[:REQS - CAP]
        owners = jnp.concatenate([jnp.full((CAP,), hottest, jnp.int32), picked])
        owners = jax.random.permutation(second, owners)
        slot_pick = jax.random.randint(key_slot, (REQS,), 0, BLK_DEV).astype(jnp.int32)
        row_index = jnp.arange(REQS, dtype=jnp.int32) // NBR_DEV
        slot_pick = jnp.where((owners == bucket) & (slot_pick == row_index), (slot_pick + 1) % BLK_DEV, slot_pick)
        return logical[owners * BLK_DEV + slot_pick].reshape(BLK_DEV, NBR_DEV)
    subkeys = jax.random.split(jax.random.fold_in(key, 7), BUCKETS * groups)
    bucket_of = jnp.arange(BUCKETS * groups, dtype=jnp.int32) // groups
    neighbour_lists = jax.vmap(one_group)(subkeys, bucket_of)
    neighbour_lists = neighbour_lists.reshape(BUCKETS, groups, BLK_DEV, NBR_DEV).transpose(0, 2, 1, 3)
    return neighbour_lists.reshape(BLOCKS, NBR).astype(jnp.int32)


def draw_neighbour_count(key, part):
    key = jax.random.fold_in(key, 3)
    counts = jax.random.randint(jax.random.fold_in(key, 1), (BLOCKS,), 1, NBR + 1).astype(jnp.int32)
    fullest = jax.random.randint(jax.random.fold_in(key, 2), (), 0, BLOCKS)
    return counts.at[fullest].set(NBR).astype(jnp.int32)


def plant(result, own_key, low, high):
    longest = result.shape.index(max(result.shape))
    spots = []
    for shift in (0, 1):
        where = [jax.random.randint(jax.random.fold_in(own_key, axis), (), 0, length) for axis, length in enumerate(result.shape)]
        where[longest] = (where[longest] + shift) % result.shape[longest]
        spots.append(tuple(where))
    return result.at[spots[0]].set(low).at[spots[1]].set(high)


def levels(rng, shape, cuts, least, high):
    gain, own = 1.0, jax.random.fold_in(rng, 6)
    for dim, parts in cuts:
        heights = jnp.exp(jax.random.uniform(jax.random.fold_in(own, dim), (parts,), jnp.float32, least / len(cuts), high / len(cuts)))
        gain = gain * jnp.repeat(heights, shape[dim] // parts).reshape([-1 if axis == dim else 1 for axis in range(len(shape))])
    return gain


def gaussian(own_key, shape, spread, limit, cuts=(), kind=jnp.bfloat16):
    level = levels(own_key, shape, cuts, -0.22, 0.18) if cuts else 1.0
    drawn = jax.random.normal(own_key, shape, jnp.float32) * spread * level
    return jnp.minimum(jnp.maximum(drawn, -limit), limit).astype(kind)


def setup_inputs(seed: int = 0) -> dict:
    seeds = jax.random.split(jax.random.key(seed), 7)
    embeddings = gaussian(seeds[0], (BLOCKS, FRAMES, D), 1.0, 6.0, ((0, 64),))
    prior_scores = gaussian(seeds[1], (BLOCKS, FRAMES, SCORES), 1.0, 6.0, ((0, 64),))
    frame_valid = plant((jax.random.randint(seeds[2], (BLOCKS, FRAMES), 0, 8) < 7).astype(jnp.int32), jax.random.fold_in(seeds[2], 1), 0, 1)
    neighbour_ids = draw_neighbour_ids(jax.random.fold_in(seeds[6], 71), 0)
    neighbour_count = draw_neighbour_count(jax.random.fold_in(seeds[6], 71), 0)
    block_home = draw_block_home(jax.random.fold_in(seeds[6], 71), 0)
    return {"embeddings": embeddings, "prior_scores": prior_scores, "frame_valid": frame_valid, "neighbour_ids": neighbour_ids, "neighbour_count": neighbour_count, "block_home": block_home}


epsilon = 1e-06
keep_share = 0.9

def normalize(values):
    floats = values.astype(jnp.float32)
    return (floats * lax.rsqrt(lax.optimization_barrier(jnp.sum(floats * floats, axis=-1, keepdims=True)) + epsilon)).astype(jnp.bfloat16)

def reference(embeddings, prior_scores, frame_valid, neighbour_ids, neighbour_count, block_home):
    normed = normalize(embeddings)
    sharpness = 2.0 * math.sqrt(D)
    valid_float = frame_valid.astype(jnp.float32)
    target = block_home[neighbour_ids].astype(jnp.int32)
    in_list = (jnp.arange(NBR, dtype=jnp.int32)[None, :] < neighbour_count[:, None]).astype(jnp.float32)
    off_diagonal = 1.0 - jnp.eye(FRAMES, dtype=jnp.float32)

    def advance(scores):

        def one_block(position):
            queries = normed[position]
            keys = normed[target[position]].astype(jnp.float32)
            affinity = jnp.einsum('fd,jgd->jfg', queries.astype(jnp.float32), keys, precision=lax.Precision.HIGHEST)
            weights = jnp.exp(sharpness * affinity) * valid_float[target[position]][:, None, :] * in_list[position][:, None, None]
            weights = lax.optimization_barrier(weights.astype(jnp.bfloat16)).astype(jnp.float32)
            own_affinity = jnp.dot(queries, queries.T, preferred_element_type=jnp.float32)
            own = jnp.exp(sharpness * own_affinity) * valid_float[position][None, :] * off_diagonal
            own = lax.optimization_barrier(own.astype(jnp.bfloat16)).astype(jnp.float32)
            key_scores = scores[target[position]].astype(jnp.float32)
            numerator = jnp.einsum('jfg,jgc->fc', weights, key_scores, precision=lax.Precision.HIGHEST)
            numerator = numerator + jnp.dot(own, scores[position].astype(jnp.float32), precision=lax.Precision.HIGHEST)
            denominator = 1.0 + lax.optimization_barrier(jnp.sum(weights, axis=(0, 2))) + lax.optimization_barrier(jnp.sum(own, axis=1))
            mixed = keep_share * numerator / denominator[:, None] + (1.0 - keep_share) * prior_scores[position].astype(jnp.float32)
            return mixed.astype(jnp.bfloat16)
        return lax.map(one_block, jnp.arange(BLOCKS, dtype=jnp.int32))
    round_one = advance(prior_scores)
    return advance(round_one)
```

```python
import math

import jax
import jax.numpy as jnp
from jax import lax
from jax.experimental import pallas as pl
from jax.experimental.pallas import tpu as pltpu
from jax.sharding import Mesh
from jax.sharding import PartitionSpec as P

epsilon = 1e-06
keep_share = 0.9

NY, NZ, NC, NX = 4, 8, 2, 4
ROWS = 16
FRAMES = 64
FEAT = 1152
CH = 128
PART = ROWS // NX
QBLOCKS = NY * ROWS
KBLOCKS = NZ * NC * PART
PAIRS = 512
UNROLL = 4
WIDE = FEAT + 2 * CH
PIECE = PART * FRAMES
SEND = PIECE + 16
LIST = 640
COUNT_AT = 600
SPARE = QBLOCKS
VMEM = 56 * 1024 * 1024
sharpness = 2.0 * math.sqrt(FEAT)


def shift(value, axis, step):
    size = lax.axis_size(axis)
    return lax.ppermute(value, axis, [(i, (i + step) % size) for i in range(size)])


def list_kernel(codes, out):
    def step(i, count):
        code = codes[i]
        out[count] = code
        return count + jnp.where(code >= 0, 1, 0)

    def eight(i, count):
        for u in range(8):
            count = step(i * 8 + u, count)
        return count

    count = lax.fori_loop(0, QBLOCKS * 32 // 8, eight, 0)
    for u in range(UNROLL):
        out[count + u] = SPARE
    out[COUNT_AT] = count


def own_kernel(piece, own_weights, own_base):
    row = lax.broadcasted_iota(jnp.int32, (FRAMES, FRAMES), 0)
    col = lax.broadcasted_iota(jnp.int32, (FRAMES, FRAMES), 1)
    for b in range(PART):
        block = piece[b * FRAMES:(b + 1) * FRAMES, :]
        units = block[:, :FEAT]
        affinity = lax.dot_general(
            units, units, (((1,), (1,)), ((), ())), preferred_element_type=jnp.float32
        )
        weights = jnp.where(row == col, 0.0, jnp.exp(sharpness * affinity)).astype(jnp.bfloat16)
        own_weights[b] = weights
        own_base[b] = jnp.dot(weights, block[:, FEAT:], preferred_element_type=jnp.float32)


def first_kernel(lst, queries, near_a, near_b, far_a, far_b, send, weights_out, q, k, acc, w, sems, out_sem):
    copies = [
        pltpu.make_async_copy(near_a, k.at[0, pl.ds(0, 5 * PIECE)], sems.at[0]),
        pltpu.make_async_copy(near_b, k.at[0, pl.ds(5 * PIECE, 3 * PIECE)], sems.at[1]),
        pltpu.make_async_copy(far_a, k.at[1, pl.ds(0, 5 * PIECE)], sems.at[2]),
        pltpu.make_async_copy(far_b, k.at[1, pl.ds(5 * PIECE, 3 * PIECE)], sems.at[3]),
        pltpu.make_async_copy(queries, q, sems.at[4]),
    ]
    for copy in copies:
        copy.start()
    acc[...] = jnp.zeros_like(acc)
    for copy in copies:
        copy.wait()
    steps = (lst[COUNT_AT] + UNROLL - 1) // UNROLL

    def step(i, carry):
        for u in range(UNROLL):
            code = lst[i * UNROLL + u]
            slot = code & 127
            row = pl.multiple_of(((code >> 7) & 31) * FRAMES, FRAMES)
            side = (code >> 12) & 1
            units = q[jnp.minimum(slot, QBLOCKS - 1)]
            keys = k[side, pl.ds(row, FRAMES), pl.ds(0, FEAT)]
            affinity = lax.dot_general(
                units, keys, (((1,), (1,)), ((), ())), preferred_element_type=jnp.float32
            )
            weights = jnp.exp(sharpness * affinity).astype(jnp.bfloat16)
            w[u, i] = weights
            acc[slot] += jnp.dot(
                weights, k[side, pl.ds(row, FRAMES), pl.ds(FEAT, 2 * CH)], preferred_element_type=jnp.float32
            )
        for u in range(UNROLL):
            pltpu.make_async_copy(w.at[u, i], weights_out.at[u, i], out_sem).start()
        return carry

    lax.fori_loop(0, steps, step, 0)
    row = lax.broadcasted_iota(jnp.int32, (FRAMES, CH), 0)
    lane = lax.broadcasted_iota(jnp.int32, (FRAMES, CH), 1)
    pick = row == lane % FRAMES
    low = lax.broadcasted_iota(jnp.int32, (1, CH), 1) < FRAMES

    def finish(d, carry):
        rows = []
        for b in range(PART):
            block = acc[d * PART + b]
            send[d, b * FRAMES:(b + 1) * FRAMES, :] = block[:, :CH].astype(jnp.bfloat16)
            mass = jnp.sum(jnp.where(pick, block[:, CH:], 0.0), axis=0, keepdims=True)
            coarse = mass.astype(jnp.bfloat16).astype(jnp.float32)
            rows.append(jnp.where(low, coarse, mass - coarse))
        rows.append(jnp.zeros((16 - PART, CH), jnp.float32))
        send[d, PIECE:SEND, :] = jnp.concatenate(rows, axis=0).astype(jnp.bfloat16)
        return carry

    lax.fori_loop(0, NY * NX, finish, 0)

    def drain(i, carry):
        for u in range(UNROLL):
            pltpu.make_async_copy(w.at[u, i], weights_out.at[u, i], out_sem).wait()
        return carry

    lax.fori_loop(0, steps, drain, 0)


def second_kernel(lst, weights_in, scores, send, acc, w, in_sem):
    steps = (lst[COUNT_AT] + UNROLL - 1) // UNROLL

    def fetch(i, carry):
        for u in range(UNROLL):
            pltpu.make_async_copy(weights_in.at[u, i], w.at[u, i], in_sem).start()
        return carry

    lax.fori_loop(0, steps, fetch, 0)
    acc[...] = jnp.zeros_like(acc)

    def drain(i, carry):
        for u in range(UNROLL):
            pltpu.make_async_copy(weights_in.at[u, i], w.at[u, i], in_sem).wait()
        return carry

    lax.fori_loop(0, steps, drain, 0)

    def step(i, carry):
        for u in range(UNROLL):
            code = lst[i * UNROLL + u]
            acc[code & 127] += jnp.dot(
                w[u, i], scores[(code >> 13) & 63], preferred_element_type=jnp.float32
            )
        return carry

    lax.fori_loop(0, steps, step, 0)
    for b in range(QBLOCKS):
        send[b] = acc[b].astype(jnp.bfloat16)


def mix_kernel(got, base, weights, prior, marks, masked, denominator, own_second):
    row = lax.broadcasted_iota(jnp.int32, (FRAMES, CH), 0)
    lane = lax.broadcasted_iota(jnp.int32, (FRAMES, CH), 1)
    pick = (row == lane % FRAMES).astype(jnp.float32)
    for b in range(PART):
        total = base[b, :, :CH]
        for d in range(NY * NX):
            total = total + got[d, b * FRAMES:(b + 1) * FRAMES, :].astype(jnp.float32)
        mass = jnp.sum(got[:, PIECE:SEND, :].astype(jnp.float32), axis=0)[b:b + 1, :]
        column = jnp.sum(pick * mass, axis=1, keepdims=True)
        full = 1.0 + column + base[b, :, CH:]
        denominator[b] = full
        mixed = keep_share * total / full + (1.0 - keep_share) * prior[b].astype(jnp.float32)
        keep = (mixed.astype(jnp.bfloat16).astype(jnp.float32) * marks[b].astype(jnp.float32)).astype(jnp.bfloat16)
        masked[b] = keep
        own_second[b] = jnp.dot(weights[b], keep, preferred_element_type=jnp.float32)


def last_kernel(got, own_second, denominator, prior, out):
    for b in range(PART):
        total = own_second[b]
        for d in range(NY * NX):
            total = total + got[d, b].astype(jnp.float32)
        mixed = keep_share * total / denominator[b]
        out[b] = (mixed + (1.0 - keep_share) * prior[b].astype(jnp.float32)).astype(jnp.bfloat16)


smem = pl.BlockSpec(memory_space=pltpu.SMEM)
vmem = pl.BlockSpec(memory_space=pltpu.VMEM)
hbm = pl.BlockSpec(memory_space=pl.ANY)
params = pltpu.CompilerParams(vmem_limit_bytes=VMEM)


def body(embeddings, prior_scores, frame_valid, neighbour_ids, neighbour_count, block_home):
    per_list = neighbour_ids.shape[1]
    y, z, c, x = (lax.axis_index(a) for a in ("y", "z", "c", "x"))
    first = x * PART
    mine = lax.dynamic_slice_in_dim(embeddings, first, PART, 0).astype(jnp.float32)
    prior = lax.dynamic_slice_in_dim(prior_scores, first, PART, 0)
    valid = lax.dynamic_slice_in_dim(frame_valid, first, PART, 0)
    units = (mine * lax.rsqrt(jnp.sum(mine * mine, axis=-1, keepdims=True) + epsilon)).astype(jnp.bfloat16)
    marks = jnp.broadcast_to(valid[:, :, None], prior.shape).astype(jnp.bfloat16)
    piece = jnp.concatenate([units, prior * marks, marks], axis=-1).reshape(PIECE, WIDE)

    queries = lax.all_gather(units, ("y", "x"), axis=0, tiled=True)

    target = jnp.take(block_home, neighbour_ids.reshape(-1), axis=0)
    column = x * per_list + jnp.arange(per_list, dtype=jnp.int32)
    in_list = column[None, :] < neighbour_count[:, None]
    target = jnp.where(in_list.reshape(-1), target, -1)
    target = lax.all_gather(target, ("y", "x"), axis=0).reshape(NY, NX, ROWS, per_list)
    source = (
        jnp.arange(NY, dtype=jnp.int32)[:, None, None, None] * ROWS
        + jnp.arange(ROWS, dtype=jnp.int32)[None, None, :, None]
    )
    wanted = (target >= 0) & (target // 256 == y) & ((target % 16) // PART == x)
    place = (target // 16) % 16
    apart = (place // 2 - z) % NZ
    order = jnp.where(
        apart == 0, 0, jnp.where(apart < 4, 2 * apart, jnp.where(apart == 4, 7, 2 * (NZ - apart) - 1))
    )
    inner = target % PART
    near = order * PART + inner
    side = (place % 2) ^ c
    whole = place * PART + inner
    codes = jnp.where(wanted, source | (near << 7) | (side << 12) | (whole << 13), -1).reshape(-1)
    lst = pl.pallas_call(
        list_kernel,
        out_shape=jax.ShapeDtypeStruct((LIST,), jnp.int32),
        in_specs=[smem],
        out_specs=smem,
    )(codes)

    up, down, held = piece, piece, [piece]
    for _ in range(3):
        up, down = shift(up, "z", 1), shift(down, "z", -1)
        held += [up, down]
    half = PIECE // 2
    last_up, last_down = shift(up[:half], "z", 1), shift(down[half:], "z", -1)
    near_a = jnp.concatenate(held[:5], axis=0)
    near_b = jnp.concatenate(held[5:] + [last_up, last_down], axis=0)
    far_a, far_b = shift(near_a, "c", 1), shift(near_b, "c", 1)

    own_weights, own_base = pl.pallas_call(
        own_kernel,
        out_shape=(
            jax.ShapeDtypeStruct((PART, FRAMES, FRAMES), jnp.bfloat16),
            jax.ShapeDtypeStruct((PART, FRAMES, 2 * CH), jnp.float32),
        ),
        in_specs=[vmem],
        out_specs=(vmem, vmem),
    )(piece)

    steps = PAIRS // UNROLL
    send, weights = pl.pallas_call(
        first_kernel,
        out_shape=(
            jax.ShapeDtypeStruct((NY * NX, SEND, CH), jnp.bfloat16),
            jax.ShapeDtypeStruct((UNROLL, steps, FRAMES, FRAMES), jnp.bfloat16),
        ),
        in_specs=[smem, hbm, hbm, hbm, hbm, hbm],
        out_specs=(vmem, hbm),
        scratch_shapes=[
            pltpu.VMEM((QBLOCKS, FRAMES, FEAT), jnp.bfloat16),
            pltpu.VMEM((NC, NZ * PIECE, WIDE), jnp.bfloat16),
            pltpu.VMEM((QBLOCKS + 1, FRAMES, 2 * CH), jnp.float32),
            pltpu.VMEM((UNROLL, steps, FRAMES, FRAMES), jnp.bfloat16),
            pltpu.SemaphoreType.DMA((5,)),
            pltpu.SemaphoreType.DMA,
        ],
        compiler_params=params,
    )(lst, queries, near_a, near_b, far_a, far_b)
    got = lax.all_to_all(send, ("y", "x"), split_axis=0, concat_axis=0, tiled=True)

    masked, denominator, own_second = pl.pallas_call(
        mix_kernel,
        out_shape=(
            jax.ShapeDtypeStruct((PART, FRAMES, CH), jnp.bfloat16),
            jax.ShapeDtypeStruct((PART, FRAMES, CH), jnp.float32),
            jax.ShapeDtypeStruct((PART, FRAMES, CH), jnp.float32),
        ),
        in_specs=[vmem] * 5,
        out_specs=(vmem,) * 3,
    )(got, own_base, own_weights, prior, marks)
    scores = lax.all_gather(masked, ("z", "c"), axis=0, tiled=True)

    send = pl.pallas_call(
        second_kernel,
        out_shape=jax.ShapeDtypeStruct((QBLOCKS, FRAMES, CH), jnp.bfloat16),
        in_specs=[smem, hbm, vmem],
        out_specs=vmem,
        scratch_shapes=[
            pltpu.VMEM((QBLOCKS + 1, FRAMES, CH), jnp.float32),
            pltpu.VMEM((UNROLL, steps, FRAMES, FRAMES), jnp.bfloat16),
            pltpu.SemaphoreType.DMA,
        ],
        compiler_params=params,
    )(lst, weights, scores)
    got = lax.all_to_all(send, ("y", "x"), split_axis=0, concat_axis=0, tiled=True)
    return pl.pallas_call(
        last_kernel,
        out_shape=jax.ShapeDtypeStruct((PART, FRAMES, CH), jnp.bfloat16),
        in_specs=[vmem] * 4,
        out_specs=vmem,
    )(got.reshape(NY * NX, PART, FRAMES, CH), own_second, denominator, prior)


def solution(mesh):
    fine = Mesh(mesh.devices.reshape(NY, NZ, NC, NX), ("y", "z", "c", "x"))
    bucket = ("y", "z", "c")
    in_specs = (P(bucket, None, None), P(bucket, None, None), P(bucket, None), P(bucket, "x"), P(bucket), P())
    out_specs = P(("y", "z", "c", "x"), None, None)
    return jax.shard_map(body, mesh=fine, in_specs=in_specs, out_specs=out_specs, check_vma=False)
```

```python
import math

import jax
import jax.numpy as jnp
from jax import lax
from jax.experimental import pallas as pl
from jax.experimental.pallas import tpu as pltpu
from jax.sharding import Mesh
from jax.sharding import PartitionSpec as P

epsilon = 1e-06
keep_share = 0.9

NY, NZ, NC, NX = 4, 8, 2, 4
ROWS = 16
FRAMES = 64
FEAT = 1152
CH = 128
PART = ROWS // NX
LATE = PART - 1
QBLOCKS = NY * ROWS
EARLY_Q = ROWS + (NY - 1) * NX
LATE_Q = NY * NX * LATE
UNROLL = 4
SLOTS = 544
WIDE = FEAT + CH
PIECE = PART * FRAMES
SEND = PIECE + 16
LIST = 640
EARLY_AT, LATE_AT = 600, 601
SPARE = QBLOCKS
VMEM = 56 * 1024 * 1024
UNREAL = 1024.0
sharpness = 2.0 * math.sqrt(FEAT)


def shift(value, axis, step):
    size = lax.axis_size(axis)
    return lax.ppermute(value, axis, [(i, (i + step) % size) for i in range(size)])


def list_kernel(codes, out, late):
    def eight(i, counts):
        early_count, late_count = counts
        for u in range(8):
            code = codes[i * 8 + u]
            out[early_count] = code
            late[late_count] = code
            is_late = (code >> 25) & 1
            real = jnp.where(code >= 0, 1, 0)
            early_count = early_count + (real & (1 - is_late))
            late_count = late_count + (real & is_late)
        return early_count, late_count

    early_count, late_count = lax.fori_loop(0, QBLOCKS * 32 // 8, eight, (0, 0))
    for u in range(UNROLL):
        out[early_count + u] = SPARE
        late[late_count + u] = SPARE
    early_steps = (early_count + UNROLL - 1) // UNROLL
    late_steps = (late_count + UNROLL - 1) // UNROLL
    start = early_steps * UNROLL

    def copy(i, carry):
        for u in range(UNROLL):
            out[start + i * UNROLL + u] = late[i * UNROLL + u]
        return carry

    lax.fori_loop(0, late_steps, copy, 0)
    out[EARLY_AT] = early_steps
    out[LATE_AT] = early_steps + late_steps


def own_kernel(piece, own_weights, own_base):
    row = lax.broadcasted_iota(jnp.int32, (FRAMES, FRAMES), 0)
    col = lax.broadcasted_iota(jnp.int32, (FRAMES, FRAMES), 1)
    for b in range(PART):
        block = piece[b * FRAMES:(b + 1) * FRAMES, :]
        units = block[:, :FEAT]
        affinity = lax.dot_general(
            units, units, (((1,), (1,)), ((), ())), preferred_element_type=jnp.float32
        )
        weights = jnp.where(row == col, 0.0, jnp.exp(sharpness * affinity)).astype(jnp.bfloat16)
        own_weights[b] = weights
        own_base[b] = jnp.dot(weights, values_of(block[:, FEAT:]), preferred_element_type=jnp.float32)


def values_of(scores):
    floats = scores.astype(jnp.float32)
    real = floats < UNREAL
    return jnp.concatenate(
        [jnp.where(real, floats, 0.0), jnp.where(real, 1.0, 0.0)], axis=1
    ).astype(jnp.bfloat16)


def key_copies(near_a, near_b, far_a, far_b, k, sems):
    return [
        pltpu.make_async_copy(near_a, k.at[0, pl.ds(0, 5 * PIECE)], sems.at[0]),
        pltpu.make_async_copy(near_b, k.at[0, pl.ds(5 * PIECE, 3 * PIECE)], sems.at[1]),
        pltpu.make_async_copy(far_a, k.at[1, pl.ds(0, 5 * PIECE)], sems.at[2]),
        pltpu.make_async_copy(far_b, k.at[1, pl.ds(5 * PIECE, 3 * PIECE)], sems.at[3]),
    ]


def work_pairs(lst, first, last, q, q_blocks, k, acc, w, weights_out, out_sem):
    def step(i, carry):
        for u in range(UNROLL):
            at = i * UNROLL + u
            code = lst[at]
            slot = code & 127
            row = pl.multiple_of(((code >> 7) & 31) * FRAMES, FRAMES)
            side = (code >> 12) & 1
            units = q[jnp.minimum((code >> 19) & 63, q_blocks - 1)]
            keys = k[side, pl.ds(row, FRAMES), pl.ds(0, FEAT)]
            affinity = lax.dot_general(
                units, keys, (((1,), (1,)), ((), ())), preferred_element_type=jnp.float32
            )
            weights = jnp.exp(sharpness * affinity).astype(jnp.bfloat16)
            w[at] = weights
            acc[slot] += jnp.dot(
                weights,
                values_of(k[side, pl.ds(row, FRAMES), pl.ds(FEAT, CH)]),
                preferred_element_type=jnp.float32,
            )
        for u in range(UNROLL):
            at = i * UNROLL + u
            pltpu.make_async_copy(w.at[at], weights_out.at[at], out_sem).start()
        return carry

    lax.fori_loop(first, last, step, 0)


def drain_pairs(first, last, w, weights_out, out_sem):
    def drain(i, carry):
        for u in range(UNROLL):
            at = i * UNROLL + u
            pltpu.make_async_copy(w.at[at], weights_out.at[at], out_sem).wait()
        return carry

    lax.fori_loop(first, last, drain, 0)


def pack_sums(acc, send, before):
    row = lax.broadcasted_iota(jnp.int32, (FRAMES, CH), 0)
    lane = lax.broadcasted_iota(jnp.int32, (FRAMES, CH), 1)
    pick = row == lane % FRAMES
    low = lax.broadcasted_iota(jnp.int32, (1, CH), 1) < FRAMES

    def finish(d, carry):
        rows = []
        for b in range(PART):
            block = acc[d * PART + b]
            sums = block[:, :CH]
            if before is not None:
                sums = sums + before[d, b * FRAMES:(b + 1) * FRAMES, :].astype(jnp.float32)
            send[d, b * FRAMES:(b + 1) * FRAMES, :] = sums.astype(jnp.bfloat16)
            mass = jnp.sum(jnp.where(pick, block[:, CH:], 0.0), axis=0, keepdims=True)
            coarse = mass.astype(jnp.bfloat16).astype(jnp.float32)
            rows.append(jnp.where(low, coarse, mass - coarse))
        rows.append(jnp.zeros((16 - PART, CH), jnp.float32))
        tail = jnp.concatenate(rows, axis=0)
        if before is not None:
            tail = tail + before[d, PIECE:SEND, :].astype(jnp.float32)
        send[d, PIECE:SEND, :] = tail.astype(jnp.bfloat16)
        return carry

    lax.fori_loop(0, NY * NX, finish, 0)


def early_kernel(lst, own_q, behind, ahead, across, near_a, near_b, far_a, far_b,
                 send, weights_out, q, k, acc, w, sems, out_sem):
    copies = key_copies(near_a, near_b, far_a, far_b, k, sems) + [
        pltpu.make_async_copy(own_q, q.at[pl.ds(0, ROWS)], sems.at[4]),
        pltpu.make_async_copy(ahead, q.at[pl.ds(ROWS, NX)], sems.at[5]),
        pltpu.make_async_copy(across, q.at[pl.ds(ROWS + NX, NX)], sems.at[6]),
        pltpu.make_async_copy(behind, q.at[pl.ds(ROWS + 2 * NX, NX)], sems.at[7]),
    ]
    for copy in copies:
        copy.start()
    acc[...] = jnp.zeros_like(acc)
    for copy in copies:
        copy.wait()
    work_pairs(lst, 0, lst[EARLY_AT], q, EARLY_Q, k, acc, w, weights_out, out_sem)
    pack_sums(acc, send, None)
    drain_pairs(0, lst[EARLY_AT], w, weights_out, out_sem)


def late_kernel(lst, queries, before, weights_in, near_a, near_b, far_a, far_b,
                send, weights_out, q, k, acc, w, sems, out_sem):
    copies = key_copies(near_a, near_b, far_a, far_b, k, sems) + [
        pltpu.make_async_copy(queries, q, sems.at[4]),
    ]
    for copy in copies:
        copy.start()
    acc[...] = jnp.zeros_like(acc)
    for copy in copies:
        copy.wait()
    work_pairs(lst, lst[EARLY_AT], lst[LATE_AT], q, LATE_Q, k, acc, w, weights_out, out_sem)
    pack_sums(acc, send, before)
    drain_pairs(lst[EARLY_AT], lst[LATE_AT], w, weights_out, out_sem)


def second_kernel(lst, weights_in, near, far, send, acc, w, in_sem):
    steps = lst[LATE_AT]

    def fetch(i, carry):
        for u in range(UNROLL):
            at = i * UNROLL + u
            pltpu.make_async_copy(weights_in.at[at], w.at[at], in_sem).start()
        return carry

    lax.fori_loop(0, steps, fetch, 0)
    acc[...] = jnp.zeros_like(acc)
    drain_pairs(0, steps, w, weights_in, in_sem)

    def step(i, carry):
        for u in range(UNROLL):
            at = i * UNROLL + u
            code = lst[at]
            block = (code >> 13) & 31
            scores = jnp.where(((code >> 12) & 1) == 0, near[block], far[block])
            acc[code & 127] += jnp.dot(w[at], scores, preferred_element_type=jnp.float32)
        return carry

    lax.fori_loop(0, steps, step, 0)
    for b in range(QBLOCKS):
        send[b] = acc[b].astype(jnp.bfloat16)


def mix_kernel(got, base, weights, prior, marks, masked, denominator, own_second):
    row = lax.broadcasted_iota(jnp.int32, (FRAMES, CH), 0)
    lane = lax.broadcasted_iota(jnp.int32, (FRAMES, CH), 1)
    pick = (row == lane % FRAMES).astype(jnp.float32)
    for b in range(PART):
        total = base[b, :, :CH]
        for d in range(NY * NX):
            total = total + got[d, b * FRAMES:(b + 1) * FRAMES, :].astype(jnp.float32)
        mass = jnp.sum(got[:, PIECE:SEND, :].astype(jnp.float32), axis=0)[b:b + 1, :]
        column = jnp.sum(pick * mass, axis=1, keepdims=True)
        full = 1.0 + column + base[b, :, CH:]
        denominator[b] = full
        mixed = keep_share * total / full + (1.0 - keep_share) * prior[b].astype(jnp.float32)
        keep = (mixed.astype(jnp.bfloat16).astype(jnp.float32) * marks[b].astype(jnp.float32)).astype(jnp.bfloat16)
        masked[b] = keep
        own_second[b] = jnp.dot(weights[b], keep, preferred_element_type=jnp.float32)


def last_kernel(got, own_second, denominator, prior, out):
    for b in range(PART):
        total = own_second[b]
        for d in range(NY * NX):
            total = total + got[d, b].astype(jnp.float32)
        mixed = keep_share * total / denominator[b]
        out[b] = (mixed + (1.0 - keep_share) * prior[b].astype(jnp.float32)).astype(jnp.bfloat16)


smem = pl.BlockSpec(memory_space=pltpu.SMEM)
vmem = pl.BlockSpec(memory_space=pltpu.VMEM)
hbm = pl.BlockSpec(memory_space=pl.ANY)
params = pltpu.CompilerParams(vmem_limit_bytes=VMEM)


def normalize(values):
    floats = values.astype(jnp.float32)
    return (floats * lax.rsqrt(jnp.sum(floats * floats, axis=-1, keepdims=True) + epsilon)).astype(jnp.bfloat16)


def body(embeddings, prior_scores, frame_valid, neighbour_ids, neighbour_count, block_home):
    per_list = neighbour_ids.shape[1]
    y, z, c, x = (lax.axis_index(a) for a in ("y", "z", "c", "x"))
    first = x * PART
    units = normalize(lax.dynamic_slice_in_dim(embeddings, first, PART, 0))
    prior = lax.dynamic_slice_in_dim(prior_scores, first, PART, 0)
    valid = lax.dynamic_slice_in_dim(frame_valid, first, PART, 0)
    marks = jnp.broadcast_to(valid[:, :, None], prior.shape).astype(jnp.bfloat16)
    marked = jnp.where(marks > 0, prior, jnp.bfloat16(2 * UNREAL))
    piece = jnp.concatenate([units, marked], axis=-1).reshape(PIECE, WIDE)

    queries = lax.all_gather(units[:LATE], ("y", "x"), axis=0, tiled=True)

    up, down = shift(piece, "z", 1), shift(piece, "z", -1)
    embeddings, piece = lax.optimization_barrier((embeddings, piece))
    all_units = normalize(embeddings)
    direct = all_units.reshape(NX, PART, FRAMES, FEAT)[:, LATE]
    behind, ahead = shift(direct, "y", 1), shift(direct, "y", -1)
    ids, _ = lax.optimization_barrier((neighbour_ids, piece))
    target = jnp.take(block_home, ids.reshape(-1), axis=0)
    column = x * per_list + jnp.arange(per_list, dtype=jnp.int32)
    in_list = column[None, :] < neighbour_count[:, None]
    target = jnp.where(in_list.reshape(-1), target, -1)
    target = lax.all_gather(target, ("y", "x"), axis=0)

    up, down, behind, ahead, target = lax.optimization_barrier((up, down, behind, ahead, target))
    held = [piece, up, down]
    half = NX // 2
    across_a, across_b = shift(behind[:half], "y", 1), shift(ahead[half:], "y", -1)
    up, down = shift(up, "z", 1), shift(down, "z", -1)
    target = target.reshape(NY, NX, ROWS, per_list)
    source_y = jnp.arange(NY, dtype=jnp.int32)[:, None, None, None]
    source_row = jnp.arange(ROWS, dtype=jnp.int32)[None, None, :, None]
    source = source_y * ROWS + source_row
    wanted = (target >= 0) & (target // 256 == y) & ((target % 16) // PART == x)
    place = (target // 16) % 16
    apart = (place // 2 - z) % NZ
    order = jnp.where(
        apart == 0, 0, jnp.where(apart < 4, 2 * apart, jnp.where(apart == 4, 7, 2 * (NZ - apart) - 1))
    )
    inner = target % PART
    near = order * PART + inner
    side = (place % 2) ^ c
    whole = (place // 2) * PART + inner
    mine = source_y == y
    straight = source_row % PART == LATE
    late = jnp.where(mine | straight, 0, 1)
    from_early = jnp.where(mine, source_row, ROWS + ((source_y - y) % NY - 1) * NX + source_row // PART)
    from_late = (source_y * NX + source_row // PART) * LATE + source_row % PART
    taken = jnp.where(late == 0, from_early, from_late)
    codes = source | (near << 7) | (side << 12) | (whole << 13) | (taken << 19) | (late << 25)
    codes = jnp.where(wanted, codes, -1).reshape(-1)
    lst = pl.pallas_call(
        list_kernel,
        out_shape=jax.ShapeDtypeStruct((LIST,), jnp.int32),
        in_specs=[smem],
        out_specs=smem,
        scratch_shapes=[pltpu.SMEM((LIST,), jnp.int32)],
    )(codes)

    up, down, across_a, across_b, lst = lax.optimization_barrier((up, down, across_a, across_b, lst))
    across = jnp.concatenate([across_a, across_b], axis=0)
    held += [up, down]
    near_a = jnp.concatenate(held, axis=0)
    up, down = shift(up, "z", 1), shift(down, "z", -1)
    far_a = shift(near_a, "c", 1)
    own_weights, own_base = pl.pallas_call(
        own_kernel,
        out_shape=(
            jax.ShapeDtypeStruct((PART, FRAMES, FRAMES), jnp.bfloat16),
            jax.ShapeDtypeStruct((PART, FRAMES, 2 * CH), jnp.float32),
        ),
        in_specs=[vmem],
        out_specs=(vmem, vmem),
    )(piece)

    up, down, own_base = lax.optimization_barrier((up, down, own_base))
    half = PIECE // 2
    last_up, last_down = shift(up[:half], "z", 1), shift(down[half:], "z", -1)
    near_b = jnp.concatenate([up, down, last_up, last_down], axis=0)
    far_b = shift(near_b, "c", 1)
    keys = (near_a, near_b, far_a, far_b)

    def scratch(q_blocks, sems):
        return [
            pltpu.VMEM((q_blocks, FRAMES, FEAT), jnp.bfloat16),
            pltpu.VMEM((NC, NZ * PIECE, WIDE), jnp.bfloat16),
            pltpu.VMEM((QBLOCKS + 1, FRAMES, 2 * CH), jnp.float32),
            pltpu.VMEM((SLOTS, FRAMES, FRAMES), jnp.bfloat16),
            pltpu.SemaphoreType.DMA((sems,)),
            pltpu.SemaphoreType.DMA,
        ]

    sums = jax.ShapeDtypeStruct((NY * NX, SEND, CH), jnp.bfloat16)
    pair_weights = jax.ShapeDtypeStruct((SLOTS, FRAMES, FRAMES), jnp.bfloat16)
    send, weights = pl.pallas_call(
        early_kernel,
        out_shape=(sums, pair_weights),
        in_specs=[smem] + [hbm] * 8,
        out_specs=(vmem, hbm),
        scratch_shapes=scratch(EARLY_Q, 8),
        compiler_params=params,
    )(lst, all_units, behind, ahead, across, *keys)
    send, weights = pl.pallas_call(
        late_kernel,
        out_shape=(sums, pair_weights),
        in_specs=[smem, hbm, vmem] + [hbm] * 5,
        out_specs=(vmem, hbm),
        scratch_shapes=scratch(LATE_Q, 5),
        input_output_aliases={3: 1},
        compiler_params=params,
    )(lst, queries, send, weights, *keys)
    got = lax.all_to_all(send, ("y", "x"), split_axis=0, concat_axis=0, tiled=True)

    masked, denominator, own_second = pl.pallas_call(
        mix_kernel,
        out_shape=(
            jax.ShapeDtypeStruct((PART, FRAMES, CH), jnp.bfloat16),
            jax.ShapeDtypeStruct((PART, FRAMES, CH), jnp.float32),
            jax.ShapeDtypeStruct((PART, FRAMES, CH), jnp.float32),
        ),
        in_specs=[vmem] * 5,
        out_specs=(vmem,) * 3,
    )(got, own_base, own_weights, prior, marks)
    near_scores = lax.all_gather(masked, "z", axis=0, tiled=True)
    far_scores = shift(near_scores, "c", 1)

    send = pl.pallas_call(
        second_kernel,
        out_shape=jax.ShapeDtypeStruct((QBLOCKS, FRAMES, CH), jnp.bfloat16),
        in_specs=[smem, hbm, vmem, vmem],
        out_specs=vmem,
        scratch_shapes=[
            pltpu.VMEM((QBLOCKS + 1, FRAMES, CH), jnp.float32),
            pltpu.VMEM((SLOTS, FRAMES, FRAMES), jnp.bfloat16),
            pltpu.SemaphoreType.DMA,
        ],
        compiler_params=params,
    )(lst, weights, near_scores, far_scores)
    got = lax.all_to_all(send, ("y", "x"), split_axis=0, concat_axis=0, tiled=True)
    return pl.pallas_call(
        last_kernel,
        out_shape=jax.ShapeDtypeStruct((PART, FRAMES, CH), jnp.bfloat16),
        in_specs=[vmem] * 4,
        out_specs=vmem,
    )(got.reshape(NY * NX, PART, FRAMES, CH), own_second, denominator, prior)


def solution(mesh):
    fine = Mesh(mesh.devices.reshape(NY, NZ, NC, NX), ("y", "z", "c", "x"))
    bucket = ("y", "z", "c")
    in_specs = (P(bucket, None, None), P(bucket, None, None), P(bucket, None), P(bucket, "x"), P(bucket), P())
    out_specs = P(("y", "z", "c", "x"), None, None)
    return jax.shard_map(body, mesh=fine, in_specs=in_specs, out_specs=out_specs, check_vma=False)
```

```python
import math

import jax
import jax.numpy as jnp
from jax import lax
from jax.experimental import pallas as pl
from jax.experimental.pallas import tpu as pltpu
from jax.sharding import Mesh
from jax.sharding import PartitionSpec as P

epsilon = 1e-06
keep_share = 0.9

NY, NZ, NC, NX = 4, 8, 2, 4
ROWS = 16
FRAMES = 64
FEAT = 1152
CH = 128
PART = ROWS // NX
SHARED = 2
STRAIGHT = NX * (PART - SHARED)
QBLOCKS = NY * ROWS
Q_SHARED = ROWS + (NY - 1) * STRAIGHT
Q_ALL = Q_SHARED + NY * NX * SHARED
UNROLL = 8
SLOTS = 520
WIDE = FEAT + CH
PIECE = PART * FRAMES
HALF = PIECE // 2
SEND = PIECE + 16
LIST = 640
STEPS_AT = 600
SPARE = QBLOCKS
VMEM = 56 * 1024 * 1024
UNREAL = 1024.0
sharpness = 2.0 * math.sqrt(FEAT)


def shift(value, axis, step):
    size = lax.axis_size(axis)
    return lax.ppermute(value, axis, [(i, (i + step) % size) for i in range(size)])


def list_kernel(codes, out):
    def eight(i, count):
        for u in range(8):
            code = codes[i * 8 + u]
            out[count] = code
            count = count + jnp.where(code >= 0, 1, 0)
        return count

    count = lax.fori_loop(0, QBLOCKS * 32 // 8, eight, 0)
    for u in range(UNROLL):
        out[count + u] = SPARE
    out[STEPS_AT] = (count + UNROLL - 1) // UNROLL


def own_kernel(piece, own_weights, own_base):
    row = lax.broadcasted_iota(jnp.int32, (FRAMES, FRAMES), 0)
    col = lax.broadcasted_iota(jnp.int32, (FRAMES, FRAMES), 1)
    for b in range(PART):
        block = piece[b * FRAMES:(b + 1) * FRAMES, :]
        units = block[:, :FEAT]
        affinity = lax.dot_general(
            units, units, (((1,), (1,)), ((), ())), preferred_element_type=jnp.float32
        )
        weights = jnp.where(row == col, 0.0, jnp.exp(sharpness * affinity)).astype(jnp.bfloat16)
        own_weights[b] = weights
        own_base[b] = jnp.dot(weights, values_of(block[:, FEAT:]), preferred_element_type=jnp.float32)


def values_of(scores):
    floats = scores.astype(jnp.float32)
    real = floats < UNREAL
    return jnp.concatenate(
        [jnp.where(real, floats, 0.0), jnp.where(real, 1.0, 0.0)], axis=1
    ).astype(jnp.bfloat16)


def first_kernel(lst, *refs):
    near, far, queries = refs[:9], refs[9:18], refs[18:23]
    send, weights_out, q, k, acc, w, sems, out_sem = refs[23:]
    copies = []
    for side, held in enumerate((near, far)):
        at = 0
        for piece in held:
            rows = piece.shape[0]
            copies.append(pltpu.make_async_copy(piece, k.at[side, pl.ds(at, rows)], sems.at[len(copies)]))
            at += rows
    at = 0
    for part in queries:
        rows = part.shape[0]
        copies.append(pltpu.make_async_copy(part, q.at[pl.ds(at, rows)], sems.at[len(copies)]))
        at += rows
    for copy in copies:
        copy.start()
    acc[...] = jnp.zeros_like(acc)
    for copy in copies:
        copy.wait()
    steps = lst[STEPS_AT]

    def step(i, carry):
        codes = [lst[i * UNROLL + u] for u in range(UNROLL)]
        sides = [(code >> 12) & 1 for code in codes]
        rows = [pl.multiple_of(((code >> 7) & 31) * FRAMES, FRAMES) for code in codes]
        weights = []
        for code, side, row in zip(codes, sides, rows):
            units = q[(code >> 18) & 127]
            keys = k[side, pl.ds(row, FRAMES), pl.ds(0, FEAT)]
            affinity = lax.dot_general(
                units, keys, (((1,), (1,)), ((), ())), preferred_element_type=jnp.float32
            )
            weights.append(jnp.exp(sharpness * affinity).astype(jnp.bfloat16))
        for u in range(UNROLL):
            w[i * UNROLL + u] = weights[u]
        sums = []
        for u, (side, row) in enumerate(zip(sides, rows)):
            values = values_of(k[side, pl.ds(row, FRAMES), pl.ds(FEAT, CH)])
            sums.append(jnp.dot(weights[u], values, preferred_element_type=jnp.float32))
        for u, code in enumerate(codes):
            acc[code & 127] += sums[u]
        group = pl.ds(i * UNROLL, UNROLL)
        pltpu.make_async_copy(w.at[group], weights_out.at[group], out_sem).start()
        return carry

    lax.fori_loop(0, steps, step, 0)
    row = lax.broadcasted_iota(jnp.int32, (FRAMES, CH), 0)
    lane = lax.broadcasted_iota(jnp.int32, (FRAMES, CH), 1)
    pick = row == lane % FRAMES
    low = lax.broadcasted_iota(jnp.int32, (1, CH), 1) < FRAMES

    def finish(d, carry):
        rows = []
        for b in range(PART):
            block = acc[d * PART + b]
            send[d, b * FRAMES:(b + 1) * FRAMES, :] = block[:, :CH].astype(jnp.bfloat16)
            mass = jnp.sum(jnp.where(pick, block[:, CH:], 0.0), axis=0, keepdims=True)
            coarse = mass.astype(jnp.bfloat16).astype(jnp.float32)
            rows.append(jnp.where(low, coarse, mass - coarse))
        rows.append(jnp.zeros((16 - PART, CH), jnp.float32))
        send[d, PIECE:SEND, :] = jnp.concatenate(rows, axis=0).astype(jnp.bfloat16)
        return carry

    lax.fori_loop(0, NY * NX, finish, 0)

    def drain(i, carry):
        group = pl.ds(i * UNROLL, UNROLL)
        pltpu.make_async_copy(w.at[group], weights_out.at[group], out_sem).wait()
        return carry

    lax.fori_loop(0, steps, drain, 0)


def second_kernel(lst, weights_in, near, far, send, acc, w, in_sem):
    steps = lst[STEPS_AT]

    def fetch(i, carry):
        group = pl.ds(i * UNROLL, UNROLL)
        pltpu.make_async_copy(weights_in.at[group], w.at[group], in_sem).start()
        return carry

    lax.fori_loop(0, steps, fetch, 0)
    acc[...] = jnp.zeros_like(acc)

    def drain(i, carry):
        group = pl.ds(i * UNROLL, UNROLL)
        pltpu.make_async_copy(weights_in.at[group], w.at[group], in_sem).wait()
        return carry

    lax.fori_loop(0, steps, drain, 0)

    def step(i, carry):
        codes = [lst[i * UNROLL + u] for u in range(UNROLL)]
        sums = []
        for u, code in enumerate(codes):
            block = (code >> 13) & 31
            scores = jnp.where(((code >> 12) & 1) == 0, near[block], far[block])
            sums.append(jnp.dot(w[i * UNROLL + u], scores, preferred_element_type=jnp.float32))
        for u, code in enumerate(codes):
            acc[code & 127] += sums[u]
        return carry

    lax.fori_loop(0, steps, step, 0)
    for b in range(QBLOCKS):
        send[b] = acc[b].astype(jnp.bfloat16)


def mix_kernel(got, base, weights, prior, marks, masked, denominator, own_second):
    row = lax.broadcasted_iota(jnp.int32, (FRAMES, CH), 0)
    lane = lax.broadcasted_iota(jnp.int32, (FRAMES, CH), 1)
    pick = (row == lane % FRAMES).astype(jnp.float32)
    for b in range(PART):
        total = base[b, :, :CH]
        for d in range(NY * NX):
            total = total + got[d, b * FRAMES:(b + 1) * FRAMES, :].astype(jnp.float32)
        mass = jnp.sum(got[:, PIECE:SEND, :].astype(jnp.float32), axis=0)[b:b + 1, :]
        column = jnp.sum(pick * mass, axis=1, keepdims=True)
        full = 1.0 + column + base[b, :, CH:]
        denominator[b] = full
        mixed = keep_share * total / full + (1.0 - keep_share) * prior[b].astype(jnp.float32)
        keep = (mixed.astype(jnp.bfloat16).astype(jnp.float32) * marks[b].astype(jnp.float32)).astype(jnp.bfloat16)
        masked[b] = keep
        own_second[b] = jnp.dot(weights[b], keep, preferred_element_type=jnp.float32)


def last_kernel(got, own_second, denominator, prior, out):
    for b in range(PART):
        total = own_second[b]
        for d in range(NY * NX):
            total = total + got[d, b].astype(jnp.float32)
        mixed = keep_share * total / denominator[b]
        out[b] = (mixed + (1.0 - keep_share) * prior[b].astype(jnp.float32)).astype(jnp.bfloat16)


smem = pl.BlockSpec(memory_space=pltpu.SMEM)
vmem = pl.BlockSpec(memory_space=pltpu.VMEM)
hbm = pl.BlockSpec(memory_space=pl.ANY)
params = pltpu.CompilerParams(vmem_limit_bytes=VMEM)


def normalize(values):
    floats = values.astype(jnp.float32)
    return (floats * lax.rsqrt(jnp.sum(floats * floats, axis=-1, keepdims=True) + epsilon)).astype(jnp.bfloat16)


def body(embeddings, prior_scores, frame_valid, neighbour_ids, neighbour_count, block_home):
    per_list = neighbour_ids.shape[1]
    y, z, c, x = (lax.axis_index(a) for a in ("y", "z", "c", "x"))
    first = x * PART
    units = normalize(lax.dynamic_slice_in_dim(embeddings, first, PART, 0))
    prior = lax.dynamic_slice_in_dim(prior_scores, first, PART, 0)
    valid = lax.dynamic_slice_in_dim(frame_valid, first, PART, 0)
    marks = jnp.broadcast_to(valid[:, :, None], prior.shape).astype(jnp.bfloat16)
    marked = jnp.where(marks > 0, prior, jnp.bfloat16(2 * UNREAL))
    piece = jnp.concatenate([units, marked], axis=-1).reshape(PIECE, WIDE)

    target = jnp.take(block_home, neighbour_ids.reshape(-1), axis=0)
    column = x * per_list + jnp.arange(per_list, dtype=jnp.int32)
    in_list = column[None, :] < neighbour_count[:, None]
    target = jnp.where(in_list.reshape(-1), target, -1).reshape(1, ROWS * per_list)

    shared = lax.all_gather(units[:SHARED], ("y", "x"), axis=0, tiled=True)
    up, down = shift(piece, "z", 1), shift(piece, "z", -1)
    embeddings, piece = lax.optimization_barrier((embeddings, piece))
    all_units = normalize(embeddings)
    straight = all_units.reshape(NX, PART, FRAMES, FEAT)[:, SHARED:].reshape(STRAIGHT, FRAMES, FEAT)
    behind, ahead = shift(straight, "y", 1), shift(straight, "y", -1)
    targets = [target, shift(target, "y", -1), shift(target, "y", 2), shift(target, "y", 1)]

    up, down, targets = lax.optimization_barrier((up, down, targets))
    near = [piece, up, down]
    far = [shift(v, "c", 1) for v in near]
    up, down = shift(up, "z", 1), shift(down, "z", -1)
    target = jnp.concatenate(targets, axis=0)
    targets = [target, shift(target, "x", -1), shift(target, "x", 2), shift(target, "x", 1)]

    up, down, behind, ahead, targets = lax.optimization_barrier((up, down, behind, ahead, targets))
    half = STRAIGHT // 2
    across_a, across_b = shift(behind[:half], "y", 1), shift(ahead[half:], "y", -1)
    held = [up, down]
    up, down = shift(up, "z", 1), shift(down, "z", -1)
    near += held
    far += [shift(v, "c", 1) for v in held]
    target = jnp.stack(targets, axis=0).reshape(NX, NY, ROWS, per_list)
    distance = jnp.arange(NY, dtype=jnp.int32)[None, :, None, None]
    source_row = jnp.arange(ROWS, dtype=jnp.int32)[None, None, :, None]
    source_y = (y + distance) % NY
    source = source_y * ROWS + source_row
    wanted = (target >= 0) & (target // 256 == y) & ((target % 16) // PART == x)
    place = (target // 16) % 16
    apart = (place // 2 - z) % NZ
    order = jnp.where(
        apart == 0, 0, jnp.where(apart < 4, 2 * apart, jnp.where(apart == 4, 7, 2 * (NZ - apart) - 1))
    )
    inner = target % PART
    side = (place % 2) ^ c
    quarter, within = source_row // PART, source_row % PART
    taken = jnp.where(
        distance == 0,
        source_row,
        jnp.where(
            within < SHARED,
            Q_SHARED + (source_y * NX + quarter) * SHARED + within,
            ROWS + (distance - 1) * STRAIGHT + quarter * (PART - SHARED) + within - SHARED,
        ),
    )
    codes = source | ((order * PART + inner) << 7) | (side << 12) | (((place // 2) * PART + inner) << 13) | (taken << 18)
    codes = jnp.where(wanted, codes, -1).reshape(-1)
    lst = pl.pallas_call(
        list_kernel,
        out_shape=jax.ShapeDtypeStruct((LIST,), jnp.int32),
        in_specs=[smem],
        out_specs=smem,
    )(codes)

    up, down, lst = lax.optimization_barrier((up, down, lst))
    last_up, last_down = shift(up[:HALF], "z", 1), shift(down[HALF:], "z", -1)
    near += [up, down]
    far += [shift(up, "c", 1), shift(down, "c", 1)]
    own_weights, own_base = pl.pallas_call(
        own_kernel,
        out_shape=(
            jax.ShapeDtypeStruct((PART, FRAMES, FRAMES), jnp.bfloat16),
            jax.ShapeDtypeStruct((PART, FRAMES, 2 * CH), jnp.float32),
        ),
        in_specs=[vmem],
        out_specs=(vmem, vmem),
    )(piece)
    near += [last_up, last_down]
    far += [shift(last_up, "c", 1), shift(last_down, "c", 1)]
    across = jnp.concatenate([across_a, across_b], axis=0)

    send, weights = pl.pallas_call(
        first_kernel,
        out_shape=(
            jax.ShapeDtypeStruct((NY * NX, SEND, CH), jnp.bfloat16),
            jax.ShapeDtypeStruct((SLOTS, FRAMES, FRAMES), jnp.bfloat16),
        ),
        in_specs=[smem] + [hbm] * 23,
        out_specs=(vmem, hbm),
        scratch_shapes=[
            pltpu.VMEM((Q_ALL, FRAMES, FEAT), jnp.bfloat16),
            pltpu.VMEM((NC, NZ * PIECE, WIDE), jnp.bfloat16),
            pltpu.VMEM((QBLOCKS + 1, FRAMES, 2 * CH), jnp.float32),
            pltpu.VMEM((SLOTS, FRAMES, FRAMES), jnp.bfloat16),
            pltpu.SemaphoreType.DMA((23,)),
            pltpu.SemaphoreType.DMA,
        ],
        compiler_params=params,
    )(lst, *near, *far, all_units, ahead, across, behind, shared)
    got = lax.all_to_all(send, ("y", "x"), split_axis=0, concat_axis=0, tiled=True)

    masked, denominator, own_second = pl.pallas_call(
        mix_kernel,
        out_shape=(
            jax.ShapeDtypeStruct((PART, FRAMES, CH), jnp.bfloat16),
            jax.ShapeDtypeStruct((PART, FRAMES, CH), jnp.float32),
            jax.ShapeDtypeStruct((PART, FRAMES, CH), jnp.float32),
        ),
        in_specs=[vmem] * 5,
        out_specs=(vmem,) * 3,
    )(got, own_base, own_weights, prior, marks)
    near_scores = lax.all_gather(masked, "z", axis=0, tiled=True)
    far_scores = shift(near_scores, "c", 1)

    send = pl.pallas_call(
        second_kernel,
        out_shape=jax.ShapeDtypeStruct((QBLOCKS, FRAMES, CH), jnp.bfloat16),
        in_specs=[smem, hbm, vmem, vmem],
        out_specs=vmem,
        scratch_shapes=[
            pltpu.VMEM((QBLOCKS + 1, FRAMES, CH), jnp.float32),
            pltpu.VMEM((SLOTS, FRAMES, FRAMES), jnp.bfloat16),
            pltpu.SemaphoreType.DMA,
        ],
        compiler_params=params,
    )(lst, weights, near_scores, far_scores)
    got = lax.all_to_all(send, ("y", "x"), split_axis=0, concat_axis=0, tiled=True)
    return pl.pallas_call(
        last_kernel,
        out_shape=jax.ShapeDtypeStruct((PART, FRAMES, CH), jnp.bfloat16),
        in_specs=[vmem] * 4,
        out_specs=vmem,
    )(got.reshape(NY * NX, PART, FRAMES, CH), own_second, denominator, prior)


def solution(mesh):
    fine = Mesh(mesh.devices.reshape(NY, NZ, NC, NX), ("y", "z", "c", "x"))
    bucket = ("y", "z", "c")
    in_specs = (P(bucket, None, None), P(bucket, None, None), P(bucket, None), P(bucket, "x"), P(bucket), P())
    out_specs = P(("y", "z", "c", "x"), None, None)
    return jax.shard_map(body, mesh=fine, in_specs=in_specs, out_specs=out_specs, check_vma=False)
```

```python
import math

import jax
import jax.numpy as jnp
from jax import lax
from jax.experimental import pallas as pl
from jax.experimental.pallas import tpu as pltpu
from jax.sharding import Mesh
from jax.sharding import PartitionSpec as P

epsilon = 1e-06
keep_share = 0.9

NY, NZ, NC, NX = 4, 8, 2, 4
ROWS = 16
FRAMES = 64
FEAT = 1152
CH = 128
PART = ROWS // NX
SHARED = 2
STRAIGHT = NX * (PART - SHARED)
QBLOCKS = NY * ROWS
Q_SHARED = ROWS + (NY - 1) * STRAIGHT
Q_ALL = Q_SHARED + NY * NX * SHARED
UNROLL = 8
SLOTS = 520
WIDE = FEAT + CH
PIECE = PART * FRAMES
HALF = PIECE // 2
SEND = PIECE + 16
SHARED_ROWS = SHARED * FRAMES
CELL = SHARED_ROWS + 16
LIST = 640
STEPS_AT = 600
SPARE = QBLOCKS
VMEM = 56 * 1024 * 1024
UNREAL = 1024.0
sharpness = 2.0 * math.sqrt(FEAT)


def shift(value, axis, step):
    size = lax.axis_size(axis)
    return lax.ppermute(value, axis, [(i, (i + step) % size) for i in range(size)])


def list_kernel(codes, out):
    def eight(i, count):
        for u in range(8):
            code = codes[i * 8 + u]
            out[count] = code
            count = count + jnp.where(code >= 0, 1, 0)
        return count

    count = lax.fori_loop(0, QBLOCKS * 32 // 8, eight, 0)
    for u in range(UNROLL):
        out[count + u] = SPARE
    out[STEPS_AT] = (count + UNROLL - 1) // UNROLL


def own_kernel(piece, own_weights, own_base):
    row = lax.broadcasted_iota(jnp.int32, (FRAMES, FRAMES), 0)
    col = lax.broadcasted_iota(jnp.int32, (FRAMES, FRAMES), 1)
    for b in range(PART):
        block = piece[b * FRAMES:(b + 1) * FRAMES, :]
        units = block[:, :FEAT]
        affinity = lax.dot_general(
            units, units, (((1,), (1,)), ((), ())), preferred_element_type=jnp.float32
        )
        weights = jnp.where(row == col, 0.0, jnp.exp(sharpness * affinity)).astype(jnp.bfloat16)
        own_weights[b] = weights
        own_base[b] = jnp.dot(weights, values_of(block[:, FEAT:]), preferred_element_type=jnp.float32)


def values_of(scores):
    floats = scores.astype(jnp.float32)
    real = floats < UNREAL
    return jnp.concatenate(
        [jnp.where(real, floats, 0.0), jnp.where(real, 1.0, 0.0)], axis=1
    ).astype(jnp.bfloat16)


def first_kernel(lst, *refs):
    near, far, queries = refs[:9], refs[9:18], refs[18:23]
    send, weights_out, q, k, acc, w, sems, out_sem = refs[23:]
    copies = []
    for side, held in enumerate((near, far)):
        at = 0
        for piece in held:
            rows = piece.shape[0]
            copies.append(pltpu.make_async_copy(piece, k.at[side, pl.ds(at, rows)], sems.at[len(copies)]))
            at += rows
    at = 0
    for part in queries[:4]:
        rows = part.shape[0]
        copies.append(pltpu.make_async_copy(part, q.at[pl.ds(at, rows)], sems.at[len(copies)]))
        at += rows
    for d in range(NY * NX):
        copies.append(
            pltpu.make_async_copy(
                queries[4].at[d, pl.ds(0, SHARED_ROWS)], q.at[pl.ds(at, SHARED_ROWS)], sems.at[len(copies)]
            )
        )
        at += SHARED_ROWS
    for copy in copies:
        copy.start()
    acc[...] = jnp.zeros_like(acc)
    for copy in copies:
        copy.wait()
    steps = lst[STEPS_AT]

    def step(i, carry):
        codes = [lst[i * UNROLL + u] for u in range(UNROLL)]
        sides = [(code >> 12) & 1 for code in codes]
        rows = [pl.multiple_of(((code >> 7) & 31) * FRAMES, FRAMES) for code in codes]
        weights = []
        for code, side, row in zip(codes, sides, rows):
            units = q[pl.ds(pl.multiple_of(((code >> 18) & 127) * FRAMES, FRAMES), FRAMES), :]
            keys = k[side, pl.ds(row, FRAMES), pl.ds(0, FEAT)]
            affinity = lax.dot_general(
                units, keys, (((1,), (1,)), ((), ())), preferred_element_type=jnp.float32
            )
            weights.append(jnp.exp(sharpness * affinity).astype(jnp.bfloat16))
        for u in range(UNROLL):
            w[i * UNROLL + u] = weights[u]
        sums = []
        for u, (side, row) in enumerate(zip(sides, rows)):
            values = values_of(k[side, pl.ds(row, FRAMES), pl.ds(FEAT, CH)])
            sums.append(jnp.dot(weights[u], values, preferred_element_type=jnp.float32))
        for u, code in enumerate(codes):
            acc[code & 127] += sums[u]
        group = pl.ds(i * UNROLL, UNROLL)
        pltpu.make_async_copy(w.at[group], weights_out.at[group], out_sem).start()
        return carry

    lax.fori_loop(0, steps, step, 0)
    row = lax.broadcasted_iota(jnp.int32, (FRAMES, CH), 0)
    lane = lax.broadcasted_iota(jnp.int32, (FRAMES, CH), 1)
    pick = row == lane % FRAMES
    low = lax.broadcasted_iota(jnp.int32, (1, CH), 1) < FRAMES

    def finish(d, carry):
        rows = []
        for b in range(PART):
            block = acc[d * PART + b]
            send[d, b * FRAMES:(b + 1) * FRAMES, :] = block[:, :CH].astype(jnp.bfloat16)
            mass = jnp.sum(jnp.where(pick, block[:, CH:], 0.0), axis=0, keepdims=True)
            coarse = mass.astype(jnp.bfloat16).astype(jnp.float32)
            rows.append(jnp.where(low, coarse, mass - coarse))
        rows.append(jnp.zeros((16 - PART, CH), jnp.float32))
        send[d, PIECE:SEND, :] = jnp.concatenate(rows, axis=0).astype(jnp.bfloat16)
        return carry

    lax.fori_loop(0, NY * NX, finish, 0)

    def drain(i, carry):
        group = pl.ds(i * UNROLL, UNROLL)
        pltpu.make_async_copy(w.at[group], weights_out.at[group], out_sem).wait()
        return carry

    lax.fori_loop(0, steps, drain, 0)


def second_kernel(lst, weights_in, near, far, send, acc, w, in_sem):
    steps = lst[STEPS_AT]

    def fetch(i, carry):
        group = pl.ds(i * UNROLL, UNROLL)
        pltpu.make_async_copy(weights_in.at[group], w.at[group], in_sem).start()
        return carry

    lax.fori_loop(0, steps, fetch, 0)
    acc[...] = jnp.zeros_like(acc)

    def drain(i, carry):
        group = pl.ds(i * UNROLL, UNROLL)
        pltpu.make_async_copy(weights_in.at[group], w.at[group], in_sem).wait()
        return carry

    lax.fori_loop(0, steps, drain, 0)

    def step(i, carry):
        codes = [lst[i * UNROLL + u] for u in range(UNROLL)]
        sums = []
        for u, code in enumerate(codes):
            block = (code >> 13) & 31
            scores = jnp.where(((code >> 12) & 1) == 0, near[block], far[block])
            sums.append(jnp.dot(w[i * UNROLL + u], scores, preferred_element_type=jnp.float32))
        for u, code in enumerate(codes):
            acc[code & 127] += sums[u]
        return carry

    lax.fori_loop(0, steps, step, 0)
    for b in range(QBLOCKS):
        send[b] = acc[b].astype(jnp.bfloat16)


def mix_kernel(got, base, weights, prior, marks, masked, denominator, own_second):
    row = lax.broadcasted_iota(jnp.int32, (FRAMES, CH), 0)
    lane = lax.broadcasted_iota(jnp.int32, (FRAMES, CH), 1)
    pick = (row == lane % FRAMES).astype(jnp.float32)
    for b in range(PART):
        total = base[b, :, :CH]
        for d in range(NY * NX):
            total = total + got[d, b * FRAMES:(b + 1) * FRAMES, :].astype(jnp.float32)
        mass = jnp.sum(got[:, PIECE:SEND, :].astype(jnp.float32), axis=0)[b:b + 1, :]
        column = jnp.sum(pick * mass, axis=1, keepdims=True)
        full = 1.0 + column + base[b, :, CH:]
        denominator[b] = full
        mixed = keep_share * total / full + (1.0 - keep_share) * prior[b].astype(jnp.float32)
        keep = (mixed.astype(jnp.bfloat16).astype(jnp.float32) * marks[b].astype(jnp.float32)).astype(jnp.bfloat16)
        for d in range(NZ):
            masked[d, b] = keep
        own_second[b] = jnp.dot(weights[b], keep, preferred_element_type=jnp.float32)


def last_kernel(got, own_second, denominator, prior, out):
    for b in range(PART):
        total = own_second[b]
        for d in range(NY * NX):
            total = total + got[d, b].astype(jnp.float32)
        mixed = keep_share * total / denominator[b]
        out[b] = (mixed + (1.0 - keep_share) * prior[b].astype(jnp.float32)).astype(jnp.bfloat16)


smem = pl.BlockSpec(memory_space=pltpu.SMEM)
vmem = pl.BlockSpec(memory_space=pltpu.VMEM)
hbm = pl.BlockSpec(memory_space=pl.ANY)
params = pltpu.CompilerParams(vmem_limit_bytes=VMEM)


def normalize(values):
    floats = values.astype(jnp.float32)
    return (floats * lax.rsqrt(jnp.sum(floats * floats, axis=-1, keepdims=True) + epsilon)).astype(jnp.bfloat16)


def body(embeddings, prior_scores, frame_valid, neighbour_ids, neighbour_count, block_home):
    per_list = neighbour_ids.shape[1]
    y, z, c, x = (lax.axis_index(a) for a in ("y", "z", "c", "x"))
    first = x * PART
    units = normalize(lax.dynamic_slice_in_dim(embeddings, first, PART, 0))
    prior = lax.dynamic_slice_in_dim(prior_scores, first, PART, 0)
    valid = lax.dynamic_slice_in_dim(frame_valid, first, PART, 0)
    marks = jnp.broadcast_to(valid[:, :, None], prior.shape).astype(jnp.bfloat16)
    marked = jnp.where(marks > 0, prior, jnp.bfloat16(2 * UNREAL))
    piece = jnp.concatenate([units, marked], axis=-1).reshape(PIECE, WIDE)

    target = jnp.take(block_home, neighbour_ids.reshape(-1), axis=0)
    column = x * per_list + jnp.arange(per_list, dtype=jnp.int32)
    in_list = (column[None, :] < neighbour_count[:, None]).reshape(-1)
    numbers = jnp.concatenate([jnp.where(in_list, target // 32, -1), target % 32]).astype(jnp.bfloat16)
    numbers = jnp.pad(numbers[None, :], ((0, CELL - SHARED_ROWS - 1), (0, FEAT - 2 * ROWS * per_list)))
    shared = jnp.concatenate([units[:SHARED].reshape(SHARED_ROWS, FEAT), numbers], axis=0)

    shared = lax.all_gather(shared, ("y", "x"), axis=0)
    up, down = shift(piece, "z", 1), shift(piece, "z", -1)
    embeddings, piece = lax.optimization_barrier((embeddings, piece))
    all_units = normalize(embeddings)
    straight = all_units.reshape(NX, PART, FRAMES, FEAT)[:, SHARED:].reshape(STRAIGHT * FRAMES, FEAT)
    behind, ahead = shift(straight, "y", 1), shift(straight, "y", -1)

    up, down = lax.optimization_barrier((up, down))
    near = [piece, up, down]
    far = [shift(v, "c", 1) for v in near]
    up, down = shift(up, "z", 1), shift(down, "z", -1)

    up, down, behind, ahead = lax.optimization_barrier((up, down, behind, ahead))
    half = STRAIGHT * FRAMES // 2
    across_a, across_b = shift(behind[:half], "y", 1), shift(ahead[half:], "y", -1)
    held = [up, down]
    up, down = shift(up, "z", 1), shift(down, "z", -1)
    near += held
    far += [shift(v, "c", 1) for v in held]
    own_weights, own_base = pl.pallas_call(
        own_kernel,
        out_shape=(
            jax.ShapeDtypeStruct((PART, FRAMES, FRAMES), jnp.bfloat16),
            jax.ShapeDtypeStruct((PART, FRAMES, 2 * CH), jnp.float32),
        ),
        in_specs=[vmem],
        out_specs=(vmem, vmem),
    )(piece)

    last_up, last_down = shift(up[:HALF], "z", 1), shift(down[HALF:], "z", -1)
    near += [up, down]
    far += [shift(up, "c", 1), shift(down, "c", 1)]
    across = jnp.concatenate([across_a, across_b], axis=0)

    shared, _, own_base = lax.optimization_barrier((shared, up, own_base))
    entries = ROWS * per_list
    numbers = shared[:, SHARED_ROWS, :2 * entries].astype(jnp.int32)
    target = (numbers[:, :entries] * 32 + numbers[:, entries:]).reshape(NY, NX, ROWS, per_list)
    source_y = jnp.arange(NY, dtype=jnp.int32)[:, None, None, None]
    source_row = jnp.arange(ROWS, dtype=jnp.int32)[None, None, :, None]
    distance = (source_y - y) % NY
    source = source_y * ROWS + source_row
    wanted = (target >= 0) & (target // 256 == y) & ((target % 16) // PART == x)
    place = (target // 16) % 16
    apart = (place // 2 - z) % NZ
    order = jnp.where(
        apart == 0, 0, jnp.where(apart < 4, 2 * apart, jnp.where(apart == 4, 7, 2 * (NZ - apart) - 1))
    )
    inner = target % PART
    side = (place % 2) ^ c
    quarter, within = source_row // PART, source_row % PART
    taken = jnp.where(
        distance == 0,
        source_row,
        jnp.where(
            within < SHARED,
            Q_SHARED + (source_y * NX + quarter) * SHARED + within,
            ROWS + (distance - 1) * STRAIGHT + quarter * (PART - SHARED) + within - SHARED,
        ),
    )
    codes = source | ((order * PART + inner) << 7) | (side << 12) | (((place // 2) * PART + inner) << 13) | (taken << 18)
    codes = jnp.where(wanted, codes, -1).reshape(-1)
    lst = pl.pallas_call(
        list_kernel,
        out_shape=jax.ShapeDtypeStruct((LIST,), jnp.int32),
        in_specs=[smem],
        out_specs=smem,
    )(codes)

    last_up, last_down, lst = lax.optimization_barrier((last_up, last_down, lst))
    near += [last_up, last_down]
    far += [shift(last_up, "c", 1), shift(last_down, "c", 1)]

    send, weights = pl.pallas_call(
        first_kernel,
        out_shape=(
            jax.ShapeDtypeStruct((NY * NX, SEND, CH), jnp.bfloat16),
            jax.ShapeDtypeStruct((SLOTS, FRAMES, FRAMES), jnp.bfloat16),
        ),
        in_specs=[smem] + [hbm] * 23,
        out_specs=(vmem, hbm),
        scratch_shapes=[
            pltpu.VMEM((Q_ALL * FRAMES, FEAT), jnp.bfloat16),
            pltpu.VMEM((NC, NZ * PIECE, WIDE), jnp.bfloat16),
            pltpu.VMEM((QBLOCKS + 1, FRAMES, 2 * CH), jnp.float32),
            pltpu.VMEM((SLOTS, FRAMES, FRAMES), jnp.bfloat16),
            pltpu.SemaphoreType.DMA((22 + NY * NX,)),
            pltpu.SemaphoreType.DMA,
        ],
        compiler_params=params,
    )(lst, *near, *far, all_units.reshape(ROWS * FRAMES, FEAT), ahead, across, behind, shared)
    got = lax.all_to_all(send, ("y", "x"), split_axis=0, concat_axis=0, tiled=True)

    masked, denominator, own_second = pl.pallas_call(
        mix_kernel,
        out_shape=(
            jax.ShapeDtypeStruct((NZ, PART, FRAMES, CH), jnp.bfloat16),
            jax.ShapeDtypeStruct((PART, FRAMES, CH), jnp.float32),
            jax.ShapeDtypeStruct((PART, FRAMES, CH), jnp.float32),
        ),
        in_specs=[vmem] * 5,
        out_specs=(vmem,) * 3,
    )(got, own_base, own_weights, prior, marks)
    near_scores = lax.all_to_all(masked, "z", split_axis=0, concat_axis=0, tiled=True)
    near_scores = near_scores.reshape(NZ * PART, FRAMES, CH)
    far_scores = shift(near_scores, "c", 1)

    send = pl.pallas_call(
        second_kernel,
        out_shape=jax.ShapeDtypeStruct((QBLOCKS, FRAMES, CH), jnp.bfloat16),
        in_specs=[smem, hbm, vmem, vmem],
        out_specs=vmem,
        scratch_shapes=[
            pltpu.VMEM((QBLOCKS + 1, FRAMES, CH), jnp.float32),
            pltpu.VMEM((SLOTS, FRAMES, FRAMES), jnp.bfloat16),
            pltpu.SemaphoreType.DMA,
        ],
        compiler_params=params,
    )(lst, weights, near_scores, far_scores)
    got = lax.all_to_all(send, ("y", "x"), split_axis=0, concat_axis=0, tiled=True)
    return pl.pallas_call(
        last_kernel,
        out_shape=jax.ShapeDtypeStruct((PART, FRAMES, CH), jnp.bfloat16),
        in_specs=[vmem] * 4,
        out_specs=vmem,
    )(got.reshape(NY * NX, PART, FRAMES, CH), own_second, denominator, prior)


def solution(mesh):
    fine = Mesh(mesh.devices.reshape(NY, NZ, NC, NX), ("y", "z", "c", "x"))
    bucket = ("y", "z", "c")
    in_specs = (P(bucket, None, None), P(bucket, None, None), P(bucket, None), P(bucket, "x"), P(bucket), P())
    out_specs = P(("y", "z", "c", "x"), None, None)
    return jax.shard_map(body, mesh=fine, in_specs=in_specs, out_specs=out_specs, check_vma=False)
```

```python
import math

import jax
import jax.numpy as jnp
from jax import lax
from jax.experimental import pallas as pl
from jax.experimental.pallas import tpu as pltpu
from jax.sharding import Mesh
from jax.sharding import PartitionSpec as P

epsilon = 1e-06
keep_share = 0.9

NY, NZ, NC, NX = 4, 8, 2, 4
ROWS = 16
FRAMES = 64
FEAT = 1152
CH = 128
PART = ROWS // NX
STRAIGHT = NX * (PART - 1)
QBLOCKS = NY * ROWS
Q_TURN = ROWS + (NY - 1) * STRAIGHT
UNROLL = 8
SLOTS = 520
WIDE = FEAT + CH
PIECE = PART * FRAMES
SEND = PIECE + 16
LIST = 640
STEPS_AT = 600
SPARE = QBLOCKS
VMEM = 56 * 1024 * 1024
UNREAL = 1024.0
sharpness = 2.0 * math.sqrt(FEAT)


def shift(value, axis, step):
    size = lax.axis_size(axis)
    return lax.ppermute(value, axis, [(i, (i + step) % size) for i in range(size)])


def list_kernel(codes, out):
    def eight(i, count):
        for u in range(8):
            code = codes[i * 8 + u]
            out[count] = code
            count = count + jnp.where(code >= 0, 1, 0)
        return count

    count = lax.fori_loop(0, QBLOCKS * 32 // 8, eight, 0)
    for u in range(UNROLL):
        out[count + u] = SPARE
    out[STEPS_AT] = (count + UNROLL - 1) // UNROLL


def own_kernel(piece, own_weights, own_base):
    row = lax.broadcasted_iota(jnp.int32, (FRAMES, FRAMES), 0)
    col = lax.broadcasted_iota(jnp.int32, (FRAMES, FRAMES), 1)
    for b in range(PART):
        block = piece[b * FRAMES:(b + 1) * FRAMES, :]
        units = block[:, :FEAT]
        affinity = lax.dot_general(
            units, units, (((1,), (1,)), ((), ())), preferred_element_type=jnp.float32
        )
        weights = jnp.where(row == col, 0.0, jnp.exp(sharpness * affinity)).astype(jnp.bfloat16)
        own_weights[b] = weights
        own_base[b] = jnp.dot(weights, values_of(block[:, FEAT:]), preferred_element_type=jnp.float32)


def values_of(scores):
    floats = scores.astype(jnp.float32)
    real = floats < UNREAL
    return jnp.concatenate(
        [jnp.where(real, floats, 0.0), jnp.where(real, 1.0, 0.0)], axis=1
    ).astype(jnp.bfloat16)


def first_kernel(lst, keys, *refs):
    queries = refs[:9]
    send, weights_out, q, k, acc, w, sems, out_sem = refs[9:]
    copies = [pltpu.make_async_copy(keys, k, sems.at[0])]
    at = 0
    for part in queries:
        rows = part.shape[0]
        copies.append(pltpu.make_async_copy(part, q.at[pl.ds(at, rows)], sems.at[len(copies)]))
        at += rows
    for copy in copies:
        copy.start()
    acc[...] = jnp.zeros_like(acc)
    for copy in copies:
        copy.wait()
    steps = lst[STEPS_AT]

    def step(i, carry):
        codes = [lst[i * UNROLL + u] for u in range(UNROLL)]
        key_rows = [pl.multiple_of(((code >> 7) & 63) * FRAMES, FRAMES) for code in codes]
        query_rows = [pl.multiple_of(((code >> 13) & 63) * FRAMES, FRAMES) for code in codes]
        weights = []
        for query_row, key_row in zip(query_rows, key_rows):
            affinity = lax.dot_general(
                q[pl.ds(query_row, FRAMES), :],
                k[pl.ds(key_row, FRAMES), pl.ds(0, FEAT)],
                (((1,), (1,)), ((), ())),
                preferred_element_type=jnp.float32,
            )
            weights.append(jnp.exp(sharpness * affinity).astype(jnp.bfloat16))
        for u in range(UNROLL):
            w[i * UNROLL + u] = weights[u]
        sums = []
        for u, key_row in enumerate(key_rows):
            values = values_of(k[pl.ds(key_row, FRAMES), pl.ds(FEAT, CH)])
            sums.append(jnp.dot(weights[u], values, preferred_element_type=jnp.float32))
        for u, code in enumerate(codes):
            acc[code & 127] += sums[u]
        group = pl.ds(i * UNROLL, UNROLL)
        pltpu.make_async_copy(w.at[group], weights_out.at[group], out_sem).start()
        return carry

    lax.fori_loop(0, steps, step, 0)
    row = lax.broadcasted_iota(jnp.int32, (FRAMES, CH), 0)
    lane = lax.broadcasted_iota(jnp.int32, (FRAMES, CH), 1)
    pick = row == lane % FRAMES
    low = lax.broadcasted_iota(jnp.int32, (1, CH), 1) < FRAMES

    def finish(d, carry):
        rows = []
        for b in range(PART):
            block = acc[d * PART + b]
            send[d, b * FRAMES:(b + 1) * FRAMES, :] = block[:, :CH].astype(jnp.bfloat16)
            mass = jnp.sum(jnp.where(pick, block[:, CH:], 0.0), axis=0, keepdims=True)
            coarse = mass.astype(jnp.bfloat16).astype(jnp.float32)
            rows.append(jnp.where(low, coarse, mass - coarse))
        rows.append(jnp.zeros((16 - PART, CH), jnp.float32))
        send[d, PIECE:SEND, :] = jnp.concatenate(rows, axis=0).astype(jnp.bfloat16)
        return carry

    lax.fori_loop(0, NY * NX, finish, 0)

    def drain(i, carry):
        group = pl.ds(i * UNROLL, UNROLL)
        pltpu.make_async_copy(w.at[group], weights_out.at[group], out_sem).wait()
        return carry

    lax.fori_loop(0, steps, drain, 0)


def second_kernel(lst, weights_in, near, far, send, acc, w, in_sem):
    steps = lst[STEPS_AT]

    def fetch(i, carry):
        group = pl.ds(i * UNROLL, UNROLL)
        pltpu.make_async_copy(weights_in.at[group], w.at[group], in_sem).start()
        return carry

    lax.fori_loop(0, steps, fetch, 0)
    acc[...] = jnp.zeros_like(acc)

    def drain(i, carry):
        group = pl.ds(i * UNROLL, UNROLL)
        pltpu.make_async_copy(weights_in.at[group], w.at[group], in_sem).wait()
        return carry

    lax.fori_loop(0, steps, drain, 0)

    def step(i, carry):
        codes = [lst[i * UNROLL + u] for u in range(UNROLL)]
        sums = []
        for u, code in enumerate(codes):
            block = (code >> 21) & 31
            scores = jnp.where(((code >> 20) & 1) == 0, near[block], far[block])
            sums.append(jnp.dot(w[i * UNROLL + u], scores, preferred_element_type=jnp.float32))
        for u, code in enumerate(codes):
            acc[code & 127] += sums[u]
        return carry

    lax.fori_loop(0, steps, step, 0)
    for b in range(QBLOCKS):
        send[b] = acc[b].astype(jnp.bfloat16)


def mix_kernel(got, base, weights, prior, marks, masked, denominator, own_second):
    row = lax.broadcasted_iota(jnp.int32, (FRAMES, CH), 0)
    lane = lax.broadcasted_iota(jnp.int32, (FRAMES, CH), 1)
    pick = (row == lane % FRAMES).astype(jnp.float32)
    for b in range(PART):
        total = base[b, :, :CH]
        for d in range(NY * NX):
            total = total + got[d, b * FRAMES:(b + 1) * FRAMES, :].astype(jnp.float32)
        mass = jnp.sum(got[:, PIECE:SEND, :].astype(jnp.float32), axis=0)[b:b + 1, :]
        column = jnp.sum(pick * mass, axis=1, keepdims=True)
        full = 1.0 + column + base[b, :, CH:]
        denominator[b] = full
        mixed = keep_share * total / full + (1.0 - keep_share) * prior[b].astype(jnp.float32)
        keep = (mixed.astype(jnp.bfloat16).astype(jnp.float32) * marks[b].astype(jnp.float32)).astype(jnp.bfloat16)
        for d in range(NZ):
            masked[d, b] = keep
        own_second[b] = jnp.dot(weights[b], keep, preferred_element_type=jnp.float32)


def last_kernel(got, own_second, denominator, prior, out):
    for b in range(PART):
        total = own_second[b]
        for d in range(NY * NX):
            total = total + got[d, b].astype(jnp.float32)
        mixed = keep_share * total / denominator[b]
        out[b] = (mixed + (1.0 - keep_share) * prior[b].astype(jnp.float32)).astype(jnp.bfloat16)


smem = pl.BlockSpec(memory_space=pltpu.SMEM)
vmem = pl.BlockSpec(memory_space=pltpu.VMEM)
hbm = pl.BlockSpec(memory_space=pl.ANY)
params = pltpu.CompilerParams(vmem_limit_bytes=VMEM)


def normalize(values):
    floats = values.astype(jnp.float32)
    return (floats * lax.rsqrt(jnp.sum(floats * floats, axis=-1, keepdims=True) + epsilon)).astype(jnp.bfloat16)


def body(embeddings, prior_scores, frame_valid, neighbour_ids, neighbour_count, block_home):
    per_list = neighbour_ids.shape[1]
    y, z, c, x = (lax.axis_index(a) for a in ("y", "z", "c", "x"))
    first = x * PART
    units = normalize(lax.dynamic_slice_in_dim(embeddings, first, PART, 0))
    prior = lax.dynamic_slice_in_dim(prior_scores, first, PART, 0)
    valid = lax.dynamic_slice_in_dim(frame_valid, first, PART, 0)
    marks = jnp.broadcast_to(valid[:, :, None], prior.shape).astype(jnp.bfloat16)
    marked = jnp.where(marks > 0, prior, jnp.bfloat16(2 * UNREAL))
    piece = jnp.concatenate([units, marked], axis=-1).reshape(PIECE, WIDE)

    keys = lax.all_gather(piece, ("z", "c"), axis=0, tiled=True)

    embeddings, piece = lax.optimization_barrier((embeddings, piece))
    turn = units[0]
    turned = [shift(turn, "y", -1), shift(turn, "y", 2), shift(turn, "y", 1)]
    all_units = normalize(embeddings)
    straight = all_units.reshape(NX, PART, FRAMES, FEAT)[:, 1:].reshape(STRAIGHT * FRAMES, FEAT)
    turned, straight = lax.optimization_barrier((turned, straight))
    behind, ahead = shift(straight, "y", 1), shift(straight, "y", -1)

    turned = jnp.concatenate(turned, axis=0)
    ids, block_home, turned = lax.optimization_barrier((neighbour_ids, block_home, turned))
    target = jnp.take(block_home, ids.reshape(-1), axis=0)
    column = x * per_list + jnp.arange(per_list, dtype=jnp.int32)
    in_list = (column[None, :] < neighbour_count[:, None]).reshape(-1)
    target = lax.all_gather(jnp.where(in_list, target, -1), ("y", "x"), axis=0)

    turned = [turned, shift(turned, "x", -1), shift(turned, "x", 2), shift(turned, "x", 1)]
    half = STRAIGHT * FRAMES // 2
    across = [shift(behind[:half], "y", 1), shift(ahead[half:], "y", -1)]

    target = target.reshape(NY, NX, ROWS, per_list)
    source_y = jnp.arange(NY, dtype=jnp.int32)[:, None, None, None]
    source_row = jnp.arange(ROWS, dtype=jnp.int32)[None, None, :, None]
    distance = (source_y - y) % NY
    source = source_y * ROWS + source_row
    wanted = (target >= 0) & (target // 256 == y) & ((target % 16) // PART == x)
    place = (target // 16) % 16
    inner = target % PART
    side = (place % 2) ^ c
    quarter, within = source_row // PART, source_row % PART
    taken = jnp.where(
        distance == 0,
        source_row,
        jnp.where(
            within == 0,
            Q_TURN + ((quarter - x) % NX) * (NY - 1) + distance - 1,
            ROWS + (distance - 1) * STRAIGHT + quarter * (PART - 1) + within - 1,
        ),
    )
    codes = source | ((place * PART + inner) << 7) | (taken << 13) | (side << 20) | (((place // 2) * PART + inner) << 21)
    codes = jnp.where(wanted, codes, -1).reshape(-1)
    lst = pl.pallas_call(
        list_kernel,
        out_shape=jax.ShapeDtypeStruct((LIST,), jnp.int32),
        in_specs=[smem],
        out_specs=smem,
    )(codes)
    own_weights, own_base = pl.pallas_call(
        own_kernel,
        out_shape=(
            jax.ShapeDtypeStruct((PART, FRAMES, FRAMES), jnp.bfloat16),
            jax.ShapeDtypeStruct((PART, FRAMES, 2 * CH), jnp.float32),
        ),
        in_specs=[vmem],
        out_specs=(vmem, vmem),
    )(piece)

    send, weights = pl.pallas_call(
        first_kernel,
        out_shape=(
            jax.ShapeDtypeStruct((NY * NX, SEND, CH), jnp.bfloat16),
            jax.ShapeDtypeStruct((SLOTS, FRAMES, FRAMES), jnp.bfloat16),
        ),
        in_specs=[smem] + [hbm] * 10,
        out_specs=(vmem, hbm),
        scratch_shapes=[
            pltpu.VMEM((QBLOCKS * FRAMES, FEAT), jnp.bfloat16),
            pltpu.VMEM((NZ * NC * PIECE, WIDE), jnp.bfloat16),
            pltpu.VMEM((QBLOCKS + 1, FRAMES, 2 * CH), jnp.float32),
            pltpu.VMEM((SLOTS, FRAMES, FRAMES), jnp.bfloat16),
            pltpu.SemaphoreType.DMA((10,)),
            pltpu.SemaphoreType.DMA,
        ],
        compiler_params=params,
    )(lst, keys, all_units.reshape(ROWS * FRAMES, FEAT), ahead, *across, behind, *turned)
    got = lax.all_to_all(send, ("y", "x"), split_axis=0, concat_axis=0, tiled=True)

    masked, denominator, own_second = pl.pallas_call(
        mix_kernel,
        out_shape=(
            jax.ShapeDtypeStruct((NZ, PART, FRAMES, CH), jnp.bfloat16),
            jax.ShapeDtypeStruct((PART, FRAMES, CH), jnp.float32),
            jax.ShapeDtypeStruct((PART, FRAMES, CH), jnp.float32),
        ),
        in_specs=[vmem] * 5,
        out_specs=(vmem,) * 3,
    )(got, own_base, own_weights, prior, marks)
    near_scores = lax.all_to_all(masked, "z", split_axis=0, concat_axis=0, tiled=True)
    near_scores = near_scores.reshape(NZ * PART, FRAMES, CH)
    far_scores = shift(near_scores, "c", 1)

    send = pl.pallas_call(
        second_kernel,
        out_shape=jax.ShapeDtypeStruct((QBLOCKS, FRAMES, CH), jnp.bfloat16),
        in_specs=[smem, hbm, vmem, vmem],
        out_specs=vmem,
        scratch_shapes=[
            pltpu.VMEM((QBLOCKS + 1, FRAMES, CH), jnp.float32),
            pltpu.VMEM((SLOTS, FRAMES, FRAMES), jnp.bfloat16),
            pltpu.SemaphoreType.DMA,
        ],
        compiler_params=params,
    )(lst, weights, near_scores, far_scores)
    got = lax.all_to_all(send, ("y", "x"), split_axis=0, concat_axis=0, tiled=True)
    return pl.pallas_call(
        last_kernel,
        out_shape=jax.ShapeDtypeStruct((PART, FRAMES, CH), jnp.bfloat16),
        in_specs=[vmem] * 4,
        out_specs=vmem,
    )(got.reshape(NY * NX, PART, FRAMES, CH), own_second, denominator, prior)


def solution(mesh):
    fine = Mesh(mesh.devices.reshape(NY, NZ, NC, NX), ("y", "z", "c", "x"))
    bucket = ("y", "z", "c")
    in_specs = (P(bucket, None, None), P(bucket, None, None), P(bucket, None), P(bucket, "x"), P(bucket), P())
    out_specs = P(("y", "z", "c", "x"), None, None)
    return jax.shard_map(body, mesh=fine, in_specs=in_specs, out_specs=out_specs, check_vma=False)
```

```python
import math

import jax
import jax.numpy as jnp
from jax import lax
from jax.experimental import pallas as pl
from jax.experimental.pallas import tpu as pltpu
from jax.sharding import Mesh
from jax.sharding import PartitionSpec as P

epsilon = 1e-06
keep_share = 0.9

NY, NZ, NC, NX = 4, 8, 2, 4
ROWS = 16
FRAMES = 64
FEAT = 1152
CH = 128
PART = ROWS // NX
STRAIGHT = NX * (PART - 1)
QBLOCKS = NY * ROWS
Q_TURN = ROWS + (NY - 1) * STRAIGHT
UNROLL = 8
SLOTS = 520
WIDE = FEAT + CH
PIECE = PART * FRAMES
SEND = PIECE + 16
LIST = 640
STEPS_AT = 600
SPARE = QBLOCKS
UNREAL = 1024.0
sharpness = 2.0 * math.sqrt(FEAT)


def shift(value, axis, step):
    size = lax.axis_size(axis)
    return lax.ppermute(value, axis, [(i, (i + step) % size) for i in range(size)])


def list_kernel(codes, out):
    def eight(i, count):
        for u in range(8):
            code = codes[i * 8 + u]
            out[count] = code
            count = count + jnp.where(code >= 0, 1, 0)
        return count

    count = lax.fori_loop(0, QBLOCKS * 32 // 8, eight, 0)
    for u in range(UNROLL):
        out[count + u] = SPARE
    out[STEPS_AT] = (count + UNROLL - 1) // UNROLL


def own_kernel(piece, own_weights, own_base):
    row = lax.broadcasted_iota(jnp.int32, (FRAMES, FRAMES), 0)
    col = lax.broadcasted_iota(jnp.int32, (FRAMES, FRAMES), 1)
    for b in range(PART):
        block = piece[b * FRAMES:(b + 1) * FRAMES, :]
        units = block[:, :FEAT]
        affinity = lax.dot_general(
            units, units, (((1,), (1,)), ((), ())), preferred_element_type=jnp.float32
        )
        weights = jnp.where(row == col, 0.0, jnp.exp(sharpness * affinity)).astype(jnp.bfloat16)
        own_weights[b] = weights
        own_base[b] = jnp.dot(weights, values_of(block[:, FEAT:]), preferred_element_type=jnp.float32)


def values_of(scores):
    floats = scores.astype(jnp.float32)
    real = floats < UNREAL
    return jnp.concatenate(
        [jnp.where(real, floats, 0.0), jnp.where(real, 1.0, 0.0)], axis=1
    ).astype(jnp.bfloat16)


def first_kernel(lst, keys, *refs):
    queries = refs[:9]
    send, weights_out, q, k, acc, w, sems, out_sem = refs[9:]
    copies = [pltpu.make_async_copy(keys, k, sems.at[0])]
    at = 0
    for part in queries:
        rows = part.shape[0]
        copies.append(pltpu.make_async_copy(part, q.at[pl.ds(at, rows)], sems.at[len(copies)]))
        at += rows
    for copy in copies:
        copy.start()
    acc[...] = jnp.zeros_like(acc)
    for copy in copies:
        copy.wait()
    steps = lst[STEPS_AT]

    def step(i, carry):
        codes = [lst[i * UNROLL + u] for u in range(UNROLL)]
        key_rows = [pl.multiple_of(((code >> 7) & 63) * FRAMES, FRAMES) for code in codes]
        query_rows = [pl.multiple_of(((code >> 13) & 63) * FRAMES, FRAMES) for code in codes]
        weights = []
        for query_row, key_row in zip(query_rows, key_rows):
            affinity = lax.dot_general(
                q[pl.ds(query_row, FRAMES), :],
                k[pl.ds(key_row, FRAMES), pl.ds(0, FEAT)],
                (((1,), (1,)), ((), ())),
                preferred_element_type=jnp.float32,
            )
            weights.append(jnp.exp(sharpness * affinity).astype(jnp.bfloat16))
        for u in range(UNROLL):
            w[i * UNROLL + u] = weights[u]
        sums = []
        for u, key_row in enumerate(key_rows):
            values = values_of(k[pl.ds(key_row, FRAMES), pl.ds(FEAT, CH)])
            sums.append(jnp.dot(weights[u], values, preferred_element_type=jnp.float32))
        for u, code in enumerate(codes):
            acc[code & 127] += sums[u]
        group = pl.ds(i * UNROLL, UNROLL)
        pltpu.make_async_copy(w.at[group], weights_out.at[group], out_sem).start()
        return carry

    lax.fori_loop(0, steps, step, 0)
    row = lax.broadcasted_iota(jnp.int32, (FRAMES, CH), 0)
    lane = lax.broadcasted_iota(jnp.int32, (FRAMES, CH), 1)
    pick = row == lane % FRAMES
    low = lax.broadcasted_iota(jnp.int32, (1, CH), 1) < FRAMES

    def finish(d, carry):
        rows = []
        for b in range(PART):
            block = acc[d * PART + b]
            send[d, b * FRAMES:(b + 1) * FRAMES, :] = block[:, :CH].astype(jnp.bfloat16)
            mass = jnp.sum(jnp.where(pick, block[:, CH:], 0.0), axis=0, keepdims=True)
            coarse = mass.astype(jnp.bfloat16).astype(jnp.float32)
            rows.append(jnp.where(low, coarse, mass - coarse))
        rows.append(jnp.zeros((16 - PART, CH), jnp.float32))
        send[d, PIECE:SEND, :] = jnp.concatenate(rows, axis=0).astype(jnp.bfloat16)
        return carry

    lax.fori_loop(0, NY * NX, finish, 0)

    def drain(i, carry):
        group = pl.ds(i * UNROLL, UNROLL)
        pltpu.make_async_copy(w.at[group], weights_out.at[group], out_sem).wait()
        return carry

    lax.fori_loop(0, steps, drain, 0)


def second_kernel(lst, weights_in, near, far, send, acc, w, in_sem):
    steps = lst[STEPS_AT]

    def fetch(i, carry):
        group = pl.ds(i * UNROLL, UNROLL)
        pltpu.make_async_copy(weights_in.at[group], w.at[group], in_sem).start()
        return carry

    lax.fori_loop(0, steps, fetch, 0)
    acc[...] = jnp.zeros_like(acc)

    def drain(i, carry):
        group = pl.ds(i * UNROLL, UNROLL)
        pltpu.make_async_copy(weights_in.at[group], w.at[group], in_sem).wait()
        return carry

    lax.fori_loop(0, steps, drain, 0)

    def step(i, carry):
        codes = [lst[i * UNROLL + u] for u in range(UNROLL)]
        sums = []
        for u, code in enumerate(codes):
            block = (code >> 21) & 31
            scores = jnp.where(((code >> 20) & 1) == 0, near[block], far[block])
            sums.append(jnp.dot(w[i * UNROLL + u], scores, preferred_element_type=jnp.float32))
        for u, code in enumerate(codes):
            acc[code & 127] += sums[u]
        return carry

    lax.fori_loop(0, steps, step, 0)
    for b in range(QBLOCKS):
        send[b] = acc[b].astype(jnp.bfloat16)


def mix_kernel(got, base, weights, prior, marks, masked, denominator, own_second):
    row = lax.broadcasted_iota(jnp.int32, (FRAMES, CH), 0)
    lane = lax.broadcasted_iota(jnp.int32, (FRAMES, CH), 1)
    pick = (row == lane % FRAMES).astype(jnp.float32)
    for b in range(PART):
        total = base[b, :, :CH]
        for d in range(NY * NX):
            total = total + got[d, b * FRAMES:(b + 1) * FRAMES, :].astype(jnp.float32)
        mass = jnp.sum(got[:, PIECE:SEND, :].astype(jnp.float32), axis=0)[b:b + 1, :]
        column = jnp.sum(pick * mass, axis=1, keepdims=True)
        full = 1.0 + column + base[b, :, CH:]
        denominator[b] = full
        mixed = keep_share * total / full + (1.0 - keep_share) * prior[b].astype(jnp.float32)
        keep = (mixed.astype(jnp.bfloat16).astype(jnp.float32) * marks[b].astype(jnp.float32)).astype(jnp.bfloat16)
        for d in range(NZ):
            masked[d, b] = keep
        own_second[b] = jnp.dot(weights[b], keep, preferred_element_type=jnp.float32)


def last_kernel(got, own_second, denominator, prior, out):
    for b in range(PART):
        total = own_second[b]
        for d in range(NY * NX):
            total = total + got[d, b].astype(jnp.float32)
        mixed = keep_share * total / denominator[b]
        out[b] = (mixed + (1.0 - keep_share) * prior[b].astype(jnp.float32)).astype(jnp.bfloat16)


smem = pl.BlockSpec(memory_space=pltpu.SMEM)
vmem = pl.BlockSpec(memory_space=pltpu.VMEM)
hbm = pl.BlockSpec(memory_space=pl.ANY)


def limit(mebibytes):
    return pltpu.CompilerParams(vmem_limit_bytes=mebibytes * 1024 * 1024)


def normalize(values):
    floats = values.astype(jnp.float32)
    return (floats * lax.rsqrt(jnp.sum(floats * floats, axis=-1, keepdims=True) + epsilon)).astype(jnp.bfloat16)


def body(embeddings, prior_scores, frame_valid, neighbour_ids, neighbour_count, block_home):
    per_list = neighbour_ids.shape[1]
    y, z, c, x = (lax.axis_index(a) for a in ("y", "z", "c", "x"))
    first = x * PART
    units = normalize(lax.dynamic_slice_in_dim(embeddings, first, PART, 0))
    prior = lax.dynamic_slice_in_dim(prior_scores, first, PART, 0)
    valid = lax.dynamic_slice_in_dim(frame_valid, first, PART, 0)
    marks = jnp.broadcast_to(valid[:, :, None], prior.shape).astype(jnp.bfloat16)
    marked = jnp.where(marks > 0, prior, jnp.bfloat16(2 * UNREAL))
    piece = jnp.concatenate([units, marked], axis=-1).reshape(PIECE, WIDE)

    keys = lax.all_gather(piece, ("z", "c"), axis=0, tiled=True)

    embeddings, piece = lax.optimization_barrier((embeddings, piece))
    turn = units[0]
    turned = [shift(turn, "y", -1), shift(turn, "y", 2), shift(turn, "y", 1)]
    all_units = normalize(embeddings)
    straight = all_units.reshape(NX, PART, FRAMES, FEAT)[:, 1:].reshape(STRAIGHT * FRAMES, FEAT)
    turned, straight = lax.optimization_barrier((turned, straight))
    behind, ahead = shift(straight, "y", 1), shift(straight, "y", -1)

    turned = jnp.concatenate(turned, axis=0)
    ids, block_home, turned = lax.optimization_barrier((neighbour_ids, block_home, turned))
    target = jnp.take(block_home, ids.reshape(-1), axis=0)
    column = x * per_list + jnp.arange(per_list, dtype=jnp.int32)
    in_list = (column[None, :] < neighbour_count[:, None]).reshape(-1)
    target = lax.all_gather(jnp.where(in_list, target, -1), ("y", "x"), axis=0)

    turned = [turned, shift(turned, "x", -1), shift(turned, "x", 2), shift(turned, "x", 1)]
    target = target.reshape(NY, NX, ROWS, per_list)
    source_y = jnp.arange(NY, dtype=jnp.int32)[:, None, None, None]
    source_row = jnp.arange(ROWS, dtype=jnp.int32)[None, None, :, None]
    distance = (source_y - y) % NY
    source = source_y * ROWS + source_row
    wanted = (target >= 0) & (target // 256 == y) & ((target % 16) // PART == x)
    place = (target // 16) % 16
    inner = target % PART
    side = (place % 2) ^ c
    quarter, within = source_row // PART, source_row % PART
    taken = jnp.where(
        distance == 0,
        source_row,
        jnp.where(
            within == 0,
            Q_TURN + ((quarter - x) % NX) * (NY - 1) + distance - 1,
            ROWS + (distance - 1) * STRAIGHT + quarter * (PART - 1) + within - 1,
        ),
    )
    codes = source | ((place * PART + inner) << 7) | (taken << 13) | (side << 20) | (((place // 2) * PART + inner) << 21)
    codes = jnp.where(wanted, codes, -1).reshape(-1)
    lst = pl.pallas_call(
        list_kernel,
        out_shape=jax.ShapeDtypeStruct((LIST,), jnp.int32),
        in_specs=[smem],
        out_specs=smem,
        compiler_params=limit(1),
    )(codes)
    half = STRAIGHT * FRAMES // 2
    behind, ahead, turned, lst = lax.optimization_barrier((behind, ahead, turned, lst))
    across = [shift(behind[:half], "y", 1), shift(ahead[half:], "y", -1)]
    own_weights, own_base = pl.pallas_call(
        own_kernel,
        out_shape=(
            jax.ShapeDtypeStruct((PART, FRAMES, FRAMES), jnp.bfloat16),
            jax.ShapeDtypeStruct((PART, FRAMES, 2 * CH), jnp.float32),
        ),
        in_specs=[vmem],
        out_specs=(vmem, vmem),
        compiler_params=limit(4),
    )(piece)

    send, weights = pl.pallas_call(
        first_kernel,
        out_shape=(
            jax.ShapeDtypeStruct((NY * NX, SEND, CH), jnp.bfloat16),
            jax.ShapeDtypeStruct((SLOTS, FRAMES, FRAMES), jnp.bfloat16),
        ),
        in_specs=[smem] + [hbm] * 10,
        out_specs=(vmem, hbm),
        scratch_shapes=[
            pltpu.VMEM((QBLOCKS * FRAMES, FEAT), jnp.bfloat16),
            pltpu.VMEM((NZ * NC * PIECE, WIDE), jnp.bfloat16),
            pltpu.VMEM((QBLOCKS + 1, FRAMES, 2 * CH), jnp.float32),
            pltpu.VMEM((SLOTS, FRAMES, FRAMES), jnp.bfloat16),
            pltpu.SemaphoreType.DMA((10,)),
            pltpu.SemaphoreType.DMA,
        ],
        compiler_params=limit(38),
    )(lst, keys, all_units.reshape(ROWS * FRAMES, FEAT), ahead, *across, behind, *turned)
    got = lax.all_to_all(send, ("y", "x"), split_axis=0, concat_axis=0, tiled=True)

    masked, denominator, own_second = pl.pallas_call(
        mix_kernel,
        out_shape=(
            jax.ShapeDtypeStruct((NZ, PART, FRAMES, CH), jnp.bfloat16),
            jax.ShapeDtypeStruct((PART, FRAMES, CH), jnp.float32),
            jax.ShapeDtypeStruct((PART, FRAMES, CH), jnp.float32),
        ),
        in_specs=[vmem] * 5,
        out_specs=(vmem,) * 3,
        compiler_params=limit(8),
    )(got, own_base, own_weights, prior, marks)
    near_scores = lax.all_to_all(masked, "z", split_axis=0, concat_axis=0, tiled=True)
    near_scores = near_scores.reshape(NZ * PART, FRAMES, CH)
    far_scores = shift(near_scores, "c", 1)

    send = pl.pallas_call(
        second_kernel,
        out_shape=jax.ShapeDtypeStruct((QBLOCKS, FRAMES, CH), jnp.bfloat16),
        in_specs=[smem, hbm, vmem, vmem],
        out_specs=vmem,
        scratch_shapes=[
            pltpu.VMEM((QBLOCKS + 1, FRAMES, CH), jnp.float32),
            pltpu.VMEM((SLOTS, FRAMES, FRAMES), jnp.bfloat16),
            pltpu.SemaphoreType.DMA,
        ],
        compiler_params=limit(16),
    )(lst, weights, near_scores, far_scores)
    got = lax.all_to_all(send, ("y", "x"), split_axis=0, concat_axis=0, tiled=True)
    return pl.pallas_call(
        last_kernel,
        out_shape=jax.ShapeDtypeStruct((PART, FRAMES, CH), jnp.bfloat16),
        in_specs=[vmem] * 4,
        out_specs=vmem,
        compiler_params=limit(8),
    )(got.reshape(NY * NX, PART, FRAMES, CH), own_second, denominator, prior)


def solution(mesh):
    fine = Mesh(mesh.devices.reshape(NY, NZ, NC, NX), ("y", "z", "c", "x"))
    bucket = ("y", "z", "c")
    in_specs = (P(bucket, None, None), P(bucket, None, None), P(bucket, None), P(bucket, "x"), P(bucket), P())
    out_specs = P(("y", "z", "c", "x"), None, None)
    return jax.shard_map(body, mesh=fine, in_specs=in_specs, out_specs=out_specs, check_vma=False)
```

```python
import math

import jax
import jax.numpy as jnp
from jax import lax
from jax.experimental import pallas as pl
from jax.experimental.pallas import tpu as pltpu
from jax.sharding import Mesh
from jax.sharding import PartitionSpec as P

epsilon = 1e-06
keep_share = 0.9

NY, NZ, NC, NX = 4, 8, 2, 4
ROWS = 16
FRAMES = 64
FEAT = 1152
CH = 128
PART = ROWS // NX
TURN = 2
STRAIGHT = NX * (PART - TURN)
QBLOCKS = NY * ROWS
Q_TURN = ROWS + (NY - 1) * STRAIGHT
UNROLL = 8
SLOTS = 520
WIDE = FEAT + CH
PIECE = PART * FRAMES
SEND = PIECE + 16
LIST = 640
STEPS_AT = 600
SPARE = QBLOCKS
UNREAL = 1024.0
sharpness = 2.0 * math.sqrt(FEAT)


def shift(value, axis, step):
    size = lax.axis_size(axis)
    return lax.ppermute(value, axis, [(i, (i + step) % size) for i in range(size)])


def list_kernel(codes, out):
    def eight(i, count):
        for u in range(8):
            code = codes[i * 8 + u]
            out[count] = code
            count = count + jnp.where(code >= 0, 1, 0)
        return count

    count = lax.fori_loop(0, QBLOCKS * 32 // 8, eight, 0)
    for u in range(UNROLL):
        out[count + u] = SPARE
    out[STEPS_AT] = (count + UNROLL - 1) // UNROLL


def own_kernel(piece, own_weights, own_base):
    row = lax.broadcasted_iota(jnp.int32, (FRAMES, FRAMES), 0)
    col = lax.broadcasted_iota(jnp.int32, (FRAMES, FRAMES), 1)
    for b in range(PART):
        block = piece[b * FRAMES:(b + 1) * FRAMES, :]
        units = block[:, :FEAT]
        affinity = lax.dot_general(
            units, units, (((1,), (1,)), ((), ())), preferred_element_type=jnp.float32
        )
        weights = jnp.where(row == col, 0.0, jnp.exp(sharpness * affinity)).astype(jnp.bfloat16)
        own_weights[b] = weights
        own_base[b] = jnp.dot(weights, values_of(block[:, FEAT:]), preferred_element_type=jnp.float32)


def values_of(scores):
    floats = scores.astype(jnp.float32)
    real = floats < UNREAL
    return jnp.concatenate(
        [jnp.where(real, floats, 0.0), jnp.where(real, 1.0, 0.0)], axis=1
    ).astype(jnp.bfloat16)


def first_kernel(lst, keys, *refs):
    queries = refs[:10]
    send, w, q, k, acc, sems = refs[10:]
    copies = [pltpu.make_async_copy(keys, k, sems.at[0])]
    at = 0
    for part in queries:
        rows = part.shape[0]
        copies.append(pltpu.make_async_copy(part, q.at[pl.ds(at, rows)], sems.at[len(copies)]))
        at += rows
    for copy in copies:
        copy.start()
    acc[...] = jnp.zeros_like(acc)
    for copy in copies:
        copy.wait()
    steps = lst[STEPS_AT]

    def step(i, carry):
        codes = [lst[i * UNROLL + u] for u in range(UNROLL)]
        key_rows = [pl.multiple_of(((code >> 7) & 63) * FRAMES, FRAMES) for code in codes]
        query_rows = [pl.multiple_of(((code >> 13) & 63) * FRAMES, FRAMES) for code in codes]
        weights = []
        for query_row, key_row in zip(query_rows, key_rows):
            affinity = lax.dot_general(
                q[pl.ds(query_row, FRAMES), :],
                k[pl.ds(key_row, FRAMES), pl.ds(0, FEAT)],
                (((1,), (1,)), ((), ())),
                preferred_element_type=jnp.float32,
            )
            weights.append(jnp.exp(sharpness * affinity).astype(jnp.bfloat16))
        for u in range(UNROLL // 2):
            w[i * (UNROLL // 2) + u] = jnp.concatenate(weights[2 * u:2 * u + 2], axis=1)
        sums = []
        for u, key_row in enumerate(key_rows):
            values = values_of(k[pl.ds(key_row, FRAMES), pl.ds(FEAT, CH)])
            sums.append(jnp.dot(weights[u], values, preferred_element_type=jnp.float32))
        for u, code in enumerate(codes):
            acc[code & 127] += sums[u]
        return carry

    lax.fori_loop(0, steps, step, 0)
    row = lax.broadcasted_iota(jnp.int32, (FRAMES, CH), 0)
    lane = lax.broadcasted_iota(jnp.int32, (FRAMES, CH), 1)
    pick = row == lane % FRAMES
    low = lax.broadcasted_iota(jnp.int32, (1, CH), 1) < FRAMES

    def finish(d, carry):
        rows = []
        for b in range(PART):
            block = acc[d * PART + b]
            send[d, b * FRAMES:(b + 1) * FRAMES, :] = block[:, :CH].astype(jnp.bfloat16)
            mass = jnp.sum(jnp.where(pick, block[:, CH:], 0.0), axis=0, keepdims=True)
            coarse = mass.astype(jnp.bfloat16).astype(jnp.float32)
            rows.append(jnp.where(low, coarse, mass - coarse))
        rows.append(jnp.zeros((16 - PART, CH), jnp.float32))
        send[d, PIECE:SEND, :] = jnp.concatenate(rows, axis=0).astype(jnp.bfloat16)
        return carry

    lax.fori_loop(0, NY * NX, finish, 0)


def second_kernel(lst, w, near, far, send, acc):
    steps = lst[STEPS_AT]
    acc[...] = jnp.zeros_like(acc)

    def step(i, carry):
        codes = [lst[i * UNROLL + u] for u in range(UNROLL)]
        sums = []
        for u, code in enumerate(codes):
            block = (code >> 21) & 31
            scores = jnp.where(((code >> 20) & 1) == 0, near[block], far[block])
            weights = w[i * (UNROLL // 2) + u // 2][:, (u % 2) * FRAMES:(u % 2 + 1) * FRAMES]
            sums.append(jnp.dot(weights, scores, preferred_element_type=jnp.float32))
        for u, code in enumerate(codes):
            acc[code & 127] += sums[u]
        return carry

    lax.fori_loop(0, steps, step, 0)
    for b in range(QBLOCKS):
        send[b] = acc[b].astype(jnp.bfloat16)


def mix_kernel(got, base, weights, prior, marks, masked, denominator, own_second):
    row = lax.broadcasted_iota(jnp.int32, (FRAMES, CH), 0)
    lane = lax.broadcasted_iota(jnp.int32, (FRAMES, CH), 1)
    pick = (row == lane % FRAMES).astype(jnp.float32)
    for b in range(PART):
        total = base[b, :, :CH]
        for d in range(NY * NX):
            total = total + got[d, b * FRAMES:(b + 1) * FRAMES, :].astype(jnp.float32)
        mass = jnp.sum(got[:, PIECE:SEND, :].astype(jnp.float32), axis=0)[b:b + 1, :]
        column = jnp.sum(pick * mass, axis=1, keepdims=True)
        full = 1.0 + column + base[b, :, CH:]
        denominator[b] = full
        mixed = keep_share * total / full + (1.0 - keep_share) * prior[b].astype(jnp.float32)
        keep = (mixed.astype(jnp.bfloat16).astype(jnp.float32) * marks[b].astype(jnp.float32)).astype(jnp.bfloat16)
        for d in range(NZ):
            masked[d, b] = keep
        own_second[b] = jnp.dot(weights[b], keep, preferred_element_type=jnp.float32)


def last_kernel(got, own_second, denominator, prior, out):
    for b in range(PART):
        total = own_second[b]
        for d in range(NY * NX):
            total = total + got[d, b].astype(jnp.float32)
        mixed = keep_share * total / denominator[b]
        out[b] = (mixed + (1.0 - keep_share) * prior[b].astype(jnp.float32)).astype(jnp.bfloat16)


smem = pl.BlockSpec(memory_space=pltpu.SMEM)
vmem = pl.BlockSpec(memory_space=pltpu.VMEM)
hbm = pl.BlockSpec(memory_space=pl.ANY)


def limit(mebibytes):
    return pltpu.CompilerParams(vmem_limit_bytes=mebibytes * 1024 * 1024)


def normalize(values):
    floats = values.astype(jnp.float32)
    return (floats * lax.rsqrt(jnp.sum(floats * floats, axis=-1, keepdims=True) + epsilon)).astype(jnp.bfloat16)


def body(embeddings, prior_scores, frame_valid, neighbour_ids, neighbour_count, block_home):
    per_list = neighbour_ids.shape[1]
    y, z, c, x = (lax.axis_index(a) for a in ("y", "z", "c", "x"))
    first = x * PART
    units = normalize(lax.dynamic_slice_in_dim(embeddings, first, PART, 0))
    prior = lax.dynamic_slice_in_dim(prior_scores, first, PART, 0)
    valid = lax.dynamic_slice_in_dim(frame_valid, first, PART, 0)
    marks = jnp.broadcast_to(valid[:, :, None], prior.shape).astype(jnp.bfloat16)
    marked = jnp.where(marks > 0, prior, jnp.bfloat16(2 * UNREAL))
    piece = jnp.concatenate([units, marked], axis=-1).reshape(PIECE, WIDE)

    keys = lax.all_gather(piece, ("z", "c"), axis=0, tiled=True)

    embeddings, ids, block_home, piece = lax.optimization_barrier((embeddings, neighbour_ids, block_home, piece))
    target = jnp.take(block_home, ids.reshape(-1), axis=0)
    column = x * per_list + jnp.arange(per_list, dtype=jnp.int32)
    in_list = (column[None, :] < neighbour_count[:, None]).reshape(-1)
    target = jnp.where(in_list, target, -1)
    target = jnp.broadcast_to(target[None, :], (NY * NX, ROWS * per_list))
    target = lax.all_to_all(target, ("y", "x"), split_axis=0, concat_axis=0, tiled=True)

    units, target = lax.optimization_barrier((units, target))
    turn = units[:TURN].reshape(TURN * FRAMES, FEAT)
    turned = [
        shift(turn, "y", -1), shift(turn[:FRAMES], "y", 2), shift(turn[FRAMES:], "y", -2), shift(turn, "y", 1)
    ]
    all_units = normalize(embeddings)
    straight = all_units.reshape(NX, PART, FRAMES, FEAT)[:, TURN:].reshape(STRAIGHT * FRAMES, FEAT)
    turned, straight = lax.optimization_barrier((turned, straight))
    behind, ahead = shift(straight, "y", 1), shift(straight, "y", -1)
    turned = jnp.concatenate(turned, axis=0)
    half = turned.shape[0] // 2
    turned = [
        turned,
        shift(turned, "x", -1),
        shift(turned[:half], "x", 2),
        shift(turned[half:], "x", -2),
        shift(turned, "x", 1),
    ]
    half = STRAIGHT * FRAMES // 2
    across = [shift(behind[:half], "y", 1), shift(ahead[half:], "y", -1)]

    target = target.reshape(NY, NX, ROWS, per_list)
    source_y = jnp.arange(NY, dtype=jnp.int32)[:, None, None, None]
    source_row = jnp.arange(ROWS, dtype=jnp.int32)[None, None, :, None]
    distance = (source_y - y) % NY
    source = source_y * ROWS + source_row
    wanted = (target >= 0) & (target // 256 == y) & ((target % 16) // PART == x)
    place = (target // 16) % 16
    inner = target % PART
    side = (place % 2) ^ c
    quarter, within = source_row // PART, source_row % PART
    taken = jnp.where(
        distance == 0,
        source_row,
        jnp.where(
            within < TURN,
            Q_TURN + (((quarter - x) % NX) * (NY - 1) + distance - 1) * TURN + within,
            ROWS + (distance - 1) * STRAIGHT + quarter * (PART - TURN) + within - TURN,
        ),
    )
    codes = source | ((place * PART + inner) << 7) | (taken << 13) | (side << 20) | (((place // 2) * PART + inner) << 21)
    codes = jnp.where(wanted, codes, -1).reshape(-1)
    lst = pl.pallas_call(
        list_kernel,
        out_shape=jax.ShapeDtypeStruct((LIST,), jnp.int32),
        in_specs=[smem],
        out_specs=smem,
        compiler_params=limit(1),
    )(codes)
    own_weights, own_base = pl.pallas_call(
        own_kernel,
        out_shape=(
            jax.ShapeDtypeStruct((PART, FRAMES, FRAMES), jnp.bfloat16),
            jax.ShapeDtypeStruct((PART, FRAMES, 2 * CH), jnp.float32),
        ),
        in_specs=[vmem],
        out_specs=(vmem, vmem),
        compiler_params=limit(4),
    )(piece)

    send, weights = pl.pallas_call(
        first_kernel,
        out_shape=(
            jax.ShapeDtypeStruct((NY * NX, SEND, CH), jnp.bfloat16),
            jax.ShapeDtypeStruct((SLOTS // 2, FRAMES, 2 * FRAMES), jnp.bfloat16),
        ),
        in_specs=[smem] + [hbm] * 11,
        out_specs=(vmem, vmem),
        scratch_shapes=[
            pltpu.VMEM((QBLOCKS * FRAMES, FEAT), jnp.bfloat16),
            pltpu.VMEM((NZ * NC * PIECE, WIDE), jnp.bfloat16),
            pltpu.VMEM((QBLOCKS + 1, FRAMES, 2 * CH), jnp.float32),
            pltpu.SemaphoreType.DMA((11,)),
        ],
        compiler_params=limit(32),
    )(lst, keys, all_units.reshape(ROWS * FRAMES, FEAT), ahead, *across, behind, *turned)
    got = lax.all_to_all(send, ("y", "x"), split_axis=0, concat_axis=0, tiled=True)

    masked, denominator, own_second = pl.pallas_call(
        mix_kernel,
        out_shape=(
            jax.ShapeDtypeStruct((NZ, PART, FRAMES, CH), jnp.bfloat16),
            jax.ShapeDtypeStruct((PART, FRAMES, CH), jnp.float32),
            jax.ShapeDtypeStruct((PART, FRAMES, CH), jnp.float32),
        ),
        in_specs=[vmem] * 5,
        out_specs=(vmem,) * 3,
        compiler_params=limit(8),
    )(got, own_base, own_weights, prior, marks)
    near_scores = lax.all_to_all(masked, "z", split_axis=0, concat_axis=0, tiled=True)
    near_scores = near_scores.reshape(NZ * PART, FRAMES, CH)
    far_scores = shift(near_scores, "c", 1)

    send = pl.pallas_call(
        second_kernel,
        out_shape=jax.ShapeDtypeStruct((QBLOCKS, FRAMES, CH), jnp.bfloat16),
        in_specs=[smem, vmem, vmem, vmem],
        out_specs=vmem,
        scratch_shapes=[pltpu.VMEM((QBLOCKS + 1, FRAMES, CH), jnp.float32)],
        compiler_params=limit(12),
    )(lst, weights, near_scores, far_scores)
    got = lax.all_to_all(send, ("y", "x"), split_axis=0, concat_axis=0, tiled=True)
    return pl.pallas_call(
        last_kernel,
        out_shape=jax.ShapeDtypeStruct((PART, FRAMES, CH), jnp.bfloat16),
        in_specs=[vmem] * 4,
        out_specs=vmem,
        compiler_params=limit(8),
    )(got.reshape(NY * NX, PART, FRAMES, CH), own_second, denominator, prior)


def solution(mesh):
    fine = Mesh(mesh.devices.reshape(NY, NZ, NC, NX), ("y", "z", "c", "x"))
    bucket = ("y", "z", "c")
    in_specs = (P(bucket, None, None), P(bucket, None, None), P(bucket, None), P(bucket, "x"), P(bucket), P())
    out_specs = P(("y", "z", "c", "x"), None, None)
    return jax.shard_map(body, mesh=fine, in_specs=in_specs, out_specs=out_specs, check_vma=False)
```

```python
import math

import jax
import jax.numpy as jnp
from jax import lax
from jax.experimental import pallas as pl
from jax.experimental.pallas import tpu as pltpu
from jax.sharding import Mesh
from jax.sharding import PartitionSpec as P

epsilon = 1e-06
keep_share = 0.9

NY, NZ, NC, NX = 4, 8, 2, 4
ROWS = 16
FRAMES = 64
FEAT = 1152
CH = 128
PART = ROWS // NX
TURN = 2
STRAIGHT = NX * (PART - TURN)
QBLOCKS = NY * ROWS
Q_TURN = ROWS + (NY - 1) * STRAIGHT
UNROLL = 8
SLOTS = 520
WIDE = FEAT + CH
PIECE = PART * FRAMES
SEND = PIECE + 16
LIST = 640
STEPS_AT = 600
SPARE = QBLOCKS
UNREAL = 1024.0
sharpness = 2.0 * math.sqrt(FEAT)


def shift(value, axis, step):
    size = lax.axis_size(axis)
    return lax.ppermute(value, axis, [(i, (i + step) % size) for i in range(size)])


def list_kernel(codes, out):
    def eight(i, count):
        for u in range(8):
            code = codes[i * 8 + u]
            out[count] = code
            count = count + jnp.where(code >= 0, 1, 0)
        return count

    count = lax.fori_loop(0, QBLOCKS * 32 // 8, eight, 0)
    for u in range(UNROLL):
        out[count + u] = SPARE
    out[STEPS_AT] = (count + UNROLL - 1) // UNROLL


def own_kernel(piece, own_weights, own_base):
    row = lax.broadcasted_iota(jnp.int32, (FRAMES, FRAMES), 0)
    col = lax.broadcasted_iota(jnp.int32, (FRAMES, FRAMES), 1)
    for b in range(PART):
        block = piece[b * FRAMES:(b + 1) * FRAMES, :]
        units = block[:, :FEAT]
        affinity = lax.dot_general(
            units, units, (((1,), (1,)), ((), ())), preferred_element_type=jnp.float32
        )
        weights = jnp.where(row == col, 0.0, jnp.exp(sharpness * affinity)).astype(jnp.bfloat16)
        own_weights[b] = weights
        own_base[b] = jnp.dot(weights, values_of(block[:, FEAT:]), preferred_element_type=jnp.float32)


def values_of(scores):
    floats = scores.astype(jnp.float32)
    real = floats < UNREAL
    return jnp.concatenate(
        [jnp.where(real, floats, 0.0), jnp.where(real, 1.0, 0.0)], axis=1
    ).astype(jnp.bfloat16)


def pairs_copy(source, target, sem, i):
    group = pl.ds(i * (UNROLL // 2), UNROLL // 2)
    return pltpu.make_async_copy(source.at[group], target.at[group], sem)


def join_kernel(one, two_a, two_b, three, out, sems):
    rows = TURN * FRAMES
    copies = [
        pltpu.make_async_copy(one, out.at[pl.ds(0, rows)], sems.at[0]),
        pltpu.make_async_copy(two_a, out.at[pl.ds(rows, FRAMES)], sems.at[1]),
        pltpu.make_async_copy(two_b, out.at[pl.ds(rows + FRAMES, FRAMES)], sems.at[2]),
        pltpu.make_async_copy(three, out.at[pl.ds(rows + 2 * FRAMES, rows)], sems.at[3]),
    ]
    for copy in copies:
        copy.start()
    for copy in copies:
        copy.wait()


def first_kernel(lst, keys, *refs):
    queries = refs[:10]
    send_out, w_out, q, k, acc, send, w, sems, w_sem, send_sem = refs[10:]
    copies = [pltpu.make_async_copy(keys, k, sems.at[0])]
    at = 0
    for part in queries:
        rows = part.shape[0]
        copies.append(pltpu.make_async_copy(part, q.at[pl.ds(at, rows)], sems.at[len(copies)]))
        at += rows
    for copy in copies:
        copy.start()
    acc[...] = jnp.zeros_like(acc)
    for copy in copies:
        copy.wait()
    steps = lst[STEPS_AT]

    def step(i, carry):
        codes = [lst[i * UNROLL + u] for u in range(UNROLL)]
        key_rows = [pl.multiple_of(((code >> 7) & 63) * FRAMES, FRAMES) for code in codes]
        query_rows = [pl.multiple_of(((code >> 13) & 63) * FRAMES, FRAMES) for code in codes]
        weights = []
        for query_row, key_row in zip(query_rows, key_rows):
            affinity = lax.dot_general(
                q[pl.ds(query_row, FRAMES), :],
                k[pl.ds(key_row, FRAMES), pl.ds(0, FEAT)],
                (((1,), (1,)), ((), ())),
                preferred_element_type=jnp.float32,
            )
            weights.append(jnp.exp(sharpness * affinity).astype(jnp.bfloat16))
        for u in range(UNROLL // 2):
            w[i * (UNROLL // 2) + u] = jnp.concatenate(weights[2 * u:2 * u + 2], axis=1)
        sums = []
        for u, key_row in enumerate(key_rows):
            values = values_of(k[pl.ds(key_row, FRAMES), pl.ds(FEAT, CH)])
            sums.append(jnp.dot(weights[u], values, preferred_element_type=jnp.float32))
        for u, code in enumerate(codes):
            acc[code & 127] += sums[u]
        pairs_copy(w, w_out, w_sem, i).start()
        return carry

    lax.fori_loop(0, steps, step, 0)
    row = lax.broadcasted_iota(jnp.int32, (FRAMES, CH), 0)
    lane = lax.broadcasted_iota(jnp.int32, (FRAMES, CH), 1)
    pick = row == lane % FRAMES
    low = lax.broadcasted_iota(jnp.int32, (1, CH), 1) < FRAMES

    def finish(d, carry):
        rows = []
        for b in range(PART):
            block = acc[d * PART + b]
            send[d, b * FRAMES:(b + 1) * FRAMES, :] = block[:, :CH].astype(jnp.bfloat16)
            mass = jnp.sum(jnp.where(pick, block[:, CH:], 0.0), axis=0, keepdims=True)
            coarse = mass.astype(jnp.bfloat16).astype(jnp.float32)
            rows.append(jnp.where(low, coarse, mass - coarse))
        rows.append(jnp.zeros((16 - PART, CH), jnp.float32))
        send[d, PIECE:SEND, :] = jnp.concatenate(rows, axis=0).astype(jnp.bfloat16)
        pltpu.make_async_copy(send.at[d], send_out.at[d], send_sem).start()
        return carry

    lax.fori_loop(0, NY * NX, finish, 0)

    def drain_send(d, carry):
        pltpu.make_async_copy(send.at[d], send_out.at[d], send_sem).wait()
        return carry

    lax.fori_loop(0, NY * NX, drain_send, 0)

    def drain(i, carry):
        pairs_copy(w, w_out, w_sem, i).wait()
        return carry

    lax.fori_loop(0, steps, drain, 0)


def second_kernel(lst, w_in, near, far, send, acc, w, w_sem):
    steps = lst[STEPS_AT]

    def fetch(i, carry):
        pairs_copy(w_in, w, w_sem, i).start()
        return carry

    lax.fori_loop(0, steps, fetch, 0)
    acc[...] = jnp.zeros_like(acc)

    def drain(i, carry):
        pairs_copy(w_in, w, w_sem, i).wait()
        return carry

    lax.fori_loop(0, steps, drain, 0)

    def step(i, carry):
        codes = [lst[i * UNROLL + u] for u in range(UNROLL)]
        sums = []
        for u, code in enumerate(codes):
            block = (code >> 21) & 31
            scores = jnp.where(((code >> 20) & 1) == 0, near[block], far[block])
            weights = w[i * (UNROLL // 2) + u // 2][:, (u % 2) * FRAMES:(u % 2 + 1) * FRAMES]
            sums.append(jnp.dot(weights, scores, preferred_element_type=jnp.float32))
        for u, code in enumerate(codes):
            acc[code & 127] += sums[u]
        return carry

    lax.fori_loop(0, steps, step, 0)
    for b in range(QBLOCKS):
        send[b] = acc[b].astype(jnp.bfloat16)


def mix_kernel(got, base, weights, prior, marks, masked, denominator, own_second):
    row = lax.broadcasted_iota(jnp.int32, (FRAMES, CH), 0)
    lane = lax.broadcasted_iota(jnp.int32, (FRAMES, CH), 1)
    pick = (row == lane % FRAMES).astype(jnp.float32)
    for b in range(PART):
        total = base[b, :, :CH]
        for d in range(NY * NX):
            total = total + got[d, b * FRAMES:(b + 1) * FRAMES, :].astype(jnp.float32)
        mass = jnp.sum(got[:, PIECE:SEND, :].astype(jnp.float32), axis=0)[b:b + 1, :]
        column = jnp.sum(pick * mass, axis=1, keepdims=True)
        full = 1.0 + column + base[b, :, CH:]
        denominator[b] = full
        mixed = keep_share * total / full + (1.0 - keep_share) * prior[b].astype(jnp.float32)
        keep = (mixed.astype(jnp.bfloat16).astype(jnp.float32) * marks[b].astype(jnp.float32)).astype(jnp.bfloat16)
        for d in range(NZ):
            masked[d, b] = keep
        own_second[b] = jnp.dot(weights[b], keep, preferred_element_type=jnp.float32)


def last_kernel(got, own_second, denominator, prior, out):
    for b in range(PART):
        total = own_second[b]
        for d in range(NY * NX):
            total = total + got[d, b].astype(jnp.float32)
        mixed = keep_share * total / denominator[b]
        out[b] = (mixed + (1.0 - keep_share) * prior[b].astype(jnp.float32)).astype(jnp.bfloat16)


smem = pl.BlockSpec(memory_space=pltpu.SMEM)
vmem = pl.BlockSpec(memory_space=pltpu.VMEM)
hbm = pl.BlockSpec(memory_space=pl.ANY)
far_memory = pl.BlockSpec(memory_space=pltpu.HBM)


def limit(mebibytes):
    return pltpu.CompilerParams(vmem_limit_bytes=mebibytes * 1024 * 1024)


def normalize(values):
    floats = values.astype(jnp.float32)
    return (floats * lax.rsqrt(jnp.sum(floats * floats, axis=-1, keepdims=True) + epsilon)).astype(jnp.bfloat16)


def body(embeddings, prior_scores, frame_valid, neighbour_ids, neighbour_count, block_home):
    per_list = neighbour_ids.shape[1]
    y, z, c, x = (lax.axis_index(a) for a in ("y", "z", "c", "x"))
    first = x * PART
    units = normalize(lax.dynamic_slice_in_dim(embeddings, first, PART, 0))
    prior = lax.dynamic_slice_in_dim(prior_scores, first, PART, 0)
    valid = lax.dynamic_slice_in_dim(frame_valid, first, PART, 0)
    marks = jnp.broadcast_to(valid[:, :, None], prior.shape).astype(jnp.bfloat16)
    marked = jnp.where(marks > 0, prior, jnp.bfloat16(2 * UNREAL))
    piece = jnp.concatenate([units, marked], axis=-1).reshape(PIECE, WIDE)

    keys = lax.all_gather(piece, ("z", "c"), axis=0, tiled=True)

    embeddings, ids, block_home, piece = lax.optimization_barrier((embeddings, neighbour_ids, block_home, piece))
    target = jnp.take(block_home, ids.reshape(-1), axis=0)
    column = x * per_list + jnp.arange(per_list, dtype=jnp.int32)
    in_list = (column[None, :] < neighbour_count[:, None]).reshape(-1)
    target = jnp.where(in_list, target, -1)
    target = jnp.broadcast_to(target[None, :], (NY * NX, ROWS * per_list))
    target = lax.all_to_all(target, ("y", "x"), split_axis=0, concat_axis=0, tiled=True)

    turn = units[:TURN].reshape(TURN * FRAMES, FEAT)
    turned = [
        shift(turn, "y", -1), shift(turn[:FRAMES], "y", 2), shift(turn[FRAMES:], "y", -2), shift(turn, "y", 1)
    ]
    all_units = normalize(embeddings)
    straight = all_units.reshape(NX, PART, FRAMES, FEAT)[:, TURN:].reshape(STRAIGHT * FRAMES, FEAT)
    turned, straight, target = lax.optimization_barrier((turned, straight, target))
    behind, ahead = shift(straight, "y", 1), shift(straight, "y", -1)
    rows = (NY - 1) * TURN * FRAMES
    turned = pl.pallas_call(
        join_kernel,
        out_shape=jax.ShapeDtypeStruct((rows, FEAT), jnp.bfloat16),
        in_specs=[hbm] * 4,
        out_specs=hbm,
        scratch_shapes=[pltpu.SemaphoreType.DMA((4,))],
        compiler_params=limit(1),
    )(*turned)
    following, leading = shift(turned, "x", -1), shift(turned, "x", 1)
    over = [shift(leading[:rows // 2], "x", 1), shift(following[rows // 2:], "x", -1)]
    turned = [turned, following, *over, leading]

    target = target.reshape(NY, NX, ROWS, per_list)
    source_y = jnp.arange(NY, dtype=jnp.int32)[:, None, None, None]
    source_row = jnp.arange(ROWS, dtype=jnp.int32)[None, None, :, None]
    distance = (source_y - y) % NY
    source = source_y * ROWS + source_row
    wanted = (target >= 0) & (target // 256 == y) & ((target % 16) // PART == x)
    place = (target // 16) % 16
    inner = target % PART
    side = (place % 2) ^ c
    quarter, within = source_row // PART, source_row % PART
    taken = jnp.where(
        distance == 0,
        source_row,
        jnp.where(
            within < TURN,
            Q_TURN + (((quarter - x) % NX) * (NY - 1) + distance - 1) * TURN + within,
            ROWS + (distance - 1) * STRAIGHT + quarter * (PART - TURN) + within - TURN,
        ),
    )
    codes = source | ((place * PART + inner) << 7) | (taken << 13) | (side << 20) | (((place // 2) * PART + inner) << 21)
    codes = jnp.where(wanted, codes, -1).reshape(-1)
    lst = pl.pallas_call(
        list_kernel,
        out_shape=jax.ShapeDtypeStruct((LIST,), jnp.int32),
        in_specs=[smem],
        out_specs=smem,
        compiler_params=limit(1),
    )(codes)
    half = STRAIGHT * FRAMES // 2
    behind, ahead, lst = lax.optimization_barrier((behind, ahead, lst))
    across = [shift(behind[:half], "y", 1), shift(ahead[half:], "y", -1)]
    own_weights, own_base = pl.pallas_call(
        own_kernel,
        out_shape=(
            jax.ShapeDtypeStruct((PART, FRAMES, FRAMES), jnp.bfloat16),
            jax.ShapeDtypeStruct((PART, FRAMES, 2 * CH), jnp.float32),
        ),
        in_specs=[vmem],
        out_specs=(vmem, vmem),
        compiler_params=limit(4),
    )(piece)

    send, weights = pl.pallas_call(
        first_kernel,
        out_shape=(
            jax.ShapeDtypeStruct((NY * NX, SEND, CH), jnp.bfloat16),
            jax.ShapeDtypeStruct((SLOTS // 2, FRAMES, 2 * FRAMES), jnp.bfloat16),
        ),
        in_specs=[smem] + [hbm] * 11,
        out_specs=(far_memory, far_memory),
        scratch_shapes=[
            pltpu.VMEM((QBLOCKS * FRAMES, FEAT), jnp.bfloat16),
            pltpu.VMEM((NZ * NC * PIECE, WIDE), jnp.bfloat16),
            pltpu.VMEM((QBLOCKS + 1, FRAMES, 2 * CH), jnp.float32),
            pltpu.VMEM((NY * NX, SEND, CH), jnp.bfloat16),
            pltpu.VMEM((SLOTS // 2, FRAMES, 2 * FRAMES), jnp.bfloat16),
            pltpu.SemaphoreType.DMA((11,)),
            pltpu.SemaphoreType.DMA,
            pltpu.SemaphoreType.DMA,
        ],
        compiler_params=limit(32),
    )(lst, keys, all_units.reshape(ROWS * FRAMES, FEAT), ahead, *across, behind, *turned)
    got = lax.all_to_all(send, ("y", "x"), split_axis=0, concat_axis=0, tiled=True)

    masked, denominator, own_second = pl.pallas_call(
        mix_kernel,
        out_shape=(
            jax.ShapeDtypeStruct((NZ, PART, FRAMES, CH), jnp.bfloat16),
            jax.ShapeDtypeStruct((PART, FRAMES, CH), jnp.float32),
            jax.ShapeDtypeStruct((PART, FRAMES, CH), jnp.float32),
        ),
        in_specs=[vmem] * 5,
        out_specs=(vmem,) * 3,
        compiler_params=limit(8),
    )(got, own_base, own_weights, prior, marks)
    near_scores = lax.all_to_all(masked, "z", split_axis=0, concat_axis=0, tiled=True)
    near_scores = near_scores.reshape(NZ * PART, FRAMES, CH)
    far_scores = shift(near_scores, "c", 1)

    send = pl.pallas_call(
        second_kernel,
        out_shape=jax.ShapeDtypeStruct((QBLOCKS, FRAMES, CH), jnp.bfloat16),
        in_specs=[smem, far_memory, vmem, vmem],
        out_specs=vmem,
        scratch_shapes=[
            pltpu.VMEM((QBLOCKS + 1, FRAMES, CH), jnp.float32),
            pltpu.VMEM((SLOTS // 2, FRAMES, 2 * FRAMES), jnp.bfloat16),
            pltpu.SemaphoreType.DMA,
        ],
        compiler_params=limit(12),
    )(lst, weights, near_scores, far_scores)
    got = lax.all_to_all(send, ("y", "x"), split_axis=0, concat_axis=0, tiled=True)
    return pl.pallas_call(
        last_kernel,
        out_shape=jax.ShapeDtypeStruct((PART, FRAMES, CH), jnp.bfloat16),
        in_specs=[vmem] * 4,
        out_specs=vmem,
        compiler_params=limit(8),
    )(got.reshape(NY * NX, PART, FRAMES, CH), own_second, denominator, prior)


def solution(mesh):
    fine = Mesh(mesh.devices.reshape(NY, NZ, NC, NX), ("y", "z", "c", "x"))
    bucket = ("y", "z", "c")
    in_specs = (P(bucket, None, None), P(bucket, None, None), P(bucket, None), P(bucket, "x"), P(bucket), P())
    out_specs = P(("y", "z", "c", "x"), None, None)
    return jax.shard_map(body, mesh=fine, in_specs=in_specs, out_specs=out_specs, check_vma=False)
```

```python
import math

import jax
import jax.numpy as jnp
from jax import lax
from jax.experimental import pallas as pl
from jax.experimental.pallas import tpu as pltpu
from jax.sharding import Mesh
from jax.sharding import PartitionSpec as P

epsilon = 1e-06
keep_share = 0.9

NY, NZ, NC, NX = 4, 8, 2, 4
ROWS = 16
FRAMES = 64
FEAT = 1152
CH = 128
PART = ROWS // NX
TURN = 2
STRAIGHT = NX * (PART - TURN)
QBLOCKS = NY * ROWS
Q_TURN = ROWS + (NY - 1) * STRAIGHT
UNROLL = 8
SLOTS = 520
WIDE = FEAT + CH
PIECE = PART * FRAMES
SEND = PIECE + 16
LIST = 640
STEPS_AT = 600
SPARE = QBLOCKS
UNREAL = 1024.0
sharpness = 2.0 * math.sqrt(FEAT)


def shift(value, axis, step):
    size = lax.axis_size(axis)
    return lax.ppermute(value, axis, [(i, (i + step) % size) for i in range(size)])


def list_kernel(codes, out):
    def eight(i, count):
        for u in range(8):
            code = codes[i * 8 + u]
            out[count] = code
            count = count + jnp.where(code >= 0, 1, 0)
        return count

    count = lax.fori_loop(0, QBLOCKS * 32 // 8, eight, 0)
    for u in range(UNROLL):
        out[count + u] = SPARE
    out[STEPS_AT] = (count + UNROLL - 1) // UNROLL


def own_kernel(piece, own_weights, own_base):
    row = lax.broadcasted_iota(jnp.int32, (FRAMES, FRAMES), 0)
    col = lax.broadcasted_iota(jnp.int32, (FRAMES, FRAMES), 1)
    for b in range(PART):
        block = piece[b * FRAMES:(b + 1) * FRAMES, :]
        units = block[:, :FEAT]
        affinity = lax.dot_general(
            units, units, (((1,), (1,)), ((), ())), preferred_element_type=jnp.float32
        )
        weights = jnp.where(row == col, 0.0, jnp.exp(sharpness * affinity)).astype(jnp.bfloat16)
        own_weights[b] = weights
        own_base[b] = jnp.dot(weights, values_of(block[:, FEAT:]), preferred_element_type=jnp.float32)


def values_of(scores):
    floats = scores.astype(jnp.float32)
    real = floats < UNREAL
    return jnp.concatenate(
        [jnp.where(real, floats, 0.0), jnp.where(real, 1.0, 0.0)], axis=1
    ).astype(jnp.bfloat16)


def pairs_copy(source, target, sem, i):
    group = pl.ds(i * (UNROLL // 2), UNROLL // 2)
    return pltpu.make_async_copy(source.at[group], target.at[group], sem)


def join_kernel(*refs):
    parts, out, sems = refs[:3], refs[3], refs[4]
    rows = TURN * FRAMES
    copies = [
        pltpu.make_async_copy(part, out.at[pl.ds(d * rows, rows)], sems.at[d]) for d, part in enumerate(parts)
    ]
    for copy in copies:
        copy.start()
    for copy in copies:
        copy.wait()


def first_kernel(lst, keys, *refs):
    queries = refs[:10]
    send_out, w_out, q, k, acc, send, w, sems, w_sem, send_sem = refs[10:]
    copies = [pltpu.make_async_copy(keys, k, sems.at[0])]
    at = 0
    for part in queries:
        rows = part.shape[0]
        copies.append(pltpu.make_async_copy(part, q.at[pl.ds(at, rows)], sems.at[len(copies)]))
        at += rows
    for copy in copies:
        copy.start()
    acc[...] = jnp.zeros_like(acc)
    for copy in copies:
        copy.wait()
    steps = lst[STEPS_AT]

    def step(i, carry):
        codes = [lst[i * UNROLL + u] for u in range(UNROLL)]
        key_rows = [pl.multiple_of(((code >> 7) & 63) * FRAMES, FRAMES) for code in codes]
        query_rows = [pl.multiple_of(((code >> 13) & 63) * FRAMES, FRAMES) for code in codes]
        weights = []
        for query_row, key_row in zip(query_rows, key_rows):
            affinity = lax.dot_general(
                q[pl.ds(query_row, FRAMES), :],
                k[pl.ds(key_row, FRAMES), pl.ds(0, FEAT)],
                (((1,), (1,)), ((), ())),
                preferred_element_type=jnp.float32,
            )
            weights.append(jnp.exp(sharpness * affinity).astype(jnp.bfloat16))
        for u in range(UNROLL // 2):
            w[i * (UNROLL // 2) + u] = jnp.concatenate(weights[2 * u:2 * u + 2], axis=1)
        sums = []
        for u, key_row in enumerate(key_rows):
            values = values_of(k[pl.ds(key_row, FRAMES), pl.ds(FEAT, CH)])
            sums.append(jnp.dot(weights[u], values, preferred_element_type=jnp.float32))
        for u, code in enumerate(codes):
            acc[code & 127] += sums[u]
        pairs_copy(w, w_out, w_sem, i).start()
        return carry

    lax.fori_loop(0, steps, step, 0)
    row = lax.broadcasted_iota(jnp.int32, (FRAMES, CH), 0)
    lane = lax.broadcasted_iota(jnp.int32, (FRAMES, CH), 1)
    pick = row == lane % FRAMES
    low = lax.broadcasted_iota(jnp.int32, (1, CH), 1) < FRAMES

    def finish(d, carry):
        rows = []
        for b in range(PART):
            block = acc[d * PART + b]
            send[d, b * FRAMES:(b + 1) * FRAMES, :] = block[:, :CH].astype(jnp.bfloat16)
            mass = jnp.sum(jnp.where(pick, block[:, CH:], 0.0), axis=0, keepdims=True)
            coarse = mass.astype(jnp.bfloat16).astype(jnp.float32)
            rows.append(jnp.where(low, coarse, mass - coarse))
        rows.append(jnp.zeros((16 - PART, CH), jnp.float32))
        send[d, PIECE:SEND, :] = jnp.concatenate(rows, axis=0).astype(jnp.bfloat16)
        pltpu.make_async_copy(send.at[d], send_out.at[d], send_sem).start()
        return carry

    lax.fori_loop(0, NY * NX, finish, 0)

    def drain_send(d, carry):
        pltpu.make_async_copy(send.at[d], send_out.at[d], send_sem).wait()
        return carry

    lax.fori_loop(0, NY * NX, drain_send, 0)

    def drain(i, carry):
        pairs_copy(w, w_out, w_sem, i).wait()
        return carry

    lax.fori_loop(0, steps, drain, 0)


def second_kernel(lst, w_in, near, far, send, acc, w, w_sem):
    steps = lst[STEPS_AT]

    def fetch(i, carry):
        pairs_copy(w_in, w, w_sem, i).start()
        return carry

    lax.fori_loop(0, steps, fetch, 0)
    acc[...] = jnp.zeros_like(acc)

    def drain(i, carry):
        pairs_copy(w_in, w, w_sem, i).wait()
        return carry

    lax.fori_loop(0, steps, drain, 0)

    def step(i, carry):
        codes = [lst[i * UNROLL + u] for u in range(UNROLL)]
        sums = []
        for u, code in enumerate(codes):
            block = (code >> 21) & 31
            scores = jnp.where(((code >> 20) & 1) == 0, near[block], far[block])
            weights = w[i * (UNROLL // 2) + u // 2][:, (u % 2) * FRAMES:(u % 2 + 1) * FRAMES]
            sums.append(jnp.dot(weights, scores, preferred_element_type=jnp.float32))
        for u, code in enumerate(codes):
            acc[code & 127] += sums[u]
        return carry

    lax.fori_loop(0, steps, step, 0)
    for b in range(QBLOCKS):
        send[b] = acc[b].astype(jnp.bfloat16)


def mix_kernel(got, base, weights, prior, marks, masked, denominator, own_second):
    row = lax.broadcasted_iota(jnp.int32, (FRAMES, CH), 0)
    lane = lax.broadcasted_iota(jnp.int32, (FRAMES, CH), 1)
    pick = (row == lane % FRAMES).astype(jnp.float32)
    for b in range(PART):
        total = base[b, :, :CH]
        for d in range(NY * NX):
            total = total + got[d, b * FRAMES:(b + 1) * FRAMES, :].astype(jnp.float32)
        mass = jnp.sum(got[:, PIECE:SEND, :].astype(jnp.float32), axis=0)[b:b + 1, :]
        column = jnp.sum(pick * mass, axis=1, keepdims=True)
        full = 1.0 + column + base[b, :, CH:]
        denominator[b] = full
        mixed = keep_share * total / full + (1.0 - keep_share) * prior[b].astype(jnp.float32)
        keep = (mixed.astype(jnp.bfloat16).astype(jnp.float32) * marks[b].astype(jnp.float32)).astype(jnp.bfloat16)
        for d in range(NZ):
            masked[d, b] = keep
        own_second[b] = jnp.dot(weights[b], keep, preferred_element_type=jnp.float32)


def last_kernel(got, own_second, denominator, prior, out):
    for b in range(PART):
        total = own_second[b]
        for d in range(NY * NX):
            total = total + got[d, b].astype(jnp.float32)
        mixed = keep_share * total / denominator[b]
        out[b] = (mixed + (1.0 - keep_share) * prior[b].astype(jnp.float32)).astype(jnp.bfloat16)


smem = pl.BlockSpec(memory_space=pltpu.SMEM)
vmem = pl.BlockSpec(memory_space=pltpu.VMEM)
hbm = pl.BlockSpec(memory_space=pl.ANY)
far_memory = pl.BlockSpec(memory_space=pltpu.HBM)


def limit(mebibytes):
    return pltpu.CompilerParams(vmem_limit_bytes=mebibytes * 1024 * 1024)


def normalize(values):
    floats = values.astype(jnp.float32)
    return (floats * lax.rsqrt(jnp.sum(floats * floats, axis=-1, keepdims=True) + epsilon)).astype(jnp.bfloat16)


def body(embeddings, prior_scores, frame_valid, neighbour_ids, neighbour_count, block_home):
    per_list = neighbour_ids.shape[1]
    y, z, c, x = (lax.axis_index(a) for a in ("y", "z", "c", "x"))
    first = x * PART
    units = normalize(lax.dynamic_slice_in_dim(embeddings, first, PART, 0))
    prior = lax.dynamic_slice_in_dim(prior_scores, first, PART, 0)
    valid = lax.dynamic_slice_in_dim(frame_valid, first, PART, 0)
    marks = jnp.broadcast_to(valid[:, :, None], prior.shape).astype(jnp.bfloat16)
    marked = jnp.where(marks > 0, prior, jnp.bfloat16(2 * UNREAL))
    piece = jnp.concatenate([units, marked], axis=-1).reshape(PIECE, WIDE)

    keys = lax.all_gather(piece, ("z", "c"), axis=0, tiled=True)

    embeddings, ids, block_home, piece = lax.optimization_barrier((embeddings, neighbour_ids, block_home, piece))
    target = jnp.take(block_home, ids.reshape(-1), axis=0)
    column = x * per_list + jnp.arange(per_list, dtype=jnp.int32)
    in_list = (column[None, :] < neighbour_count[:, None]).reshape(-1)
    target = jnp.where(in_list, target, -1)
    target = jnp.broadcast_to(target[None, :], (NY * NX, ROWS * per_list))
    target = lax.all_to_all(target, ("y", "x"), split_axis=0, concat_axis=0, tiled=True)

    turn = units[:TURN].reshape(TURN * FRAMES, FEAT)
    one, two, three = shift(turn, "y", -1), shift(turn, "y", 2), shift(turn, "y", 1)
    all_units = normalize(embeddings)
    straight = all_units.reshape(NX, PART, FRAMES, FEAT)[:, TURN:].reshape(STRAIGHT * FRAMES, FEAT)
    one, three, straight, target = lax.optimization_barrier((one, three, straight, target))
    behind, ahead = shift(straight, "y", 1), shift(straight, "y", -1)
    rows = (NY - 1) * TURN * FRAMES
    turned = pl.pallas_call(
        join_kernel,
        out_shape=jax.ShapeDtypeStruct((rows, FEAT), jnp.bfloat16),
        in_specs=[hbm] * 3,
        out_specs=hbm,
        scratch_shapes=[pltpu.SemaphoreType.DMA((3,))],
        compiler_params=limit(1),
    )(one, two, three)
    following, leading = shift(turned, "x", -1), shift(turned, "x", 1)
    over = [shift(leading[:rows // 2], "x", 1), shift(following[rows // 2:], "x", -1)]
    turned = [turned, following, *over, leading]

    target = target.reshape(NY, NX, ROWS, per_list)
    source_y = jnp.arange(NY, dtype=jnp.int32)[:, None, None, None]
    source_row = jnp.arange(ROWS, dtype=jnp.int32)[None, None, :, None]
    distance = (source_y - y) % NY
    source = source_y * ROWS + source_row
    wanted = (target >= 0) & (target // 256 == y) & ((target % 16) // PART == x)
    place = (target // 16) % 16
    inner = target % PART
    side = (place % 2) ^ c
    quarter, within = source_row // PART, source_row % PART
    taken = jnp.where(
        distance == 0,
        source_row,
        jnp.where(
            within < TURN,
            Q_TURN + (((quarter - x) % NX) * (NY - 1) + distance - 1) * TURN + within,
            ROWS + (distance - 1) * STRAIGHT + quarter * (PART - TURN) + within - TURN,
        ),
    )
    codes = source | ((place * PART + inner) << 7) | (taken << 13) | (side << 20) | (((place // 2) * PART + inner) << 21)
    codes = jnp.where(wanted, codes, -1).reshape(-1)
    lst = pl.pallas_call(
        list_kernel,
        out_shape=jax.ShapeDtypeStruct((LIST,), jnp.int32),
        in_specs=[smem],
        out_specs=smem,
        compiler_params=limit(1),
    )(codes)
    half = STRAIGHT * FRAMES // 2
    behind, ahead, lst = lax.optimization_barrier((behind, ahead, lst))
    across = [shift(behind[:half], "y", 1), shift(ahead[half:], "y", -1)]
    own_weights, own_base = pl.pallas_call(
        own_kernel,
        out_shape=(
            jax.ShapeDtypeStruct((PART, FRAMES, FRAMES), jnp.bfloat16),
            jax.ShapeDtypeStruct((PART, FRAMES, 2 * CH), jnp.float32),
        ),
        in_specs=[vmem],
        out_specs=(vmem, vmem),
        compiler_params=limit(4),
    )(piece)

    send, weights = pl.pallas_call(
        first_kernel,
        out_shape=(
            jax.ShapeDtypeStruct((NY * NX, SEND, CH), jnp.bfloat16),
            jax.ShapeDtypeStruct((SLOTS // 2, FRAMES, 2 * FRAMES), jnp.bfloat16),
        ),
        in_specs=[smem] + [hbm] * 11,
        out_specs=(far_memory, far_memory),
        scratch_shapes=[
            pltpu.VMEM((QBLOCKS * FRAMES, FEAT), jnp.bfloat16),
            pltpu.VMEM((NZ * NC * PIECE, WIDE), jnp.bfloat16),
            pltpu.VMEM((QBLOCKS + 1, FRAMES, 2 * CH), jnp.float32),
            pltpu.VMEM((NY * NX, SEND, CH), jnp.bfloat16),
            pltpu.VMEM((SLOTS // 2, FRAMES, 2 * FRAMES), jnp.bfloat16),
            pltpu.SemaphoreType.DMA((11,)),
            pltpu.SemaphoreType.DMA,
            pltpu.SemaphoreType.DMA,
        ],
        compiler_params=limit(58),
    )(lst, keys, all_units.reshape(ROWS * FRAMES, FEAT), ahead, *across, behind, *turned)
    got = lax.all_to_all(send, ("y", "x"), split_axis=0, concat_axis=0, tiled=True)

    masked, denominator, own_second = pl.pallas_call(
        mix_kernel,
        out_shape=(
            jax.ShapeDtypeStruct((NZ, PART, FRAMES, CH), jnp.bfloat16),
            jax.ShapeDtypeStruct((PART, FRAMES, CH), jnp.float32),
            jax.ShapeDtypeStruct((PART, FRAMES, CH), jnp.float32),
        ),
        in_specs=[vmem] * 5,
        out_specs=(vmem,) * 3,
        compiler_params=limit(8),
    )(got, own_base, own_weights, prior, marks)
    near_scores = lax.all_to_all(masked, "z", split_axis=0, concat_axis=0, tiled=True)
    near_scores = near_scores.reshape(NZ * PART, FRAMES, CH)
    far_scores = shift(near_scores, "c", 1)

    send = pl.pallas_call(
        second_kernel,
        out_shape=jax.ShapeDtypeStruct((QBLOCKS, FRAMES, CH), jnp.bfloat16),
        in_specs=[smem, far_memory, vmem, vmem],
        out_specs=vmem,
        scratch_shapes=[
            pltpu.VMEM((QBLOCKS + 1, FRAMES, CH), jnp.float32),
            pltpu.VMEM((SLOTS // 2, FRAMES, 2 * FRAMES), jnp.bfloat16),
            pltpu.SemaphoreType.DMA,
        ],
        compiler_params=limit(57),
    )(lst, weights, near_scores, far_scores)
    got = lax.all_to_all(send, ("y", "x"), split_axis=0, concat_axis=0, tiled=True)
    return pl.pallas_call(
        last_kernel,
        out_shape=jax.ShapeDtypeStruct((PART, FRAMES, CH), jnp.bfloat16),
        in_specs=[vmem] * 4,
        out_specs=vmem,
        compiler_params=limit(8),
    )(got.reshape(NY * NX, PART, FRAMES, CH), own_second, denominator, prior)


def solution(mesh):
    fine = Mesh(mesh.devices.reshape(NY, NZ, NC, NX), ("y", "z", "c", "x"))
    bucket = ("y", "z", "c")
    in_specs = (P(bucket, None, None), P(bucket, None, None), P(bucket, None), P(bucket, "x"), P(bucket), P())
    out_specs = P(("y", "z", "c", "x"), None, None)
    return jax.shard_map(body, mesh=fine, in_specs=in_specs, out_specs=out_specs, check_vma=False)
```

```python
import math

import jax
import jax.numpy as jnp
from jax import lax
from jax.experimental import pallas as pl
from jax.experimental.pallas import tpu as pltpu
from jax.sharding import Mesh
from jax.sharding import PartitionSpec as P

epsilon = 1e-06
keep_share = 0.9

NY, NZ, NC, NX = 4, 8, 2, 4
ROWS = 16
FRAMES = 64
FEAT = 1152
CH = 128
PART = ROWS // NX
TURN = 2
STRAIGHT = NX * (PART - TURN)
QBLOCKS = NY * ROWS
Q_TURN = ROWS + (NY - 1) * STRAIGHT
UNROLL = 8
SLOTS = 528
WIDE = FEAT + CH
PIECE = PART * FRAMES
SEND = PIECE + 16
LIST = 640
EARLY_AT, STEPS_AT = 600, 601
SPARE = QBLOCKS
UNREAL = 1024.0
sharpness = 2.0 * math.sqrt(FEAT)


def shift(value, axis, step):
    size = lax.axis_size(axis)
    return lax.ppermute(value, axis, [(i, (i + step) % size) for i in range(size)])


def normalize(values):
    floats = values.astype(jnp.float32)
    return (floats * lax.rsqrt(jnp.sum(floats * floats, axis=-1, keepdims=True) + epsilon)).astype(jnp.bfloat16)


def prep_kernel(embeddings, prior, valid, piece, turn, e, p, sems):
    first = lax.axis_index("x") * PART
    copies = [
        pltpu.make_async_copy(embeddings.at[pl.ds(first, PART)], e, sems.at[0]),
        pltpu.make_async_copy(prior.at[pl.ds(first, PART)], p, sems.at[1]),
    ]
    for copy in copies:
        copy.start()
    for copy in copies:
        copy.wait()
    row = lax.broadcasted_iota(jnp.int32, (FRAMES, FRAMES), 0)
    col = lax.broadcasted_iota(jnp.int32, (FRAMES, FRAMES), 1)
    pick = row == col
    for b in range(PART):
        units = normalize(e[b])
        real = valid[pl.ds(first + b, 1), :].astype(jnp.float32)
        column = jnp.sum(jnp.where(pick, real, 0.0), axis=1, keepdims=True)
        marked = jnp.where(column > 0.0, p[b].astype(jnp.float32), 2.0 * UNREAL).astype(jnp.bfloat16)
        rows = pl.ds(b * FRAMES, FRAMES)
        piece[rows, :FEAT] = units
        piece[rows, FEAT:] = marked
        if b < TURN:
            turn[rows, :] = units


def list_kernel(codes, out, late):
    def eight(i, counts):
        early_count, late_count = counts
        for u in range(8):
            code = codes[i * 8 + u]
            out[early_count] = code
            late[late_count] = code
            is_late = (code >> 12) & 1
            real = jnp.where(code >= 0, 1, 0)
            early_count = early_count + (real & (1 - is_late))
            late_count = late_count + (real & is_late)
        return early_count, late_count

    early_count, late_count = lax.fori_loop(0, QBLOCKS * 32 // 8, eight, (0, 0))
    for u in range(UNROLL):
        out[early_count + u] = SPARE
        late[late_count + u] = SPARE
    early_steps = (early_count + UNROLL - 1) // UNROLL
    late_steps = (late_count + UNROLL - 1) // UNROLL
    start = early_steps * UNROLL

    def copy(i, carry):
        for u in range(UNROLL):
            out[start + i * UNROLL + u] = late[i * UNROLL + u]
        return carry

    lax.fori_loop(0, late_steps, copy, 0)
    out[EARLY_AT] = early_steps
    out[STEPS_AT] = early_steps + late_steps


def own_kernel(piece, own_weights, own_base):
    row = lax.broadcasted_iota(jnp.int32, (FRAMES, FRAMES), 0)
    col = lax.broadcasted_iota(jnp.int32, (FRAMES, FRAMES), 1)
    for b in range(PART):
        block = piece[b * FRAMES:(b + 1) * FRAMES, :]
        units = block[:, :FEAT]
        affinity = lax.dot_general(
            units, units, (((1,), (1,)), ((), ())), preferred_element_type=jnp.float32
        )
        weights = jnp.where(row == col, 0.0, jnp.exp(sharpness * affinity)).astype(jnp.bfloat16)
        own_weights[b] = weights
        own_base[b] = jnp.dot(weights, values_of(block[:, FEAT:]), preferred_element_type=jnp.float32)


def values_of(scores):
    floats = scores.astype(jnp.float32)
    real = floats < UNREAL
    return jnp.concatenate(
        [jnp.where(real, floats, 0.0), jnp.where(real, 1.0, 0.0)], axis=1
    ).astype(jnp.bfloat16)


def pairs_copy(source, target, sem, i):
    group = pl.ds(i * (UNROLL // 2), UNROLL // 2)
    return pltpu.make_async_copy(source.at[group], target.at[group], sem)


def join_kernel(*refs):
    parts, out, sems = refs[:3], refs[3], refs[4]
    rows = TURN * FRAMES
    copies = [
        pltpu.make_async_copy(part, out.at[pl.ds(d * rows, rows)], sems.at[d]) for d, part in enumerate(parts)
    ]
    for copy in copies:
        copy.start()
    for copy in copies:
        copy.wait()


def first_kernel(lst, keys, *refs):
    queries = refs[:10]
    send_out, w_out, q, k, acc, send, w, sems, w_sem, send_sem = refs[10:]
    half = k.shape[0] // 2
    copies = [pltpu.make_async_copy(keys.at[pl.ds(0, half)], k.at[pl.ds(0, half)], sems.at[0])]
    at = 0
    for part in queries:
        rows = part.shape[0]
        copies.append(pltpu.make_async_copy(part, q.at[pl.ds(at, rows)], sems.at[len(copies)]))
        at += rows
    rest = pltpu.make_async_copy(keys.at[pl.ds(half, half)], k.at[pl.ds(half, half)], sems.at[len(copies)])
    for copy in copies:
        copy.start()
    rest.start()
    acc[...] = jnp.zeros_like(acc)
    for copy in copies:
        copy.wait()
    early_steps, steps = lst[EARLY_AT], lst[STEPS_AT]

    def step(i, carry):
        codes = [lst[i * UNROLL + u] for u in range(UNROLL)]
        key_rows = [pl.multiple_of(((code >> 7) & 63) * FRAMES, FRAMES) for code in codes]
        query_rows = [pl.multiple_of(((code >> 13) & 63) * FRAMES, FRAMES) for code in codes]
        weights = []
        for query_row, key_row in zip(query_rows, key_rows):
            affinity = lax.dot_general(
                q[pl.ds(query_row, FRAMES), :],
                k[pl.ds(key_row, FRAMES), pl.ds(0, FEAT)],
                (((1,), (1,)), ((), ())),
                preferred_element_type=jnp.float32,
            )
            weights.append(jnp.exp(sharpness * affinity).astype(jnp.bfloat16))
        for u in range(UNROLL // 2):
            w[i * (UNROLL // 2) + u] = jnp.concatenate(weights[2 * u:2 * u + 2], axis=1)
        sums = []
        for u, key_row in enumerate(key_rows):
            values = values_of(k[pl.ds(key_row, FRAMES), pl.ds(FEAT, CH)])
            sums.append(jnp.dot(weights[u], values, preferred_element_type=jnp.float32))
        for u, code in enumerate(codes):
            acc[code & 127] += sums[u]
        pairs_copy(w, w_out, w_sem, i).start()
        return carry

    lax.fori_loop(0, early_steps, step, 0)
    rest.wait()
    lax.fori_loop(early_steps, steps, step, 0)
    row = lax.broadcasted_iota(jnp.int32, (FRAMES, CH), 0)
    lane = lax.broadcasted_iota(jnp.int32, (FRAMES, CH), 1)
    pick = row == lane % FRAMES
    low = lax.broadcasted_iota(jnp.int32, (1, CH), 1) < FRAMES

    def finish(d, carry):
        rows = []
        for b in range(PART):
            block = acc[d * PART + b]
            send[d, b * FRAMES:(b + 1) * FRAMES, :] = block[:, :CH].astype(jnp.bfloat16)
            mass = jnp.sum(jnp.where(pick, block[:, CH:], 0.0), axis=0, keepdims=True)
            coarse = mass.astype(jnp.bfloat16).astype(jnp.float32)
            rows.append(jnp.where(low, coarse, mass - coarse))
        rows.append(jnp.zeros((16 - PART, CH), jnp.float32))
        send[d, PIECE:SEND, :] = jnp.concatenate(rows, axis=0).astype(jnp.bfloat16)
        pltpu.make_async_copy(send.at[d], send_out.at[d], send_sem).start()
        return carry

    lax.fori_loop(0, NY * NX, finish, 0)

    def drain_send(d, carry):
        pltpu.make_async_copy(send.at[d], send_out.at[d], send_sem).wait()
        return carry

    lax.fori_loop(0, NY * NX, drain_send, 0)

    def drain(i, carry):
        pairs_copy(w, w_out, w_sem, i).wait()
        return carry

    lax.fori_loop(0, steps, drain, 0)


def second_kernel(lst, w_in, near, far, send_out, acc, w, scores, send, w_sem, sems, send_sem):
    steps = lst[STEPS_AT]
    copies = [
        pltpu.make_async_copy(near, scores.at[0], sems.at[0]),
        pltpu.make_async_copy(far, scores.at[1], sems.at[1]),
    ]
    for copy in copies:
        copy.start()

    def fetch(i, carry):
        pairs_copy(w_in, w, w_sem, i).start()
        return carry

    lax.fori_loop(0, steps, fetch, 0)
    acc[...] = jnp.zeros_like(acc)
    for copy in copies:
        copy.wait()

    def drain(i, carry):
        pairs_copy(w_in, w, w_sem, i).wait()
        return carry

    lax.fori_loop(0, steps, drain, 0)

    def step(i, carry):
        codes = [lst[i * UNROLL + u] for u in range(UNROLL)]
        sums = []
        for u, code in enumerate(codes):
            weights = w[i * (UNROLL // 2) + u // 2][:, (u % 2) * FRAMES:(u % 2 + 1) * FRAMES]
            sums.append(
                jnp.dot(
                    weights, scores[(code >> 20) & 1, (code >> 21) & 31], preferred_element_type=jnp.float32
                )
            )
        for u, code in enumerate(codes):
            acc[code & 127] += sums[u]
        return carry

    lax.fori_loop(0, steps, step, 0)
    groups = [pl.ds(d * PART, PART) for d in range(NY * NX)]
    for group in groups:
        send[group] = acc[group].astype(jnp.bfloat16)
        pltpu.make_async_copy(send.at[group], send_out.at[group], send_sem).start()
    for group in groups:
        pltpu.make_async_copy(send.at[group], send_out.at[group], send_sem).wait()


def mix_kernel(got, base, weights, prior, marks, masked, denominator, own_second):
    row = lax.broadcasted_iota(jnp.int32, (FRAMES, CH), 0)
    lane = lax.broadcasted_iota(jnp.int32, (FRAMES, CH), 1)
    pick = (row == lane % FRAMES).astype(jnp.float32)
    for b in range(PART):
        total = base[b, :, :CH]
        for d in range(NY * NX):
            total = total + got[d, b * FRAMES:(b + 1) * FRAMES, :].astype(jnp.float32)
        mass = jnp.sum(got[:, PIECE:SEND, :].astype(jnp.float32), axis=0)[b:b + 1, :]
        column = jnp.sum(pick * mass, axis=1, keepdims=True)
        full = 1.0 + column + base[b, :, CH:]
        denominator[b] = full
        mixed = keep_share * total / full + (1.0 - keep_share) * prior[b].astype(jnp.float32)
        keep = (mixed.astype(jnp.bfloat16).astype(jnp.float32) * marks[b].astype(jnp.float32)).astype(jnp.bfloat16)
        for d in range(NZ):
            masked[d, b] = keep
        own_second[b] = jnp.dot(weights[b], keep, preferred_element_type=jnp.float32)


def last_kernel(got, own_second, denominator, prior, out):
    for b in range(PART):
        total = own_second[b]
        for d in range(NY * NX):
            total = total + got[d, b].astype(jnp.float32)
        mixed = keep_share * total / denominator[b]
        out[b] = (mixed + (1.0 - keep_share) * prior[b].astype(jnp.float32)).astype(jnp.bfloat16)


smem = pl.BlockSpec(memory_space=pltpu.SMEM)
vmem = pl.BlockSpec(memory_space=pltpu.VMEM)
hbm = pl.BlockSpec(memory_space=pl.ANY)
far_memory = pl.BlockSpec(memory_space=pltpu.HBM)


def limit(mebibytes):
    return pltpu.CompilerParams(vmem_limit_bytes=mebibytes * 1024 * 1024)


def body(embeddings, prior_scores, frame_valid, neighbour_ids, neighbour_count, block_home):
    per_list = neighbour_ids.shape[1]
    y, z, c, x = (lax.axis_index(a) for a in ("y", "z", "c", "x"))
    first = x * PART
    piece, turn = pl.pallas_call(
        prep_kernel,
        out_shape=(
            jax.ShapeDtypeStruct((PIECE, WIDE), jnp.bfloat16),
            jax.ShapeDtypeStruct((TURN * FRAMES, FEAT), jnp.bfloat16),
        ),
        in_specs=[hbm, hbm, vmem],
        out_specs=(vmem, vmem),
        scratch_shapes=[
            pltpu.VMEM((PART, FRAMES, FEAT), jnp.bfloat16),
            pltpu.VMEM((PART, FRAMES, CH), jnp.bfloat16),
            pltpu.SemaphoreType.DMA((2,)),
        ],
        compiler_params=limit(59),
    )(embeddings, prior_scores, frame_valid)

    keys = lax.all_gather(piece, ("z", "c"), axis=0, tiled=True)

    embeddings, prior_scores, ids, block_home, piece = lax.optimization_barrier(
        (embeddings, prior_scores, neighbour_ids, block_home, piece)
    )
    prior = lax.dynamic_slice_in_dim(prior_scores, first, PART, 0)
    valid = lax.dynamic_slice_in_dim(frame_valid, first, PART, 0)
    marks = jnp.broadcast_to(valid[:, :, None], prior.shape).astype(jnp.bfloat16)
    target = jnp.take(block_home, ids.reshape(-1), axis=0)
    column = x * per_list + jnp.arange(per_list, dtype=jnp.int32)
    in_list = (column[None, :] < neighbour_count[:, None]).reshape(-1)
    target = jnp.where(in_list, target, -1)
    target = jnp.broadcast_to(target[None, :], (NY * NX, ROWS * per_list))
    target = lax.all_to_all(target, ("y", "x"), split_axis=0, concat_axis=0, tiled=True)

    one, two, three = shift(turn, "y", -1), shift(turn, "y", 2), shift(turn, "y", 1)
    all_units = normalize(embeddings)
    straight = all_units.reshape(NX, PART, FRAMES, FEAT)[:, TURN:].reshape(STRAIGHT * FRAMES, FEAT)
    one, three, straight, target = lax.optimization_barrier((one, three, straight, target))
    behind, ahead = shift(straight, "y", 1), shift(straight, "y", -1)
    rows = (NY - 1) * TURN * FRAMES
    turned = pl.pallas_call(
        join_kernel,
        out_shape=jax.ShapeDtypeStruct((rows, FEAT), jnp.bfloat16),
        in_specs=[hbm] * 3,
        out_specs=hbm,
        scratch_shapes=[pltpu.SemaphoreType.DMA((3,))],
        compiler_params=limit(1),
    )(one, two, three)
    following, leading = shift(turned, "x", -1), shift(turned, "x", 1)
    over = [shift(leading[:rows // 2], "x", 1), shift(following[rows // 2:], "x", -1)]
    turned = [turned, following, *over, leading]

    target = target.reshape(NY, NX, ROWS, per_list)
    source_y = jnp.arange(NY, dtype=jnp.int32)[:, None, None, None]
    source_row = jnp.arange(ROWS, dtype=jnp.int32)[None, None, :, None]
    distance = (source_y - y) % NY
    source = source_y * ROWS + source_row
    wanted = (target >= 0) & (target // 256 == y) & ((target % 16) // PART == x)
    place = (target // 16) % 16
    inner = target % PART
    side = (place % 2) ^ c
    quarter, within = source_row // PART, source_row % PART
    taken = jnp.where(
        distance == 0,
        source_row,
        jnp.where(
            within < TURN,
            Q_TURN + (((quarter - x) % NX) * (NY - 1) + distance - 1) * TURN + within,
            ROWS + (distance - 1) * STRAIGHT + quarter * (PART - TURN) + within - TURN,
        ),
    )
    codes = source | ((place * PART + inner) << 7) | (taken << 13) | (side << 20) | (((place // 2) * PART + inner) << 21)
    codes = jnp.where(wanted, codes, -1).reshape(-1)
    lst = pl.pallas_call(
        list_kernel,
        out_shape=jax.ShapeDtypeStruct((LIST,), jnp.int32),
        in_specs=[smem],
        out_specs=smem,
        scratch_shapes=[pltpu.SMEM((LIST,), jnp.int32)],
        compiler_params=limit(1),
    )(codes)
    half = STRAIGHT * FRAMES // 2
    behind, ahead, lst = lax.optimization_barrier((behind, ahead, lst))
    across = [shift(behind[:half], "y", 1), shift(ahead[half:], "y", -1)]
    own_weights, own_base = pl.pallas_call(
        own_kernel,
        out_shape=(
            jax.ShapeDtypeStruct((PART, FRAMES, FRAMES), jnp.bfloat16),
            jax.ShapeDtypeStruct((PART, FRAMES, 2 * CH), jnp.float32),
        ),
        in_specs=[vmem],
        out_specs=(vmem, vmem),
        compiler_params=limit(4),
    )(piece)

    send, weights = pl.pallas_call(
        first_kernel,
        out_shape=(
            jax.ShapeDtypeStruct((NY * NX, SEND, CH), jnp.bfloat16),
            jax.ShapeDtypeStruct((SLOTS // 2, FRAMES, 2 * FRAMES), jnp.bfloat16),
        ),
        in_specs=[smem] + [hbm] * 11,
        out_specs=(far_memory, far_memory),
        scratch_shapes=[
            pltpu.VMEM((QBLOCKS * FRAMES, FEAT), jnp.bfloat16),
            pltpu.VMEM((NZ * NC * PIECE, WIDE), jnp.bfloat16),
            pltpu.VMEM((QBLOCKS + 1, FRAMES, 2 * CH), jnp.float32),
            pltpu.VMEM((NY * NX, SEND, CH), jnp.bfloat16),
            pltpu.VMEM((SLOTS // 2, FRAMES, 2 * FRAMES), jnp.bfloat16),
            pltpu.SemaphoreType.DMA((12,)),
            pltpu.SemaphoreType.DMA,
            pltpu.SemaphoreType.DMA,
        ],
        compiler_params=limit(58),
    )(lst, keys, all_units.reshape(ROWS * FRAMES, FEAT), ahead, *across, behind, *turned)
    got = lax.all_to_all(send, ("y", "x"), split_axis=0, concat_axis=0, tiled=True)

    masked, denominator, own_second = pl.pallas_call(
        mix_kernel,
        out_shape=(
            jax.ShapeDtypeStruct((NZ, PART, FRAMES, CH), jnp.bfloat16),
            jax.ShapeDtypeStruct((PART, FRAMES, CH), jnp.float32),
            jax.ShapeDtypeStruct((PART, FRAMES, CH), jnp.float32),
        ),
        in_specs=[vmem] * 5,
        out_specs=(vmem,) * 3,
        compiler_params=limit(8),
    )(got, own_base, own_weights, prior, marks)
    near_scores = lax.all_to_all(masked, "z", split_axis=0, concat_axis=0, tiled=True)
    near_scores = near_scores.reshape(NZ * PART, FRAMES, CH)
    far_scores = shift(near_scores, "c", 1)

    send = pl.pallas_call(
        second_kernel,
        out_shape=jax.ShapeDtypeStruct((QBLOCKS, FRAMES, CH), jnp.bfloat16),
        in_specs=[smem, far_memory, hbm, hbm],
        out_specs=far_memory,
        scratch_shapes=[
            pltpu.VMEM((QBLOCKS + 1, FRAMES, CH), jnp.float32),
            pltpu.VMEM((SLOTS // 2, FRAMES, 2 * FRAMES), jnp.bfloat16),
            pltpu.VMEM((NC, NZ * PART, FRAMES, CH), jnp.bfloat16),
            pltpu.VMEM((QBLOCKS, FRAMES, CH), jnp.bfloat16),
            pltpu.SemaphoreType.DMA,
            pltpu.SemaphoreType.DMA((2,)),
            pltpu.SemaphoreType.DMA,
        ],
        compiler_params=limit(57),
    )(lst, weights, near_scores, far_scores)
    got = lax.all_to_all(send, ("y", "x"), split_axis=0, concat_axis=0, tiled=True)
    return pl.pallas_call(
        last_kernel,
        out_shape=jax.ShapeDtypeStruct((PART, FRAMES, CH), jnp.bfloat16),
        in_specs=[vmem] * 4,
        out_specs=vmem,
        compiler_params=limit(8),
    )(got.reshape(NY * NX, PART, FRAMES, CH), own_second, denominator, prior)


def solution(mesh):
    fine = Mesh(mesh.devices.reshape(NY, NZ, NC, NX), ("y", "z", "c", "x"))
    bucket = ("y", "z", "c")
    in_specs = (P(bucket, None, None), P(bucket, None, None), P(bucket, None), P(bucket, "x"), P(bucket), P())
    out_specs = P(("y", "z", "c", "x"), None, None)
    return jax.shard_map(body, mesh=fine, in_specs=in_specs, out_specs=out_specs, check_vma=False)
```

```python
import math

import jax
import jax.numpy as jnp
from jax import lax
from jax.experimental import pallas as pl
from jax.experimental.pallas import tpu as pltpu
from jax.sharding import Mesh
from jax.sharding import PartitionSpec as P

epsilon = 1e-06
keep_share = 0.9

NY, NZ, NC, NX = 4, 8, 2, 4
ROWS = 16
FRAMES = 64
FEAT = 1152
CH = 128
PART = ROWS // NX
TURN = 2
STRAIGHT = NX * (PART - TURN)
QBLOCKS = NY * ROWS
Q_TURN = ROWS + (NY - 1) * STRAIGHT
UNROLL = 8
SLOTS = 528
HELD = 4608
WIDE = FEAT + CH
PIECE = PART * FRAMES
SEND = PIECE + 16
LIST = 640
EARLY_AT, STEPS_AT = 600, 601
SPARE = QBLOCKS
UNREAL = 1024.0
sharpness = 2.0 * math.sqrt(FEAT)


def shift(value, axis, step):
    size = lax.axis_size(axis)
    return lax.ppermute(value, axis, [(i, (i + step) % size) for i in range(size)])


def normalize(values):
    floats = values.astype(jnp.float32)
    return (floats * lax.rsqrt(jnp.sum(floats * floats, axis=-1, keepdims=True) + epsilon)).astype(jnp.bfloat16)


def prep_kernel(embeddings, prior, valid, piece, turn, e, p, sems):
    first = lax.axis_index("x") * PART
    copies = [
        pltpu.make_async_copy(embeddings.at[pl.ds(first, PART)], e, sems.at[0]),
        pltpu.make_async_copy(prior.at[pl.ds(first, PART)], p, sems.at[1]),
    ]
    for copy in copies:
        copy.start()
    for copy in copies:
        copy.wait()
    row = lax.broadcasted_iota(jnp.int32, (FRAMES, FRAMES), 0)
    col = lax.broadcasted_iota(jnp.int32, (FRAMES, FRAMES), 1)
    pick = row == col
    for b in range(PART):
        units = normalize(e[b])
        real = valid[pl.ds(first + b, 1), :].astype(jnp.float32)
        column = jnp.sum(jnp.where(pick, real, 0.0), axis=1, keepdims=True)
        marked = jnp.where(column > 0.0, p[b].astype(jnp.float32), 2.0 * UNREAL).astype(jnp.bfloat16)
        rows = pl.ds(b * FRAMES, FRAMES)
        piece[rows, :FEAT] = units
        piece[rows, FEAT:] = marked
        if b < TURN:
            turn[rows, :] = units


def list_kernel(codes, out, late):
    def eight(i, counts):
        early_count, late_count = counts
        for u in range(8):
            code = codes[i * 8 + u]
            out[early_count] = code
            late[late_count] = code
            is_late = (code >> 12) & 1
            real = jnp.where(code >= 0, 1, 0)
            early_count = early_count + (real & (1 - is_late))
            late_count = late_count + (real & is_late)
        return early_count, late_count

    early_count, late_count = lax.fori_loop(0, QBLOCKS * 32 // 8, eight, (0, 0))
    for u in range(UNROLL):
        out[early_count + u] = SPARE
        late[late_count + u] = SPARE
    early_steps = (early_count + UNROLL - 1) // UNROLL
    late_steps = (late_count + UNROLL - 1) // UNROLL
    start = early_steps * UNROLL

    def copy(i, carry):
        for u in range(UNROLL):
            out[start + i * UNROLL + u] = late[i * UNROLL + u]
        return carry

    lax.fori_loop(0, late_steps, copy, 0)
    out[EARLY_AT] = early_steps
    out[STEPS_AT] = early_steps + late_steps


def own_kernel(piece, own_weights, own_base):
    row = lax.broadcasted_iota(jnp.int32, (FRAMES, FRAMES), 0)
    col = lax.broadcasted_iota(jnp.int32, (FRAMES, FRAMES), 1)
    for b in range(PART):
        block = piece[b * FRAMES:(b + 1) * FRAMES, :]
        units = block[:, :FEAT]
        affinity = lax.dot_general(
            units, units, (((1,), (1,)), ((), ())), preferred_element_type=jnp.float32
        )
        weights = jnp.where(row == col, 0.0, jnp.exp(sharpness * affinity)).astype(jnp.bfloat16)
        own_weights[b] = weights
        own_base[b] = jnp.dot(weights, values_of(block[:, FEAT:]), preferred_element_type=jnp.float32)


def values_of(scores):
    floats = scores.astype(jnp.float32)
    real = floats < UNREAL
    return jnp.concatenate(
        [jnp.where(real, floats, 0.0), jnp.where(real, 1.0, 0.0)], axis=1
    ).astype(jnp.bfloat16)


def pairs_copy(source, target, sem, i):
    group = pl.ds(i * (UNROLL // 2), UNROLL // 2)
    return pltpu.make_async_copy(source.at[group], target.at[group], sem)


def join_kernel(*refs):
    parts, out, sems = refs[:3], refs[3], refs[4]
    rows = TURN * FRAMES
    copies = [
        pltpu.make_async_copy(part, out.at[pl.ds(d * rows, rows)], sems.at[d]) for d, part in enumerate(parts)
    ]
    for copy in copies:
        copy.start()
    for copy in copies:
        copy.wait()


def first_kernel(lst, keys, *refs):
    queries = refs[:10]
    send_out, w_out, q, k, acc, send, w, sems, w_sem, send_sem = refs[10:]
    half = k.shape[0] // 2
    copies = [pltpu.make_async_copy(keys.at[pl.ds(0, half)], k.at[pl.ds(0, half)], sems.at[0])]
    at = 0
    for part in queries:
        rows = part.shape[0]
        copies.append(pltpu.make_async_copy(part, q.at[pl.ds(at, rows)], sems.at[len(copies)]))
        at += rows
    rest = pltpu.make_async_copy(keys.at[pl.ds(half, half)], k.at[pl.ds(half, half)], sems.at[len(copies)])
    for copy in copies:
        copy.start()
    rest.start()
    acc[...] = jnp.zeros_like(acc)
    for copy in copies:
        copy.wait()
    early_steps, steps = lst[EARLY_AT], lst[STEPS_AT]

    def step(i, carry):
        codes = [lst[i * UNROLL + u] for u in range(UNROLL)]
        key_rows = [pl.multiple_of(((code >> 7) & 63) * FRAMES, FRAMES) for code in codes]
        query_rows = [pl.multiple_of(((code >> 13) & 63) * FRAMES, FRAMES) for code in codes]
        weights = []
        for query_row, key_row in zip(query_rows, key_rows):
            affinity = lax.dot_general(
                q[pl.ds(query_row, FRAMES), :],
                k[pl.ds(key_row, FRAMES), pl.ds(0, FEAT)],
                (((1,), (1,)), ((), ())),
                preferred_element_type=jnp.float32,
            )
            weights.append(jnp.exp(sharpness * affinity).astype(jnp.bfloat16))
        for u in range(UNROLL // 2):
            w[i * (UNROLL // 2) + u] = jnp.concatenate(weights[2 * u:2 * u + 2], axis=1)
        sums = []
        for u, key_row in enumerate(key_rows):
            values = values_of(k[pl.ds(key_row, FRAMES), pl.ds(FEAT, CH)])
            sums.append(jnp.dot(weights[u], values, preferred_element_type=jnp.float32))
        for u, code in enumerate(codes):
            acc[code & 127] += sums[u]
        pairs_copy(w, w_out, w_sem, i).start()
        return carry

    lax.fori_loop(0, early_steps, step, 0)
    rest.wait()
    lax.fori_loop(early_steps, steps, step, 0)
    row = lax.broadcasted_iota(jnp.int32, (FRAMES, CH), 0)
    lane = lax.broadcasted_iota(jnp.int32, (FRAMES, CH), 1)
    pick = row == lane % FRAMES
    low = lax.broadcasted_iota(jnp.int32, (1, CH), 1) < FRAMES

    def finish(d, carry):
        rows = []
        for b in range(PART):
            block = acc[d * PART + b]
            send[d, b * FRAMES:(b + 1) * FRAMES, :] = block[:, :CH].astype(jnp.bfloat16)
            mass = jnp.sum(jnp.where(pick, block[:, CH:], 0.0), axis=0, keepdims=True)
            coarse = mass.astype(jnp.bfloat16).astype(jnp.float32)
            rows.append(jnp.where(low, coarse, mass - coarse))
        rows.append(jnp.zeros((16 - PART, CH), jnp.float32))
        send[d, PIECE:SEND, :] = jnp.concatenate(rows, axis=0).astype(jnp.bfloat16)
        pltpu.make_async_copy(send.at[d], send_out.at[d], send_sem).start()
        return carry

    lax.fori_loop(0, NY * NX, finish, 0)

    def drain_send(d, carry):
        pltpu.make_async_copy(send.at[d], send_out.at[d], send_sem).wait()
        return carry

    lax.fori_loop(0, NY * NX, drain_send, 0)

    def drain(i, carry):
        pairs_copy(w, w_out, w_sem, i).wait()
        return carry

    lax.fori_loop(0, steps, drain, 0)


def second_kernel(lst, w_in, near, far, send, acc, w, w_sem):
    steps = lst[STEPS_AT]

    def fetch(i, carry):
        pairs_copy(w_in, w, w_sem, i).start()
        return carry

    lax.fori_loop(0, steps, fetch, 0)
    acc[...] = jnp.zeros_like(acc)

    def drain(i, carry):
        pairs_copy(w_in, w, w_sem, i).wait()
        return carry

    lax.fori_loop(0, steps, drain, 0)

    def step(i, carry):
        codes = [lst[i * UNROLL + u] for u in range(UNROLL)]
        sums = []
        for u, code in enumerate(codes):
            weights = w[i * (UNROLL // 2) + u // 2][:, (u % 2) * FRAMES:(u % 2 + 1) * FRAMES]
            block = (code >> 21) & 31
            scores = jnp.where(((code >> 20) & 1) == 0, near[block], far[block])
            sums.append(jnp.dot(weights, scores, preferred_element_type=jnp.float32))
        for u, code in enumerate(codes):
            acc[code & 127] += sums[u]
        return carry

    lax.fori_loop(0, steps, step, 0)
    for b in range(QBLOCKS):
        send[b] = acc[b].astype(jnp.bfloat16)


def mix_kernel(got, base, weights, prior, marks, masked, denominator, own_second):
    row = lax.broadcasted_iota(jnp.int32, (FRAMES, CH), 0)
    lane = lax.broadcasted_iota(jnp.int32, (FRAMES, CH), 1)
    pick = (row == lane % FRAMES).astype(jnp.float32)
    for b in range(PART):
        total = base[b, :, :CH]
        for d in range(NY * NX):
            total = total + got[d, b * FRAMES:(b + 1) * FRAMES, :].astype(jnp.float32)
        mass = jnp.sum(got[:, PIECE:SEND, :].astype(jnp.float32), axis=0)[b:b + 1, :]
        column = jnp.sum(pick * mass, axis=1, keepdims=True)
        full = 1.0 + column + base[b, :, CH:]
        denominator[b] = full
        mixed = keep_share * total / full + (1.0 - keep_share) * prior[b].astype(jnp.float32)
        keep = (mixed.astype(jnp.bfloat16).astype(jnp.float32) * marks[b].astype(jnp.float32)).astype(jnp.bfloat16)
        for d in range(NZ):
            masked[d, b] = keep
        own_second[b] = jnp.dot(weights[b], keep, preferred_element_type=jnp.float32)


def last_kernel(got, own_second, denominator, prior, out):
    for b in range(PART):
        total = own_second[b]
        for d in range(NY * NX):
            total = total + got[d, b].astype(jnp.float32)
        mixed = keep_share * total / denominator[b]
        out[b] = (mixed + (1.0 - keep_share) * prior[b].astype(jnp.float32)).astype(jnp.bfloat16)


smem = pl.BlockSpec(memory_space=pltpu.SMEM)
vmem = pl.BlockSpec(memory_space=pltpu.VMEM)
hbm = pl.BlockSpec(memory_space=pl.ANY)
far_memory = pl.BlockSpec(memory_space=pltpu.HBM)


def limit(mebibytes):
    return pltpu.CompilerParams(vmem_limit_bytes=mebibytes * 1024 * 1024)


def body(embeddings, prior_scores, frame_valid, neighbour_ids, neighbour_count, block_home):
    per_list = neighbour_ids.shape[1]
    y, z, c, x = (lax.axis_index(a) for a in ("y", "z", "c", "x"))
    first = x * PART
    piece, turn = pl.pallas_call(
        prep_kernel,
        out_shape=(
            jax.ShapeDtypeStruct((PIECE, WIDE), jnp.bfloat16),
            jax.ShapeDtypeStruct((TURN * FRAMES, FEAT), jnp.bfloat16),
        ),
        in_specs=[hbm, hbm, vmem],
        out_specs=(vmem, vmem),
        scratch_shapes=[
            pltpu.VMEM((PART, FRAMES, FEAT), jnp.bfloat16),
            pltpu.VMEM((PART, FRAMES, CH), jnp.bfloat16),
            pltpu.SemaphoreType.DMA((2,)),
        ],
        compiler_params=limit(59),
    )(embeddings, prior_scores, frame_valid)

    keys = lax.all_gather(piece, ("z", "c"), axis=0, tiled=True)

    embeddings, prior_scores, ids, block_home, piece = lax.optimization_barrier(
        (embeddings, prior_scores, neighbour_ids, block_home, piece)
    )
    prior = lax.dynamic_slice_in_dim(prior_scores, first, PART, 0)
    valid = lax.dynamic_slice_in_dim(frame_valid, first, PART, 0)
    marks = jnp.broadcast_to(valid[:, :, None], prior.shape).astype(jnp.bfloat16)
    target = jnp.take(block_home, ids.reshape(-1), axis=0)
    column = x * per_list + jnp.arange(per_list, dtype=jnp.int32)
    in_list = (column[None, :] < neighbour_count[:, None]).reshape(-1)
    target = jnp.where(in_list, target, -1)
    target = jnp.broadcast_to(target[None, :], (NY * NX, ROWS * per_list))
    target = lax.all_to_all(target, ("y", "x"), split_axis=0, concat_axis=0, tiled=True)

    one, two, three = shift(turn, "y", -1), shift(turn, "y", 2), shift(turn, "y", 1)
    all_units = normalize(embeddings)
    straight = all_units.reshape(NX, PART, FRAMES, FEAT)[:, TURN:].reshape(STRAIGHT * FRAMES, FEAT)
    one, three, straight, target = lax.optimization_barrier((one, three, straight, target))
    behind, ahead = shift(straight, "y", 1), shift(straight, "y", -1)
    rows = (NY - 1) * TURN * FRAMES
    turned = pl.pallas_call(
        join_kernel,
        out_shape=jax.ShapeDtypeStruct((rows, FEAT), jnp.bfloat16),
        in_specs=[hbm] * 3,
        out_specs=hbm,
        scratch_shapes=[pltpu.SemaphoreType.DMA((3,))],
        compiler_params=limit(1),
    )(one, two, three)
    following, leading = shift(turned, "x", -1), shift(turned, "x", 1)
    over = [shift(leading[:rows // 2], "x", 1), shift(following[rows // 2:], "x", -1)]
    turned = [turned, following, *over, leading]

    target = target.reshape(NY, NX, ROWS, per_list)
    source_y = jnp.arange(NY, dtype=jnp.int32)[:, None, None, None]
    source_row = jnp.arange(ROWS, dtype=jnp.int32)[None, None, :, None]
    distance = (source_y - y) % NY
    source = source_y * ROWS + source_row
    wanted = (target >= 0) & (target // 256 == y) & ((target % 16) // PART == x)
    place = (target // 16) % 16
    inner = target % PART
    side = (place % 2) ^ c
    quarter, within = source_row // PART, source_row % PART
    taken = jnp.where(
        distance == 0,
        source_row,
        jnp.where(
            within < TURN,
            Q_TURN + (((quarter - x) % NX) * (NY - 1) + distance - 1) * TURN + within,
            ROWS + (distance - 1) * STRAIGHT + quarter * (PART - TURN) + within - TURN,
        ),
    )
    codes = source | ((place * PART + inner) << 7) | (taken << 13) | (side << 20) | (((place // 2) * PART + inner) << 21)
    codes = jnp.where(wanted, codes, -1).reshape(-1)
    lst = pl.pallas_call(
        list_kernel,
        out_shape=jax.ShapeDtypeStruct((LIST,), jnp.int32),
        in_specs=[smem],
        out_specs=smem,
        scratch_shapes=[pltpu.SMEM((LIST,), jnp.int32)],
        compiler_params=limit(1),
    )(codes)
    half = STRAIGHT * FRAMES // 2
    behind, ahead, lst = lax.optimization_barrier((behind, ahead, lst))
    across = [shift(behind[:half], "y", 1), shift(ahead[half:], "y", -1)]
    own_weights, own_base = pl.pallas_call(
        own_kernel,
        out_shape=(
            jax.ShapeDtypeStruct((PART, FRAMES, FRAMES), jnp.bfloat16),
            jax.ShapeDtypeStruct((PART, FRAMES, 2 * CH), jnp.float32),
        ),
        in_specs=[vmem],
        out_specs=(vmem, vmem),
        compiler_params=limit(4),
    )(piece)

    send, weights = pl.pallas_call(
        first_kernel,
        out_shape=(
            jax.ShapeDtypeStruct((NY * NX, SEND, CH), jnp.bfloat16),
            jax.ShapeDtypeStruct((HELD, FRAMES, 2 * FRAMES), jnp.bfloat16),
        ),
        in_specs=[smem] + [hbm] * 11,
        out_specs=(far_memory, far_memory),
        scratch_shapes=[
            pltpu.VMEM((QBLOCKS * FRAMES, FEAT), jnp.bfloat16),
            pltpu.VMEM((NZ * NC * PIECE, WIDE), jnp.bfloat16),
            pltpu.VMEM((QBLOCKS + 1, FRAMES, 2 * CH), jnp.float32),
            pltpu.VMEM((NY * NX, SEND, CH), jnp.bfloat16),
            pltpu.VMEM((SLOTS // 2, FRAMES, 2 * FRAMES), jnp.bfloat16),
            pltpu.SemaphoreType.DMA((12,)),
            pltpu.SemaphoreType.DMA,
            pltpu.SemaphoreType.DMA,
        ],
        compiler_params=limit(58),
    )(lst, keys, all_units.reshape(ROWS * FRAMES, FEAT), ahead, *across, behind, *turned)
    got = lax.all_to_all(send, ("y", "x"), split_axis=0, concat_axis=0, tiled=True)

    masked, denominator, own_second = pl.pallas_call(
        mix_kernel,
        out_shape=(
            jax.ShapeDtypeStruct((NZ, PART, FRAMES, CH), jnp.bfloat16),
            jax.ShapeDtypeStruct((PART, FRAMES, CH), jnp.float32),
            jax.ShapeDtypeStruct((PART, FRAMES, CH), jnp.float32),
        ),
        in_specs=[vmem] * 5,
        out_specs=(vmem,) * 3,
        compiler_params=limit(8),
    )(got, own_base, own_weights, prior, marks)
    near_scores = lax.all_to_all(masked, "z", split_axis=0, concat_axis=0, tiled=True)
    near_scores = near_scores.reshape(NZ * PART, FRAMES, CH)
    far_scores = shift(near_scores, "c", 1)

    send = pl.pallas_call(
        second_kernel,
        out_shape=jax.ShapeDtypeStruct((QBLOCKS, FRAMES, CH), jnp.bfloat16),
        in_specs=[smem, far_memory, vmem, vmem],
        out_specs=vmem,
        scratch_shapes=[
            pltpu.VMEM((QBLOCKS + 1, FRAMES, CH), jnp.float32),
            pltpu.VMEM((SLOTS // 2, FRAMES, 2 * FRAMES), jnp.bfloat16),
            pltpu.SemaphoreType.DMA,
        ],
        compiler_params=limit(16),
    )(lst, weights, near_scores, far_scores)
    got = lax.all_to_all(send, ("y", "x"), split_axis=0, concat_axis=0, tiled=True)
    return pl.pallas_call(
        last_kernel,
        out_shape=jax.ShapeDtypeStruct((PART, FRAMES, CH), jnp.bfloat16),
        in_specs=[vmem] * 4,
        out_specs=vmem,
        compiler_params=limit(8),
    )(got.reshape(NY * NX, PART, FRAMES, CH), own_second, denominator, prior)


def solution(mesh):
    fine = Mesh(mesh.devices.reshape(NY, NZ, NC, NX), ("y", "z", "c", "x"))
    bucket = ("y", "z", "c")
    in_specs = (P(bucket, None, None), P(bucket, None, None), P(bucket, None), P(bucket, "x"), P(bucket), P())
    out_specs = P(("y", "z", "c", "x"), None, None)
    return jax.shard_map(body, mesh=fine, in_specs=in_specs, out_specs=out_specs, check_vma=False)
```

```python
import math

import jax
import jax.numpy as jnp
from jax import lax
from jax.experimental import pallas as pl
from jax.experimental.pallas import tpu as pltpu
from jax.sharding import Mesh
from jax.sharding import PartitionSpec as P

epsilon = 1e-06
keep_share = 0.9

NY, NZ, NC, NX = 4, 8, 2, 4
ROWS = 16
FRAMES = 64
FEAT = 1152
CH = 128
PART = ROWS // NX
TURN = 2
STRAIGHT = NX * (PART - TURN)
QBLOCKS = NY * ROWS
Q_TURN = ROWS + (NY - 1) * STRAIGHT
UNROLL = 8
SLOTS = 528
HELD = 4608
WIDE = FEAT + CH
PIECE = PART * FRAMES
SEND = PIECE + 16
LIST = 640
EARLY_AT, STEPS_AT = 600, 601
SPARE = QBLOCKS
UNREAL = 1024.0
sharpness = 2.0 * math.sqrt(FEAT)


def shift(value, axis, step):
    size = lax.axis_size(axis)
    return lax.ppermute(value, axis, [(i, (i + step) % size) for i in range(size)])


def normalize(values):
    floats = values.astype(jnp.float32)
    return (floats * lax.rsqrt(jnp.sum(floats * floats, axis=-1, keepdims=True) + epsilon)).astype(jnp.bfloat16)


def prep_kernel(embeddings, prior, marks, piece_out, turn_out, e, p, valid, piece, sems, out_sems):
    first = lax.axis_index("x") * PART
    shared = [
        pltpu.make_async_copy(prior.at[pl.ds(first, PART)], p, sems.at[PART]),
        pltpu.make_async_copy(marks, valid, sems.at[PART + 1]),
    ]
    blocks = [pltpu.make_async_copy(embeddings.at[first + b], e.at[b], sems.at[b]) for b in range(PART)]
    for copy in shared + blocks:
        copy.start()
    for copy in shared:
        copy.wait()
    row = lax.broadcasted_iota(jnp.int32, (FRAMES, FRAMES), 0)
    col = lax.broadcasted_iota(jnp.int32, (FRAMES, FRAMES), 1)
    pick = row == col
    outs = []
    for b in range(PART):
        rows = pl.ds(b * FRAMES, FRAMES)
        real = valid[pl.ds(first + b, 1), :].astype(jnp.float32)
        column = jnp.sum(jnp.where(pick, real, 0.0), axis=1, keepdims=True)
        marked = jnp.where(column > 0.0, p[b].astype(jnp.float32), 2.0 * UNREAL).astype(jnp.bfloat16)
        piece[rows, FEAT:] = marked
        blocks[b].wait()
        piece[rows, :FEAT] = normalize(e[b])
        outs.append(pltpu.make_async_copy(piece.at[rows], piece_out.at[rows], out_sems.at[len(outs)]))
        outs[-1].start()
        if b < TURN:
            units = piece.at[rows, pl.ds(0, FEAT)]
            outs.append(pltpu.make_async_copy(units, turn_out.at[rows], out_sems.at[len(outs)]))
            outs[-1].start()
    for copy in outs:
        copy.wait()


def list_kernel(codes, out, late):
    def eight(i, counts):
        early_count, late_count = counts
        for u in range(8):
            code = codes[i * 8 + u]
            out[early_count] = code
            late[late_count] = code
            is_late = (code >> 12) & 1
            real = jnp.where(code >= 0, 1, 0)
            early_count = early_count + (real & (1 - is_late))
            late_count = late_count + (real & is_late)
        return early_count, late_count

    early_count, late_count = lax.fori_loop(0, QBLOCKS * 32 // 8, eight, (0, 0))
    for u in range(UNROLL):
        out[early_count + u] = SPARE
        late[late_count + u] = SPARE
    early_steps = (early_count + UNROLL - 1) // UNROLL
    late_steps = (late_count + UNROLL - 1) // UNROLL
    start = early_steps * UNROLL

    def copy(i, carry):
        for u in range(UNROLL):
            out[start + i * UNROLL + u] = late[i * UNROLL + u]
        return carry

    lax.fori_loop(0, late_steps, copy, 0)
    out[EARLY_AT] = early_steps
    out[STEPS_AT] = early_steps + late_steps


def own_kernel(piece, own_weights, own_base):
    row = lax.broadcasted_iota(jnp.int32, (FRAMES, FRAMES), 0)
    col = lax.broadcasted_iota(jnp.int32, (FRAMES, FRAMES), 1)
    for b in range(PART):
        block = piece[b * FRAMES:(b + 1) * FRAMES, :]
        units = block[:, :FEAT]
        affinity = lax.dot_general(
            units, units, (((1,), (1,)), ((), ())), preferred_element_type=jnp.float32
        )
        weights = jnp.where(row == col, 0.0, jnp.exp(sharpness * affinity)).astype(jnp.bfloat16)
        own_weights[b] = weights
        own_base[b] = jnp.dot(weights, values_of(block[:, FEAT:]), preferred_element_type=jnp.float32)


def values_of(scores):
    floats = scores.astype(jnp.float32)
    real = floats < UNREAL
    return jnp.concatenate(
        [jnp.where(real, floats, 0.0), jnp.where(real, 1.0, 0.0)], axis=1
    ).astype(jnp.bfloat16)


def pairs_copy(source, target, sem, i):
    group = pl.ds(i * (UNROLL // 2), UNROLL // 2)
    return pltpu.make_async_copy(source.at[group], target.at[group], sem)


def join_kernel(*refs):
    parts, out, sems = refs[:3], refs[3], refs[4]
    rows = TURN * FRAMES
    copies = [
        pltpu.make_async_copy(part, out.at[pl.ds(d * rows, rows)], sems.at[d]) for d, part in enumerate(parts)
    ]
    for copy in copies:
        copy.start()
    for copy in copies:
        copy.wait()


def first_kernel(lst_in, keys, *refs):
    queries = refs[:10]
    send_out, w_out, q, k, acc, send, w, lst, sems, w_sem, send_sem, lst_sem = refs[10:]
    lst_copy = pltpu.make_async_copy(lst_in, lst, lst_sem)
    lst_copy.start()
    half = k.shape[0] // 2
    copies = [pltpu.make_async_copy(keys.at[pl.ds(0, half)], k.at[pl.ds(0, half)], sems.at[0])]
    at = 0
    for part in queries:
        rows = part.shape[0]
        copies.append(pltpu.make_async_copy(part, q.at[pl.ds(at, rows)], sems.at[len(copies)]))
        at += rows
    rest = pltpu.make_async_copy(keys.at[pl.ds(half, half)], k.at[pl.ds(half, half)], sems.at[len(copies)])
    for copy in copies:
        copy.start()
    rest.start()
    acc[...] = jnp.zeros_like(acc)
    for copy in copies:
        copy.wait()
    lst_copy.wait()
    early_steps, steps = lst[EARLY_AT], lst[STEPS_AT]

    def step(i, carry):
        codes = [lst[i * UNROLL + u] for u in range(UNROLL)]
        key_rows = [pl.multiple_of(((code >> 7) & 63) * FRAMES, FRAMES) for code in codes]
        query_rows = [pl.multiple_of(((code >> 13) & 63) * FRAMES, FRAMES) for code in codes]
        weights = []
        for query_row, key_row in zip(query_rows, key_rows):
            affinity = lax.dot_general(
                q[pl.ds(query_row, FRAMES), :],
                k[pl.ds(key_row, FRAMES), pl.ds(0, FEAT)],
                (((1,), (1,)), ((), ())),
                preferred_element_type=jnp.float32,
            )
            weights.append(jnp.exp(sharpness * affinity).astype(jnp.bfloat16))
        for u in range(UNROLL // 2):
            w[i * (UNROLL // 2) + u] = jnp.concatenate(weights[2 * u:2 * u + 2], axis=1)
        sums = []
        for u, key_row in enumerate(key_rows):
            values = values_of(k[pl.ds(key_row, FRAMES), pl.ds(FEAT, CH)])
            sums.append(jnp.dot(weights[u], values, preferred_element_type=jnp.float32))
        for u, code in enumerate(codes):
            acc[code & 127] += sums[u]
        pairs_copy(w, w_out, w_sem, i).start()
        return carry

    lax.fori_loop(0, early_steps, step, 0)
    rest.wait()
    lax.fori_loop(early_steps, steps, step, 0)
    row = lax.broadcasted_iota(jnp.int32, (FRAMES, CH), 0)
    lane = lax.broadcasted_iota(jnp.int32, (FRAMES, CH), 1)
    pick = row == lane % FRAMES
    low = lax.broadcasted_iota(jnp.int32, (1, CH), 1) < FRAMES

    def finish(d, carry):
        rows = []
        for b in range(PART):
            block = acc[d * PART + b]
            send[d, b * FRAMES:(b + 1) * FRAMES, :] = block[:, :CH].astype(jnp.bfloat16)
            mass = jnp.sum(jnp.where(pick, block[:, CH:], 0.0), axis=0, keepdims=True)
            coarse = mass.astype(jnp.bfloat16).astype(jnp.float32)
            rows.append(jnp.where(low, coarse, mass - coarse))
        rows.append(jnp.zeros((16 - PART, CH), jnp.float32))
        send[d, PIECE:SEND, :] = jnp.concatenate(rows, axis=0).astype(jnp.bfloat16)
        pltpu.make_async_copy(send.at[d], send_out.at[d], send_sem).start()
        return carry

    lax.fori_loop(0, NY * NX, finish, 0)

    def drain_send(d, carry):
        pltpu.make_async_copy(send.at[d], send_out.at[d], send_sem).wait()
        return carry

    lax.fori_loop(0, NY * NX, drain_send, 0)

    def drain(i, carry):
        pairs_copy(w, w_out, w_sem, i).wait()
        return carry

    lax.fori_loop(0, steps, drain, 0)


def second_kernel(lst, w_in, near, far, send, acc, w, w_sem):
    steps = lst[STEPS_AT]

    def fetch(i, carry):
        pairs_copy(w_in, w, w_sem, i).start()
        return carry

    lax.fori_loop(0, steps, fetch, 0)
    acc[...] = jnp.zeros_like(acc)

    def drain(i, carry):
        pairs_copy(w_in, w, w_sem, i).wait()
        return carry

    lax.fori_loop(0, steps, drain, 0)

    def step(i, carry):
        codes = [lst[i * UNROLL + u] for u in range(UNROLL)]
        sums = []
        for u, code in enumerate(codes):
            weights = w[i * (UNROLL // 2) + u // 2][:, (u % 2) * FRAMES:(u % 2 + 1) * FRAMES]
            block = (code >> 21) & 31
            scores = jnp.where(((code >> 20) & 1) == 0, near[block], far[block])
            sums.append(jnp.dot(weights, scores, preferred_element_type=jnp.float32))
        for u, code in enumerate(codes):
            acc[code & 127] += sums[u]
        return carry

    lax.fori_loop(0, steps, step, 0)
    for b in range(QBLOCKS):
        send[b] = acc[b].astype(jnp.bfloat16)


def mix_kernel(got, base, weights, prior, marks, masked, denominator, own_second):
    row = lax.broadcasted_iota(jnp.int32, (FRAMES, CH), 0)
    lane = lax.broadcasted_iota(jnp.int32, (FRAMES, CH), 1)
    pick = (row == lane % FRAMES).astype(jnp.float32)
    for b in range(PART):
        total = base[b, :, :CH]
        for d in range(NY * NX):
            total = total + got[d, b * FRAMES:(b + 1) * FRAMES, :].astype(jnp.float32)
        mass = jnp.sum(got[:, PIECE:SEND, :].astype(jnp.float32), axis=0)[b:b + 1, :]
        column = jnp.sum(pick * mass, axis=1, keepdims=True)
        full = 1.0 + column + base[b, :, CH:]
        denominator[b] = full
        mixed = keep_share * total / full + (1.0 - keep_share) * prior[b].astype(jnp.float32)
        keep = (mixed.astype(jnp.bfloat16).astype(jnp.float32) * marks[b].astype(jnp.float32)).astype(jnp.bfloat16)
        for d in range(NZ):
            masked[d, b] = keep
        own_second[b] = jnp.dot(weights[b], keep, preferred_element_type=jnp.float32)


def last_kernel(got, own_second, denominator, prior, out):
    for b in range(PART):
        total = own_second[b]
        for d in range(NY * NX):
            total = total + got[d, b].astype(jnp.float32)
        mixed = keep_share * total / denominator[b]
        out[b] = (mixed + (1.0 - keep_share) * prior[b].astype(jnp.float32)).astype(jnp.bfloat16)


smem = pl.BlockSpec(memory_space=pltpu.SMEM)
vmem = pl.BlockSpec(memory_space=pltpu.VMEM)
hbm = pl.BlockSpec(memory_space=pl.ANY)
far_memory = pl.BlockSpec(memory_space=pltpu.HBM)


def limit(mebibytes):
    return pltpu.CompilerParams(vmem_limit_bytes=mebibytes * 1024 * 1024)


def body(embeddings, prior_scores, frame_valid, neighbour_ids, neighbour_count, block_home):
    per_list = neighbour_ids.shape[1]
    y, z, c, x = (lax.axis_index(a) for a in ("y", "z", "c", "x"))
    first = x * PART
    piece, turn = pl.pallas_call(
        prep_kernel,
        out_shape=(
            jax.ShapeDtypeStruct((PIECE, WIDE), jnp.bfloat16),
            jax.ShapeDtypeStruct((TURN * FRAMES, FEAT), jnp.bfloat16),
        ),
        in_specs=[hbm, hbm, hbm],
        out_specs=(far_memory, far_memory),
        scratch_shapes=[
            pltpu.VMEM((PART, FRAMES, FEAT), jnp.bfloat16),
            pltpu.VMEM((PART, FRAMES, CH), jnp.bfloat16),
            pltpu.VMEM((ROWS, FRAMES), jnp.int32),
            pltpu.VMEM((PIECE, WIDE), jnp.bfloat16),
            pltpu.SemaphoreType.DMA((PART + 2,)),
            pltpu.SemaphoreType.DMA((PART + TURN,)),
        ],
        compiler_params=limit(59),
    )(embeddings, prior_scores, frame_valid)

    keys = lax.all_gather(piece, ("z", "c"), axis=0, tiled=True)

    embeddings, prior_scores, ids, block_home, piece = lax.optimization_barrier(
        (embeddings, prior_scores, neighbour_ids, block_home, piece)
    )
    prior = lax.dynamic_slice_in_dim(prior_scores, first, PART, 0)
    valid = lax.dynamic_slice_in_dim(frame_valid, first, PART, 0)
    marks = jnp.broadcast_to(valid[:, :, None], prior.shape).astype(jnp.bfloat16)
    target = jnp.take(block_home, ids.reshape(-1), axis=0)
    column = x * per_list + jnp.arange(per_list, dtype=jnp.int32)
    in_list = (column[None, :] < neighbour_count[:, None]).reshape(-1)
    target = jnp.where(in_list, target, -1)
    target = jnp.broadcast_to(target[None, :], (NY * NX, ROWS * per_list))
    target = lax.all_to_all(target, ("y", "x"), split_axis=0, concat_axis=0, tiled=True)

    one, two, three = shift(turn, "y", -1), shift(turn, "y", 2), shift(turn, "y", 1)
    all_units = normalize(embeddings)
    straight = all_units.reshape(NX, PART, FRAMES, FEAT)[:, TURN:].reshape(STRAIGHT * FRAMES, FEAT)
    one, three, straight, target = lax.optimization_barrier((one, three, straight, target))
    behind, ahead = shift(straight, "y", 1), shift(straight, "y", -1)
    rows = (NY - 1) * TURN * FRAMES
    turned = pl.pallas_call(
        join_kernel,
        out_shape=jax.ShapeDtypeStruct((rows, FEAT), jnp.bfloat16),
        in_specs=[hbm] * 3,
        out_specs=hbm,
        scratch_shapes=[pltpu.SemaphoreType.DMA((3,))],
        compiler_params=limit(1),
    )(one, two, three)
    following, leading = shift(turned, "x", -1), shift(turned, "x", 1)
    over = [shift(leading[:rows // 2], "x", 1), shift(following[rows // 2:], "x", -1)]
    turned = [turned, following, *over, leading]

    target = target.reshape(NY, NX, ROWS, per_list)
    source_y = jnp.arange(NY, dtype=jnp.int32)[:, None, None, None]
    source_row = jnp.arange(ROWS, dtype=jnp.int32)[None, None, :, None]
    distance = (source_y - y) % NY
    source = source_y * ROWS + source_row
    wanted = (target >= 0) & (target // 256 == y) & ((target % 16) // PART == x)
    place = (target // 16) % 16
    inner = target % PART
    side = (place % 2) ^ c
    quarter, within = source_row // PART, source_row % PART
    taken = jnp.where(
        distance == 0,
        source_row,
        jnp.where(
            within < TURN,
            Q_TURN + (((quarter - x) % NX) * (NY - 1) + distance - 1) * TURN + within,
            ROWS + (distance - 1) * STRAIGHT + quarter * (PART - TURN) + within - TURN,
        ),
    )
    codes = source | ((place * PART + inner) << 7) | (taken << 13) | (side << 20) | (((place // 2) * PART + inner) << 21)
    codes = jnp.where(wanted, codes, -1).reshape(-1)
    lst = pl.pallas_call(
        list_kernel,
        out_shape=jax.ShapeDtypeStruct((LIST,), jnp.int32),
        in_specs=[smem],
        out_specs=smem,
        scratch_shapes=[pltpu.SMEM((LIST,), jnp.int32)],
        compiler_params=limit(1),
    )(codes)
    half = STRAIGHT * FRAMES // 2
    behind, ahead, lst = lax.optimization_barrier((behind, ahead, lst))
    across = [shift(behind[:half], "y", 1), shift(ahead[half:], "y", -1)]
    own_weights, own_base = pl.pallas_call(
        own_kernel,
        out_shape=(
            jax.ShapeDtypeStruct((PART, FRAMES, FRAMES), jnp.bfloat16),
            jax.ShapeDtypeStruct((PART, FRAMES, 2 * CH), jnp.float32),
        ),
        in_specs=[vmem],
        out_specs=(vmem, vmem),
        compiler_params=limit(4),
    )(piece)

    send, weights = pl.pallas_call(
        first_kernel,
        out_shape=(
            jax.ShapeDtypeStruct((NY * NX, SEND, CH), jnp.bfloat16),
            jax.ShapeDtypeStruct((HELD, FRAMES, 2 * FRAMES), jnp.bfloat16),
        ),
        in_specs=[hbm] * 12,
        out_specs=(far_memory, far_memory),
        scratch_shapes=[
            pltpu.VMEM((QBLOCKS * FRAMES, FEAT), jnp.bfloat16),
            pltpu.VMEM((NZ * NC * PIECE, WIDE), jnp.bfloat16),
            pltpu.VMEM((QBLOCKS + 1, FRAMES, 2 * CH), jnp.float32),
            pltpu.VMEM((NY * NX, SEND, CH), jnp.bfloat16),
            pltpu.VMEM((SLOTS // 2, FRAMES, 2 * FRAMES), jnp.bfloat16),
            pltpu.SMEM((LIST,), jnp.int32),
            pltpu.SemaphoreType.DMA((12,)),
            pltpu.SemaphoreType.DMA,
            pltpu.SemaphoreType.DMA,
            pltpu.SemaphoreType.DMA,
        ],
        compiler_params=limit(58),
    )(lst, keys, all_units.reshape(ROWS * FRAMES, FEAT), ahead, *across, behind, *turned)
    got = lax.all_to_all(send, ("y", "x"), split_axis=0, concat_axis=0, tiled=True)

    masked, denominator, own_second = pl.pallas_call(
        mix_kernel,
        out_shape=(
            jax.ShapeDtypeStruct((NZ, PART, FRAMES, CH), jnp.bfloat16),
            jax.ShapeDtypeStruct((PART, FRAMES, CH), jnp.float32),
            jax.ShapeDtypeStruct((PART, FRAMES, CH), jnp.float32),
        ),
        in_specs=[vmem] * 5,
        out_specs=(vmem,) * 3,
        compiler_params=limit(8),
    )(got, own_base, own_weights, prior, marks)
    near_scores = lax.all_to_all(masked, "z", split_axis=0, concat_axis=0, tiled=True)
    near_scores = near_scores.reshape(NZ * PART, FRAMES, CH)
    far_scores = shift(near_scores, "c", 1)

    send = pl.pallas_call(
        second_kernel,
        out_shape=jax.ShapeDtypeStruct((QBLOCKS, FRAMES, CH), jnp.bfloat16),
        in_specs=[smem, far_memory, vmem, vmem],
        out_specs=vmem,
        scratch_shapes=[
            pltpu.VMEM((QBLOCKS + 1, FRAMES, CH), jnp.float32),
            pltpu.VMEM((SLOTS // 2, FRAMES, 2 * FRAMES), jnp.bfloat16),
            pltpu.SemaphoreType.DMA,
        ],
        compiler_params=limit(16),
    )(lst, weights, near_scores, far_scores)
    got = lax.all_to_all(send, ("y", "x"), split_axis=0, concat_axis=0, tiled=True)
    return pl.pallas_call(
        last_kernel,
        out_shape=jax.ShapeDtypeStruct((PART, FRAMES, CH), jnp.bfloat16),
        in_specs=[vmem] * 4,
        out_specs=vmem,
        compiler_params=limit(8),
    )(got.reshape(NY * NX, PART, FRAMES, CH), own_second, denominator, prior)


def solution(mesh):
    fine = Mesh(mesh.devices.reshape(NY, NZ, NC, NX), ("y", "z", "c", "x"))
    bucket = ("y", "z", "c")
    in_specs = (P(bucket, None, None), P(bucket, None, None), P(bucket, None), P(bucket, "x"), P(bucket), P())
    out_specs = P(("y", "z", "c", "x"), None, None)
    return jax.shard_map(body, mesh=fine, in_specs=in_specs, out_specs=out_specs, check_vma=False)
```

```python
import math

import jax
import jax.numpy as jnp
from jax import lax
from jax.experimental import pallas as pl
from jax.experimental.pallas import tpu as pltpu
from jax.sharding import Mesh
from jax.sharding import PartitionSpec as P

epsilon = 1e-06
keep_share = 0.9

NY, NZ, NC, NX = 4, 8, 2, 4
ROWS = 16
FRAMES = 64
FEAT = 1152
CH = 128
PART = ROWS // NX
TURN = 2
STRAIGHT = NX * (PART - TURN)
QBLOCKS = NY * ROWS
Q_TURN = ROWS + (NY - 1) * STRAIGHT
UNROLL = 8
SLOTS = 528
HELD = 4608
WIDE = FEAT + CH
PIECE = PART * FRAMES
SEND = PIECE + 16
LIST = 640
FIRST_AT, SECOND_AT, STEPS_AT = 600, 601, 602
SPARE = QBLOCKS
UNREAL = 1024.0
sharpness = 2.0 * math.sqrt(FEAT)


def shift(value, axis, step):
    size = lax.axis_size(axis)
    return lax.ppermute(value, axis, [(i, (i + step) % size) for i in range(size)])


def normalize(values):
    floats = values.astype(jnp.float32)
    return (floats * lax.rsqrt(jnp.sum(floats * floats, axis=-1, keepdims=True) + epsilon)).astype(jnp.bfloat16)


def prep_kernel(embeddings, prior, marks, piece_out, turn_out, e, p, valid, piece, sems, out_sems):
    first = lax.axis_index("x") * PART
    shared = [
        pltpu.make_async_copy(prior.at[pl.ds(first, PART)], p, sems.at[PART]),
        pltpu.make_async_copy(marks, valid, sems.at[PART + 1]),
    ]
    blocks = [pltpu.make_async_copy(embeddings.at[first + b], e.at[b], sems.at[b]) for b in range(PART)]
    for copy in shared + blocks:
        copy.start()
    for copy in shared:
        copy.wait()
    row = lax.broadcasted_iota(jnp.int32, (FRAMES, FRAMES), 0)
    col = lax.broadcasted_iota(jnp.int32, (FRAMES, FRAMES), 1)
    pick = row == col
    outs = []
    for b in range(PART):
        rows = pl.ds(b * FRAMES, FRAMES)
        real = valid[pl.ds(first + b, 1), :].astype(jnp.float32)
        column = jnp.sum(jnp.where(pick, real, 0.0), axis=1, keepdims=True)
        marked = jnp.where(column > 0.0, p[b].astype(jnp.float32), 2.0 * UNREAL).astype(jnp.bfloat16)
        piece[rows, FEAT:] = marked
        blocks[b].wait()
        piece[rows, :FEAT] = normalize(e[b])
        outs.append(pltpu.make_async_copy(piece.at[rows], piece_out.at[rows], out_sems.at[len(outs)]))
        outs[-1].start()
        if b < TURN:
            units = piece.at[rows, pl.ds(0, FEAT)]
            outs.append(pltpu.make_async_copy(units, turn_out.at[rows], out_sems.at[len(outs)]))
            outs[-1].start()
    for copy in outs:
        copy.wait()


def list_kernel(codes, out, found):
    def eight(i, count):
        for u in range(8):
            code = codes[i * 8 + u]
            found[count] = code
            count = count + jnp.where(code >= 0, 1, 0)
        return count

    count = lax.fori_loop(0, QBLOCKS * 32 // 8, eight, 0)

    def kind_of(code):
        return ((code >> 12) & 1) + jnp.where(((code >> 13) & 63) >= Q_TURN, 2, 0)

    def tally(i, counts):
        kind = kind_of(found[i])
        return tuple(n + jnp.where(kind == j, 1, 0) for j, n in enumerate(counts))

    one, two, three = lax.fori_loop(0, count, tally, (0, 0, 0))

    def place(i, at):
        code = found[i]
        kind = kind_of(code)
        out[jnp.where(kind < 2, jnp.where(kind == 0, at[0], at[1]), jnp.where(kind == 2, at[2], at[3]))] = code
        return tuple(n + jnp.where(kind == j, 1, 0) for j, n in enumerate(at))

    lax.fori_loop(0, count, place, (0, one, one + two, one + two + three))
    for u in range(UNROLL):
        out[count + u] = SPARE
    out[FIRST_AT] = one // UNROLL
    out[SECOND_AT] = (one + two) // UNROLL
    out[STEPS_AT] = (count + UNROLL - 1) // UNROLL


def own_kernel(piece, own_weights, own_base):
    row = lax.broadcasted_iota(jnp.int32, (FRAMES, FRAMES), 0)
    col = lax.broadcasted_iota(jnp.int32, (FRAMES, FRAMES), 1)
    for b in range(PART):
        block = piece[b * FRAMES:(b + 1) * FRAMES, :]
        units = block[:, :FEAT]
        affinity = lax.dot_general(
            units, units, (((1,), (1,)), ((), ())), preferred_element_type=jnp.float32
        )
        weights = jnp.where(row == col, 0.0, jnp.exp(sharpness * affinity)).astype(jnp.bfloat16)
        own_weights[b] = weights
        own_base[b] = jnp.dot(weights, values_of(block[:, FEAT:]), preferred_element_type=jnp.float32)


def values_of(scores):
    floats = scores.astype(jnp.float32)
    real = floats < UNREAL
    return jnp.concatenate(
        [jnp.where(real, floats, 0.0), jnp.where(real, 1.0, 0.0)], axis=1
    ).astype(jnp.bfloat16)


def pairs_copy(source, target, sem, i):
    group = pl.ds(i * (UNROLL // 2), UNROLL // 2)
    return pltpu.make_async_copy(source.at[group], target.at[group], sem)


def join_kernel(*refs):
    parts, out, sems = refs[:3], refs[3], refs[4]
    rows = TURN * FRAMES
    copies = [
        pltpu.make_async_copy(part, out.at[pl.ds(d * rows, rows)], sems.at[d]) for d, part in enumerate(parts)
    ]
    for copy in copies:
        copy.start()
    for copy in copies:
        copy.wait()


def first_kernel(lst_in, keys, *refs):
    queries = refs[:10]
    send_out, w_out, q, k, acc, send, w, lst, sems, w_sem, send_sem, lst_sem = refs[10:]
    lst_copy = pltpu.make_async_copy(lst_in, lst, lst_sem)
    lst_copy.start()
    half = k.shape[0] // 2
    q_copies = []
    at = 0
    for part in queries:
        rows = part.shape[0]
        q_copies.append(pltpu.make_async_copy(part, q.at[pl.ds(at, rows)], sems.at[len(q_copies)]))
        at += rows
    k_copies = [
        pltpu.make_async_copy(keys.at[pl.ds(i * half, half)], k.at[pl.ds(i * half, half)], sems.at[10 + i])
        for i in range(2)
    ]
    straight, turned = q_copies[:5], q_copies[5:]
    for copy in straight + k_copies + turned:
        copy.start()
    acc[...] = jnp.zeros_like(acc)
    lst_copy.wait()
    for copy in straight + k_copies[:1]:
        copy.wait()
    steps = lst[STEPS_AT]

    def step(i, carry):
        codes = [lst[i * UNROLL + u] for u in range(UNROLL)]
        key_rows = [pl.multiple_of(((code >> 7) & 63) * FRAMES, FRAMES) for code in codes]
        query_rows = [pl.multiple_of(((code >> 13) & 63) * FRAMES, FRAMES) for code in codes]
        weights = []
        for query_row, key_row in zip(query_rows, key_rows):
            affinity = lax.dot_general(
                q[pl.ds(query_row, FRAMES), :],
                k[pl.ds(key_row, FRAMES), pl.ds(0, FEAT)],
                (((1,), (1,)), ((), ())),
                preferred_element_type=jnp.float32,
            )
            weights.append(jnp.exp(sharpness * affinity).astype(jnp.bfloat16))
        for u in range(UNROLL // 2):
            w[i * (UNROLL // 2) + u] = jnp.concatenate(weights[2 * u:2 * u + 2], axis=1)
        sums = []
        for u, key_row in enumerate(key_rows):
            values = values_of(k[pl.ds(key_row, FRAMES), pl.ds(FEAT, CH)])
            sums.append(jnp.dot(weights[u], values, preferred_element_type=jnp.float32))
        for u, code in enumerate(codes):
            acc[code & 127] += sums[u]
        pairs_copy(w, w_out, w_sem, i).start()
        return carry

    lax.fori_loop(0, lst[FIRST_AT], step, 0)
    k_copies[1].wait()
    lax.fori_loop(lst[FIRST_AT], lst[SECOND_AT], step, 0)
    for copy in turned:
        copy.wait()
    lax.fori_loop(lst[SECOND_AT], steps, step, 0)
    row = lax.broadcasted_iota(jnp.int32, (FRAMES, CH), 0)
    lane = lax.broadcasted_iota(jnp.int32, (FRAMES, CH), 1)
    pick = row == lane % FRAMES
    low = lax.broadcasted_iota(jnp.int32, (1, CH), 1) < FRAMES

    def finish(d, carry):
        rows = []
        for b in range(PART):
            block = acc[d * PART + b]
            send[d, b * FRAMES:(b + 1) * FRAMES, :] = block[:, :CH].astype(jnp.bfloat16)
            mass = jnp.sum(jnp.where(pick, block[:, CH:], 0.0), axis=0, keepdims=True)
            coarse = mass.astype(jnp.bfloat16).astype(jnp.float32)
            rows.append(jnp.where(low, coarse, mass - coarse))
        rows.append(jnp.zeros((16 - PART, CH), jnp.float32))
        send[d, PIECE:SEND, :] = jnp.concatenate(rows, axis=0).astype(jnp.bfloat16)
        pltpu.make_async_copy(send.at[d], send_out.at[d], send_sem).start()
        return carry

    lax.fori_loop(0, NY * NX, finish, 0)

    def drain_send(d, carry):
        pltpu.make_async_copy(send.at[d], send_out.at[d], send_sem).wait()
        return carry

    lax.fori_loop(0, NY * NX, drain_send, 0)

    def drain(i, carry):
        pairs_copy(w, w_out, w_sem, i).wait()
        return carry

    lax.fori_loop(0, steps, drain, 0)


def second_kernel(lst, w_in, near, far, send, acc, w, w_sem):
    steps = lst[STEPS_AT]

    def fetch(i, carry):
        pairs_copy(w_in, w, w_sem, i).start()
        return carry

    lax.fori_loop(0, steps, fetch, 0)
    acc[...] = jnp.zeros_like(acc)

    def drain(i, carry):
        pairs_copy(w_in, w, w_sem, i).wait()
        return carry

    lax.fori_loop(0, steps, drain, 0)

    def step(i, carry):
        codes = [lst[i * UNROLL + u] for u in range(UNROLL)]
        sums = []
        for u, code in enumerate(codes):
            weights = w[i * (UNROLL // 2) + u // 2][:, (u % 2) * FRAMES:(u % 2 + 1) * FRAMES]
            block = (code >> 21) & 31
            scores = jnp.where(((code >> 20) & 1) == 0, near[block], far[block])
            sums.append(jnp.dot(weights, scores, preferred_element_type=jnp.float32))
        for u, code in enumerate(codes):
            acc[code & 127] += sums[u]
        return carry

    lax.fori_loop(0, steps, step, 0)
    for b in range(QBLOCKS):
        send[b] = acc[b].astype(jnp.bfloat16)


def mix_kernel(got, base, weights, prior, marks, masked, denominator, own_second):
    row = lax.broadcasted_iota(jnp.int32, (FRAMES, CH), 0)
    lane = lax.broadcasted_iota(jnp.int32, (FRAMES, CH), 1)
    pick = (row == lane % FRAMES).astype(jnp.float32)
    for b in range(PART):
        total = base[b, :, :CH]
        for d in range(NY * NX):
            total = total + got[d, b * FRAMES:(b + 1) * FRAMES, :].astype(jnp.float32)
        mass = jnp.sum(got[:, PIECE:SEND, :].astype(jnp.float32), axis=0)[b:b + 1, :]
        column = jnp.sum(pick * mass, axis=1, keepdims=True)
        full = 1.0 + column + base[b, :, CH:]
        denominator[b] = full
        mixed = keep_share * total / full + (1.0 - keep_share) * prior[b].astype(jnp.float32)
        keep = (mixed.astype(jnp.bfloat16).astype(jnp.float32) * marks[b].astype(jnp.float32)).astype(jnp.bfloat16)
        for d in range(NZ):
            masked[d, b] = keep
        own_second[b] = jnp.dot(weights[b], keep, preferred_element_type=jnp.float32)


def last_kernel(got, own_second, denominator, prior, out):
    for b in range(PART):
        total = own_second[b]
        for d in range(NY * NX):
            total = total + got[d, b].astype(jnp.float32)
        mixed = keep_share * total / denominator[b]
        out[b] = (mixed + (1.0 - keep_share) * prior[b].astype(jnp.float32)).astype(jnp.bfloat16)


smem = pl.BlockSpec(memory_space=pltpu.SMEM)
vmem = pl.BlockSpec(memory_space=pltpu.VMEM)
hbm = pl.BlockSpec(memory_space=pl.ANY)
far_memory = pl.BlockSpec(memory_space=pltpu.HBM)


def limit(mebibytes):
    return pltpu.CompilerParams(vmem_limit_bytes=mebibytes * 1024 * 1024)


def body(embeddings, prior_scores, frame_valid, neighbour_ids, neighbour_count, block_home):
    per_list = neighbour_ids.shape[1]
    y, z, c, x = (lax.axis_index(a) for a in ("y", "z", "c", "x"))
    first = x * PART
    piece, turn = pl.pallas_call(
        prep_kernel,
        out_shape=(
            jax.ShapeDtypeStruct((PIECE, WIDE), jnp.bfloat16),
            jax.ShapeDtypeStruct((TURN * FRAMES, FEAT), jnp.bfloat16),
        ),
        in_specs=[hbm, hbm, hbm],
        out_specs=(far_memory, far_memory),
        scratch_shapes=[
            pltpu.VMEM((PART, FRAMES, FEAT), jnp.bfloat16),
            pltpu.VMEM((PART, FRAMES, CH), jnp.bfloat16),
            pltpu.VMEM((ROWS, FRAMES), jnp.int32),
            pltpu.VMEM((PIECE, WIDE), jnp.bfloat16),
            pltpu.SemaphoreType.DMA((PART + 2,)),
            pltpu.SemaphoreType.DMA((PART + TURN,)),
        ],
        compiler_params=limit(59),
    )(embeddings, prior_scores, frame_valid)

    keys = lax.all_gather(piece, ("z", "c"), axis=0, tiled=True)

    embeddings, prior_scores, ids, block_home, piece = lax.optimization_barrier(
        (embeddings, prior_scores, neighbour_ids, block_home, piece)
    )
    prior = lax.dynamic_slice_in_dim(prior_scores, first, PART, 0)
    valid = lax.dynamic_slice_in_dim(frame_valid, first, PART, 0)
    marks = jnp.broadcast_to(valid[:, :, None], prior.shape).astype(jnp.bfloat16)
    target = jnp.take(block_home, ids.reshape(-1), axis=0)
    column = x * per_list + jnp.arange(per_list, dtype=jnp.int32)
    in_list = (column[None, :] < neighbour_count[:, None]).reshape(-1)
    target = jnp.where(in_list, target, -1)
    target = jnp.broadcast_to(target[None, :], (NY * NX, ROWS * per_list))
    target = lax.all_to_all(target, ("y", "x"), split_axis=0, concat_axis=0, tiled=True)

    one, two, three = shift(turn, "y", -1), shift(turn, "y", 2), shift(turn, "y", 1)
    all_units = normalize(embeddings)
    straight = all_units.reshape(NX, PART, FRAMES, FEAT)[:, TURN:].reshape(STRAIGHT * FRAMES, FEAT)
    one, three, straight, target = lax.optimization_barrier((one, three, straight, target))
    behind, ahead = shift(straight, "y", 1), shift(straight, "y", -1)
    rows = (NY - 1) * TURN * FRAMES
    turned = pl.pallas_call(
        join_kernel,
        out_shape=jax.ShapeDtypeStruct((rows, FEAT), jnp.bfloat16),
        in_specs=[hbm] * 3,
        out_specs=hbm,
        scratch_shapes=[pltpu.SemaphoreType.DMA((3,))],
        compiler_params=limit(1),
    )(one, two, three)
    following, leading = shift(turned, "x", -1), shift(turned, "x", 1)
    over = [shift(leading[:rows // 2], "x", 1), shift(following[rows // 2:], "x", -1)]
    turned = [turned, following, *over, leading]

    target = target.reshape(NY, NX, ROWS, per_list)
    source_y = jnp.arange(NY, dtype=jnp.int32)[:, None, None, None]
    source_row = jnp.arange(ROWS, dtype=jnp.int32)[None, None, :, None]
    distance = (source_y - y) % NY
    source = source_y * ROWS + source_row
    wanted = (target >= 0) & (target // 256 == y) & ((target % 16) // PART == x)
    place = (target // 16) % 16
    inner = target % PART
    side = (place % 2) ^ c
    quarter, within = source_row // PART, source_row % PART
    taken = jnp.where(
        distance == 0,
        source_row,
        jnp.where(
            within < TURN,
            Q_TURN + (((quarter - x) % NX) * (NY - 1) + distance - 1) * TURN + within,
            ROWS + (distance - 1) * STRAIGHT + quarter * (PART - TURN) + within - TURN,
        ),
    )
    codes = source | ((place * PART + inner) << 7) | (taken << 13) | (side << 20) | (((place // 2) * PART + inner) << 21)
    codes = jnp.where(wanted, codes, -1).reshape(-1)
    lst = pl.pallas_call(
        list_kernel,
        out_shape=jax.ShapeDtypeStruct((LIST,), jnp.int32),
        in_specs=[smem],
        out_specs=smem,
        scratch_shapes=[pltpu.SMEM((LIST,), jnp.int32)],
        compiler_params=limit(1),
    )(codes)
    half = STRAIGHT * FRAMES // 2
    behind, ahead, lst = lax.optimization_barrier((behind, ahead, lst))
    across = [shift(behind[:half], "y", 1), shift(ahead[half:], "y", -1)]
    own_weights, own_base = pl.pallas_call(
        own_kernel,
        out_shape=(
            jax.ShapeDtypeStruct((PART, FRAMES, FRAMES), jnp.bfloat16),
            jax.ShapeDtypeStruct((PART, FRAMES, 2 * CH), jnp.float32),
        ),
        in_specs=[vmem],
        out_specs=(vmem, vmem),
        compiler_params=limit(4),
    )(piece)

    send, weights = pl.pallas_call(
        first_kernel,
        out_shape=(
            jax.ShapeDtypeStruct((NY * NX, SEND, CH), jnp.bfloat16),
            jax.ShapeDtypeStruct((HELD, FRAMES, 2 * FRAMES), jnp.bfloat16),
        ),
        in_specs=[hbm] * 12,
        out_specs=(far_memory, far_memory),
        scratch_shapes=[
            pltpu.VMEM((QBLOCKS * FRAMES, FEAT), jnp.bfloat16),
            pltpu.VMEM((NZ * NC * PIECE, WIDE), jnp.bfloat16),
            pltpu.VMEM((QBLOCKS + 1, FRAMES, 2 * CH), jnp.float32),
            pltpu.VMEM((NY * NX, SEND, CH), jnp.bfloat16),
            pltpu.VMEM((SLOTS // 2, FRAMES, 2 * FRAMES), jnp.bfloat16),
            pltpu.SMEM((LIST,), jnp.int32),
            pltpu.SemaphoreType.DMA((12,)),
            pltpu.SemaphoreType.DMA,
            pltpu.SemaphoreType.DMA,
            pltpu.SemaphoreType.DMA,
        ],
        compiler_params=limit(58),
    )(lst, keys, all_units.reshape(ROWS * FRAMES, FEAT), ahead, *across, behind, *turned)
    got = lax.all_to_all(send, ("y", "x"), split_axis=0, concat_axis=0, tiled=True)

    masked, denominator, own_second = pl.pallas_call(
        mix_kernel,
        out_shape=(
            jax.ShapeDtypeStruct((NZ, PART, FRAMES, CH), jnp.bfloat16),
            jax.ShapeDtypeStruct((PART, FRAMES, CH), jnp.float32),
            jax.ShapeDtypeStruct((PART, FRAMES, CH), jnp.float32),
        ),
        in_specs=[vmem] * 5,
        out_specs=(vmem,) * 3,
        compiler_params=limit(8),
    )(got, own_base, own_weights, prior, marks)
    near_scores = lax.all_to_all(masked, "z", split_axis=0, concat_axis=0, tiled=True)
    near_scores = near_scores.reshape(NZ * PART, FRAMES, CH)
    far_scores = shift(near_scores, "c", 1)

    send = pl.pallas_call(
        second_kernel,
        out_shape=jax.ShapeDtypeStruct((QBLOCKS, FRAMES, CH), jnp.bfloat16),
        in_specs=[smem, far_memory, vmem, vmem],
        out_specs=vmem,
        scratch_shapes=[
            pltpu.VMEM((QBLOCKS + 1, FRAMES, CH), jnp.float32),
            pltpu.VMEM((SLOTS // 2, FRAMES, 2 * FRAMES), jnp.bfloat16),
            pltpu.SemaphoreType.DMA,
        ],
        compiler_params=limit(16),
    )(lst, weights, near_scores, far_scores)
    got = lax.all_to_all(send, ("y", "x"), split_axis=0, concat_axis=0, tiled=True)
    return pl.pallas_call(
        last_kernel,
        out_shape=jax.ShapeDtypeStruct((PART, FRAMES, CH), jnp.bfloat16),
        in_specs=[vmem] * 4,
        out_specs=vmem,
        compiler_params=limit(8),
    )(got.reshape(NY * NX, PART, FRAMES, CH), own_second, denominator, prior)


def solution(mesh):
    fine = Mesh(mesh.devices.reshape(NY, NZ, NC, NX), ("y", "z", "c", "x"))
    bucket = ("y", "z", "c")
    in_specs = (P(bucket, None, None), P(bucket, None, None), P(bucket, None), P(bucket, "x"), P(bucket), P())
    out_specs = P(("y", "z", "c", "x"), None, None)
    return jax.shard_map(body, mesh=fine, in_specs=in_specs, out_specs=out_specs, check_vma=False)
```

```python
import math

import jax
import jax.numpy as jnp
from jax import lax
from jax.experimental import pallas as pl
from jax.experimental.pallas import tpu as pltpu
from jax.sharding import Mesh
from jax.sharding import PartitionSpec as P

epsilon = 1e-06
keep_share = 0.9

NY, NZ, NC, NX = 4, 8, 2, 4
ROWS = 16
FRAMES = 64
FEAT = 1152
CH = 128
PART = ROWS // NX
TURN = 2
STRAIGHT = NX * (PART - TURN)
QBLOCKS = NY * ROWS
Q_TURN = ROWS + (NY - 1) * STRAIGHT
UNROLL = 8
SLOTS = 528
HELD = 4608
WIDE = FEAT + CH
PIECE = PART * FRAMES
SEND = PIECE + 16
LIST = 640
QUARTERS = 4
PARTS_AT, STEPS_AT = 600, 610
SPARE = QBLOCKS
UNREAL = 1024.0
sharpness = 2.0 * math.sqrt(FEAT)


def shift(value, axis, step):
    size = lax.axis_size(axis)
    return lax.ppermute(value, axis, [(i, (i + step) % size) for i in range(size)])


def normalize(values):
    floats = values.astype(jnp.float32)
    return (floats * lax.rsqrt(jnp.sum(floats * floats, axis=-1, keepdims=True) + epsilon)).astype(jnp.bfloat16)


def prep_kernel(embeddings, prior, marks, piece_out, turn_out, e, p, valid, piece, sems, out_sems):
    first = lax.axis_index("x") * PART
    shared = [
        pltpu.make_async_copy(prior.at[pl.ds(first, PART)], p, sems.at[PART]),
        pltpu.make_async_copy(marks, valid, sems.at[PART + 1]),
    ]
    blocks = [pltpu.make_async_copy(embeddings.at[first + b], e.at[b], sems.at[b]) for b in range(PART)]
    for copy in shared + blocks:
        copy.start()
    for copy in shared:
        copy.wait()
    row = lax.broadcasted_iota(jnp.int32, (FRAMES, FRAMES), 0)
    col = lax.broadcasted_iota(jnp.int32, (FRAMES, FRAMES), 1)
    pick = row == col
    outs = []
    for b in range(PART):
        rows = pl.ds(b * FRAMES, FRAMES)
        real = valid[pl.ds(first + b, 1), :].astype(jnp.float32)
        column = jnp.sum(jnp.where(pick, real, 0.0), axis=1, keepdims=True)
        marked = jnp.where(column > 0.0, p[b].astype(jnp.float32), 2.0 * UNREAL).astype(jnp.bfloat16)
        piece[rows, FEAT:] = marked
        blocks[b].wait()
        piece[rows, :FEAT] = normalize(e[b])
        outs.append(pltpu.make_async_copy(piece.at[rows], piece_out.at[rows], out_sems.at[len(outs)]))
        outs[-1].start()
        if b < TURN:
            units = piece.at[rows, pl.ds(0, FEAT)]
            outs.append(pltpu.make_async_copy(units, turn_out.at[rows], out_sems.at[len(outs)]))
            outs[-1].start()
    for copy in outs:
        copy.wait()


def list_kernel(codes, out, found):
    def eight(i, count):
        for u in range(8):
            code = codes[i * 8 + u]
            found[count] = code
            count = count + jnp.where(code >= 0, 1, 0)
        return count

    count = lax.fori_loop(0, QBLOCKS * 32 // 8, eight, 0)

    def kind_of(code):
        return jnp.where(((code >> 13) & 63) >= Q_TURN, QUARTERS, (code >> 11) & 3)

    def tally(i, counts):
        kind = kind_of(found[i])
        return tuple(n + jnp.where(kind == j, 1, 0) for j, n in enumerate(counts))

    counts = lax.fori_loop(0, count, tally, (0,) * QUARTERS)
    starts = [0]
    for n in counts:
        starts.append(starts[-1] + n)

    def place(i, at):
        code = found[i]
        kind = kind_of(code)
        slot = at[QUARTERS]
        for j in range(QUARTERS):
            slot = jnp.where(kind == j, at[j], slot)
        out[slot] = code
        return tuple(n + jnp.where(kind == j, 1, 0) for j, n in enumerate(at))

    lax.fori_loop(0, count, place, tuple(starts))
    for u in range(UNROLL):
        out[count + u] = SPARE
    for j in range(QUARTERS):
        out[PARTS_AT + j] = starts[j + 1] // UNROLL
    out[STEPS_AT] = (count + UNROLL - 1) // UNROLL


def own_kernel(piece, own_weights, own_base):
    row = lax.broadcasted_iota(jnp.int32, (FRAMES, FRAMES), 0)
    col = lax.broadcasted_iota(jnp.int32, (FRAMES, FRAMES), 1)
    for b in range(PART):
        block = piece[b * FRAMES:(b + 1) * FRAMES, :]
        units = block[:, :FEAT]
        affinity = lax.dot_general(
            units, units, (((1,), (1,)), ((), ())), preferred_element_type=jnp.float32
        )
        weights = jnp.where(row == col, 0.0, jnp.exp(sharpness * affinity)).astype(jnp.bfloat16)
        own_weights[b] = weights
        own_base[b] = jnp.dot(weights, values_of(block[:, FEAT:]), preferred_element_type=jnp.float32)


def values_of(scores):
    floats = scores.astype(jnp.float32)
    real = floats < UNREAL
    return jnp.concatenate(
        [jnp.where(real, floats, 0.0), jnp.where(real, 1.0, 0.0)], axis=1
    ).astype(jnp.bfloat16)


def pairs_copy(source, target, sem, i):
    group = pl.ds(i * (UNROLL // 2), UNROLL // 2)
    return pltpu.make_async_copy(source.at[group], target.at[group], sem)


def join_kernel(*refs):
    parts, out, sems = refs[:3], refs[3], refs[4]
    rows = TURN * FRAMES
    copies = [
        pltpu.make_async_copy(part, out.at[pl.ds(d * rows, rows)], sems.at[d]) for d, part in enumerate(parts)
    ]
    for copy in copies:
        copy.start()
    for copy in copies:
        copy.wait()


def first_kernel(lst_in, keys, *refs):
    queries = refs[:10]
    send_out, w_out, q, k, acc, send, w, lst, sems, w_sem, send_sem, lst_sem = refs[10:]
    lst_copy = pltpu.make_async_copy(lst_in, lst, lst_sem)
    lst_copy.start()
    quarter = k.shape[0] // QUARTERS
    q_copies = []
    at = 0
    for part in queries:
        rows = part.shape[0]
        q_copies.append(pltpu.make_async_copy(part, q.at[pl.ds(at, rows)], sems.at[len(q_copies)]))
        at += rows
    k_copies = [
        pltpu.make_async_copy(
            keys.at[pl.ds(i * quarter, quarter)], k.at[pl.ds(i * quarter, quarter)], sems.at[10 + i]
        )
        for i in range(QUARTERS)
    ]
    straight, turned = q_copies[:5], q_copies[5:]
    for copy in straight + k_copies + turned:
        copy.start()
    acc[...] = jnp.zeros_like(acc)
    lst_copy.wait()
    for copy in straight:
        copy.wait()
    steps = lst[STEPS_AT]

    def step(i, carry):
        codes = [lst[i * UNROLL + u] for u in range(UNROLL)]
        key_rows = [pl.multiple_of(((code >> 7) & 63) * FRAMES, FRAMES) for code in codes]
        query_rows = [pl.multiple_of(((code >> 13) & 63) * FRAMES, FRAMES) for code in codes]
        weights = []
        for query_row, key_row in zip(query_rows, key_rows):
            affinity = lax.dot_general(
                q[pl.ds(query_row, FRAMES), :],
                k[pl.ds(key_row, FRAMES), pl.ds(0, FEAT)],
                (((1,), (1,)), ((), ())),
                preferred_element_type=jnp.float32,
            )
            weights.append(jnp.exp(sharpness * affinity).astype(jnp.bfloat16))
        for u in range(UNROLL // 2):
            w[i * (UNROLL // 2) + u] = jnp.concatenate(weights[2 * u:2 * u + 2], axis=1)
        sums = []
        for u, key_row in enumerate(key_rows):
            values = values_of(k[pl.ds(key_row, FRAMES), pl.ds(FEAT, CH)])
            sums.append(jnp.dot(weights[u], values, preferred_element_type=jnp.float32))
        for u, code in enumerate(codes):
            acc[code & 127] += sums[u]
        pairs_copy(w, w_out, w_sem, i).start()
        return carry

    done = 0
    for j in range(QUARTERS):
        k_copies[j].wait()
        lax.fori_loop(done, lst[PARTS_AT + j], step, 0)
        done = lst[PARTS_AT + j]
    for copy in turned:
        copy.wait()
    lax.fori_loop(done, steps, step, 0)
    row = lax.broadcasted_iota(jnp.int32, (FRAMES, CH), 0)
    lane = lax.broadcasted_iota(jnp.int32, (FRAMES, CH), 1)
    pick = row == lane % FRAMES
    low = lax.broadcasted_iota(jnp.int32, (1, CH), 1) < FRAMES

    def finish(d, carry):
        rows = []
        for b in range(PART):
            block = acc[d * PART + b]
            send[d, b * FRAMES:(b + 1) * FRAMES, :] = block[:, :CH].astype(jnp.bfloat16)
            mass = jnp.sum(jnp.where(pick, block[:, CH:], 0.0), axis=0, keepdims=True)
            coarse = mass.astype(jnp.bfloat16).astype(jnp.float32)
            rows.append(jnp.where(low, coarse, mass - coarse))
        rows.append(jnp.zeros((16 - PART, CH), jnp.float32))
        send[d, PIECE:SEND, :] = jnp.concatenate(rows, axis=0).astype(jnp.bfloat16)
        pltpu.make_async_copy(send.at[d], send_out.at[d], send_sem).start()
        return carry

    lax.fori_loop(0, NY * NX, finish, 0)

    def drain_send(d, carry):
        pltpu.make_async_copy(send.at[d], send_out.at[d], send_sem).wait()
        return carry

    lax.fori_loop(0, NY * NX, drain_send, 0)

    def drain(i, carry):
        pairs_copy(w, w_out, w_sem, i).wait()
        return carry

    lax.fori_loop(0, steps, drain, 0)


def second_kernel(lst, w_in, near, far, send, acc, w, w_sem):
    steps = lst[STEPS_AT]

    def fetch(i, carry):
        pairs_copy(w_in, w, w_sem, i).start()
        return carry

    lax.fori_loop(0, steps, fetch, 0)
    acc[...] = jnp.zeros_like(acc)

    def drain(i, carry):
        pairs_copy(w_in, w, w_sem, i).wait()
        return carry

    lax.fori_loop(0, steps, drain, 0)

    def step(i, carry):
        codes = [lst[i * UNROLL + u] for u in range(UNROLL)]
        sums = []
        for u, code in enumerate(codes):
            weights = w[i * (UNROLL // 2) + u // 2][:, (u % 2) * FRAMES:(u % 2 + 1) * FRAMES]
            block = (code >> 21) & 31
            scores = jnp.where(((code >> 20) & 1) == 0, near[block], far[block])
            sums.append(jnp.dot(weights, scores, preferred_element_type=jnp.float32))
        for u, code in enumerate(codes):
            acc[code & 127] += sums[u]
        return carry

    lax.fori_loop(0, steps, step, 0)
    for b in range(QBLOCKS):
        send[b] = acc[b].astype(jnp.bfloat16)


def mix_kernel(got, base, weights, prior, marks, masked, denominator, own_second):
    row = lax.broadcasted_iota(jnp.int32, (FRAMES, CH), 0)
    lane = lax.broadcasted_iota(jnp.int32, (FRAMES, CH), 1)
    pick = (row == lane % FRAMES).astype(jnp.float32)
    for b in range(PART):
        total = base[b, :, :CH]
        for d in range(NY * NX):
            total = total + got[d, b * FRAMES:(b + 1) * FRAMES, :].astype(jnp.float32)
        mass = jnp.sum(got[:, PIECE:SEND, :].astype(jnp.float32), axis=0)[b:b + 1, :]
        column = jnp.sum(pick * mass, axis=1, keepdims=True)
        full = 1.0 + column + base[b, :, CH:]
        denominator[b] = full
        mixed = keep_share * total / full + (1.0 - keep_share) * prior[b].astype(jnp.float32)
        keep = (mixed.astype(jnp.bfloat16).astype(jnp.float32) * marks[b].astype(jnp.float32)).astype(jnp.bfloat16)
        for d in range(NZ):
            masked[d, b] = keep
        own_second[b] = jnp.dot(weights[b], keep, preferred_element_type=jnp.float32)


def last_kernel(got, own_second, denominator, prior, out):
    for b in range(PART):
        total = own_second[b]
        for d in range(NY * NX):
            total = total + got[d, b].astype(jnp.float32)
        mixed = keep_share * total / denominator[b]
        out[b] = (mixed + (1.0 - keep_share) * prior[b].astype(jnp.float32)).astype(jnp.bfloat16)


smem = pl.BlockSpec(memory_space=pltpu.SMEM)
vmem = pl.BlockSpec(memory_space=pltpu.VMEM)
hbm = pl.BlockSpec(memory_space=pl.ANY)
far_memory = pl.BlockSpec(memory_space=pltpu.HBM)


def limit(mebibytes):
    return pltpu.CompilerParams(vmem_limit_bytes=mebibytes * 1024 * 1024)


def body(embeddings, prior_scores, frame_valid, neighbour_ids, neighbour_count, block_home):
    per_list = neighbour_ids.shape[1]
    y, z, c, x = (lax.axis_index(a) for a in ("y", "z", "c", "x"))
    first = x * PART
    piece, turn = pl.pallas_call(
        prep_kernel,
        out_shape=(
            jax.ShapeDtypeStruct((PIECE, WIDE), jnp.bfloat16),
            jax.ShapeDtypeStruct((TURN * FRAMES, FEAT), jnp.bfloat16),
        ),
        in_specs=[hbm, hbm, hbm],
        out_specs=(far_memory, far_memory),
        scratch_shapes=[
            pltpu.VMEM((PART, FRAMES, FEAT), jnp.bfloat16),
            pltpu.VMEM((PART, FRAMES, CH), jnp.bfloat16),
            pltpu.VMEM((ROWS, FRAMES), jnp.int32),
            pltpu.VMEM((PIECE, WIDE), jnp.bfloat16),
            pltpu.SemaphoreType.DMA((PART + 2,)),
            pltpu.SemaphoreType.DMA((PART + TURN,)),
        ],
        compiler_params=limit(59),
    )(embeddings, prior_scores, frame_valid)

    keys = lax.all_gather(piece, ("z", "c"), axis=0, tiled=True)

    embeddings, prior_scores, ids, block_home, piece = lax.optimization_barrier(
        (embeddings, prior_scores, neighbour_ids, block_home, piece)
    )
    prior = lax.dynamic_slice_in_dim(prior_scores, first, PART, 0)
    valid = lax.dynamic_slice_in_dim(frame_valid, first, PART, 0)
    marks = jnp.broadcast_to(valid[:, :, None], prior.shape).astype(jnp.bfloat16)
    target = jnp.take(block_home, ids.reshape(-1), axis=0)
    column = x * per_list + jnp.arange(per_list, dtype=jnp.int32)
    in_list = (column[None, :] < neighbour_count[:, None]).reshape(-1)
    target = jnp.where(in_list, target, -1)
    target = jnp.broadcast_to(target[None, :], (NY * NX, ROWS * per_list))
    target = lax.all_to_all(target, ("y", "x"), split_axis=0, concat_axis=0, tiled=True)

    one, two, three = shift(turn, "y", -1), shift(turn, "y", 2), shift(turn, "y", 1)
    all_units = normalize(embeddings)
    straight = all_units.reshape(NX, PART, FRAMES, FEAT)[:, TURN:].reshape(STRAIGHT * FRAMES, FEAT)
    one, three, straight, target = lax.optimization_barrier((one, three, straight, target))
    behind, ahead = shift(straight, "y", 1), shift(straight, "y", -1)
    rows = (NY - 1) * TURN * FRAMES
    turned = pl.pallas_call(
        join_kernel,
        out_shape=jax.ShapeDtypeStruct((rows, FEAT), jnp.bfloat16),
        in_specs=[hbm] * 3,
        out_specs=hbm,
        scratch_shapes=[pltpu.SemaphoreType.DMA((3,))],
        compiler_params=limit(1),
    )(one, two, three)
    following, leading = shift(turned, "x", -1), shift(turned, "x", 1)
    over = [shift(leading[:rows // 2], "x", 1), shift(following[rows // 2:], "x", -1)]
    turned = [turned, following, *over, leading]

    target = target.reshape(NY, NX, ROWS, per_list)
    source_y = jnp.arange(NY, dtype=jnp.int32)[:, None, None, None]
    source_row = jnp.arange(ROWS, dtype=jnp.int32)[None, None, :, None]
    distance = (source_y - y) % NY
    source = source_y * ROWS + source_row
    wanted = (target >= 0) & (target // 256 == y) & ((target % 16) // PART == x)
    place = (target // 16) % 16
    inner = target % PART
    side = (place % 2) ^ c
    quarter, within = source_row // PART, source_row % PART
    taken = jnp.where(
        distance == 0,
        source_row,
        jnp.where(
            within < TURN,
            Q_TURN + (((quarter - x) % NX) * (NY - 1) + distance - 1) * TURN + within,
            ROWS + (distance - 1) * STRAIGHT + quarter * (PART - TURN) + within - TURN,
        ),
    )
    codes = source | ((place * PART + inner) << 7) | (taken << 13) | (side << 20) | (((place // 2) * PART + inner) << 21)
    codes = jnp.where(wanted, codes, -1).reshape(-1)
    lst = pl.pallas_call(
        list_kernel,
        out_shape=jax.ShapeDtypeStruct((LIST,), jnp.int32),
        in_specs=[smem],
        out_specs=smem,
        scratch_shapes=[pltpu.SMEM((LIST,), jnp.int32)],
        compiler_params=limit(1),
    )(codes)
    half = STRAIGHT * FRAMES // 2
    behind, ahead, lst = lax.optimization_barrier((behind, ahead, lst))
    across = [shift(behind[:half], "y", 1), shift(ahead[half:], "y", -1)]
    own_weights, own_base = pl.pallas_call(
        own_kernel,
        out_shape=(
            jax.ShapeDtypeStruct((PART, FRAMES, FRAMES), jnp.bfloat16),
            jax.ShapeDtypeStruct((PART, FRAMES, 2 * CH), jnp.float32),
        ),
        in_specs=[vmem],
        out_specs=(vmem, vmem),
        compiler_params=limit(4),
    )(piece)

    send, weights = pl.pallas_call(
        first_kernel,
        out_shape=(
            jax.ShapeDtypeStruct((NY * NX, SEND, CH), jnp.bfloat16),
            jax.ShapeDtypeStruct((HELD, FRAMES, 2 * FRAMES), jnp.bfloat16),
        ),
        in_specs=[hbm] * 12,
        out_specs=(far_memory, far_memory),
        scratch_shapes=[
            pltpu.VMEM((QBLOCKS * FRAMES, FEAT), jnp.bfloat16),
            pltpu.VMEM((NZ * NC * PIECE, WIDE), jnp.bfloat16),
            pltpu.VMEM((QBLOCKS + 1, FRAMES, 2 * CH), jnp.float32),
            pltpu.VMEM((NY * NX, SEND, CH), jnp.bfloat16),
            pltpu.VMEM((SLOTS // 2, FRAMES, 2 * FRAMES), jnp.bfloat16),
            pltpu.SMEM((LIST,), jnp.int32),
            pltpu.SemaphoreType.DMA((14,)),
            pltpu.SemaphoreType.DMA,
            pltpu.SemaphoreType.DMA,
            pltpu.SemaphoreType.DMA,
        ],
        compiler_params=limit(58),
    )(lst, keys, all_units.reshape(ROWS * FRAMES, FEAT), ahead, *across, behind, *turned)
    got = lax.all_to_all(send, ("y", "x"), split_axis=0, concat_axis=0, tiled=True)

    masked, denominator, own_second = pl.pallas_call(
        mix_kernel,
        out_shape=(
            jax.ShapeDtypeStruct((NZ, PART, FRAMES, CH), jnp.bfloat16),
            jax.ShapeDtypeStruct((PART, FRAMES, CH), jnp.float32),
            jax.ShapeDtypeStruct((PART, FRAMES, CH), jnp.float32),
        ),
        in_specs=[vmem] * 5,
        out_specs=(vmem,) * 3,
        compiler_params=limit(8),
    )(got, own_base, own_weights, prior, marks)
    near_scores = lax.all_to_all(masked, "z", split_axis=0, concat_axis=0, tiled=True)
    near_scores = near_scores.reshape(NZ * PART, FRAMES, CH)
    far_scores = shift(near_scores, "c", 1)

    send = pl.pallas_call(
        second_kernel,
        out_shape=jax.ShapeDtypeStruct((QBLOCKS, FRAMES, CH), jnp.bfloat16),
        in_specs=[smem, far_memory, vmem, vmem],
        out_specs=vmem,
        scratch_shapes=[
            pltpu.VMEM((QBLOCKS + 1, FRAMES, CH), jnp.float32),
            pltpu.VMEM((SLOTS // 2, FRAMES, 2 * FRAMES), jnp.bfloat16),
            pltpu.SemaphoreType.DMA,
        ],
        compiler_params=limit(16),
    )(lst, weights, near_scores, far_scores)
    got = lax.all_to_all(send, ("y", "x"), split_axis=0, concat_axis=0, tiled=True)
    return pl.pallas_call(
        last_kernel,
        out_shape=jax.ShapeDtypeStruct((PART, FRAMES, CH), jnp.bfloat16),
        in_specs=[vmem] * 4,
        out_specs=vmem,
        compiler_params=limit(8),
    )(got.reshape(NY * NX, PART, FRAMES, CH), own_second, denominator, prior)


def solution(mesh):
    fine = Mesh(mesh.devices.reshape(NY, NZ, NC, NX), ("y", "z", "c", "x"))
    bucket = ("y", "z", "c")
    in_specs = (P(bucket, None, None), P(bucket, None, None), P(bucket, None), P(bucket, "x"), P(bucket), P())
    out_specs = P(("y", "z", "c", "x"), None, None)
    return jax.shard_map(body, mesh=fine, in_specs=in_specs, out_specs=out_specs, check_vma=False)
```

```python
import math

import jax
import jax.numpy as jnp
from jax import lax
from jax.experimental import pallas as pl
from jax.experimental.pallas import tpu as pltpu
from jax.sharding import Mesh
from jax.sharding import PartitionSpec as P

epsilon = 1e-06
keep_share = 0.9

NY, NZ, NC, NX = 4, 8, 2, 4
ROWS = 16
FRAMES = 64
FEAT = 1152
CH = 128
PART = ROWS // NX
TURN = 2
STRAIGHT = NX * (PART - TURN)
QBLOCKS = NY * ROWS
Q_TURN = ROWS + (NY - 1) * STRAIGHT
UNROLL = 8
SLOTS = 528
HELD = 4608
WIDE = FEAT + CH
PIECE = PART * FRAMES
SEND = PIECE + 16
LIST = 640
QUARTERS = 4
PARTS_AT, STEPS_AT = 600, 610
SPARE = QBLOCKS
UNREAL = 1024.0
sharpness = 2.0 * math.sqrt(FEAT)


def shift(value, axis, step):
    size = lax.axis_size(axis)
    return lax.ppermute(value, axis, [(i, (i + step) % size) for i in range(size)])


def normalize(values):
    floats = values.astype(jnp.float32)
    return (floats * lax.rsqrt(jnp.sum(floats * floats, axis=-1, keepdims=True) + epsilon)).astype(jnp.bfloat16)


def prep_kernel(embeddings, prior, marks, piece_out, turn_out, e, p, valid, piece, sems, out_sems):
    first = lax.axis_index("x") * PART
    shared = [
        pltpu.make_async_copy(prior.at[pl.ds(first, PART)], p, sems.at[PART]),
        pltpu.make_async_copy(marks, valid, sems.at[PART + 1]),
    ]
    blocks = [pltpu.make_async_copy(embeddings.at[first + b], e.at[b], sems.at[b]) for b in range(PART)]
    for copy in shared + blocks:
        copy.start()
    for copy in shared:
        copy.wait()
    row = lax.broadcasted_iota(jnp.int32, (FRAMES, FRAMES), 0)
    col = lax.broadcasted_iota(jnp.int32, (FRAMES, FRAMES), 1)
    pick = row == col
    outs = []
    for b in range(PART):
        rows = pl.ds(b * FRAMES, FRAMES)
        real = valid[pl.ds(first + b, 1), :].astype(jnp.float32)
        column = jnp.sum(jnp.where(pick, real, 0.0), axis=1, keepdims=True)
        marked = jnp.where(column > 0.0, p[b].astype(jnp.float32), 2.0 * UNREAL).astype(jnp.bfloat16)
        piece[rows, FEAT:] = marked
        blocks[b].wait()
        piece[rows, :FEAT] = normalize(e[b])
        outs.append(pltpu.make_async_copy(piece.at[rows], piece_out.at[rows], out_sems.at[len(outs)]))
        outs[-1].start()
        if b < TURN:
            units = piece.at[rows, pl.ds(0, FEAT)]
            outs.append(pltpu.make_async_copy(units, turn_out.at[rows], out_sems.at[len(outs)]))
            outs[-1].start()
    for copy in outs:
        copy.wait()


def list_kernel(codes, out, found):
    def eight(i, count):
        for u in range(8):
            code = codes[i * 8 + u]
            found[count] = code
            count = count + jnp.where(code >= 0, 1, 0)
        return count

    count = lax.fori_loop(0, QBLOCKS * 32 // 8, eight, 0)

    def kind_of(code):
        return jnp.where(((code >> 13) & 63) >= Q_TURN, QUARTERS, (code >> 11) & 3)

    def tally(i, counts):
        kind = kind_of(found[i])
        return tuple(n + jnp.where(kind == j, 1, 0) for j, n in enumerate(counts))

    counts = lax.fori_loop(0, count, tally, (0,) * QUARTERS)
    starts = [0]
    for n in counts:
        starts.append(starts[-1] + n)

    def place(i, at):
        code = found[i]
        kind = kind_of(code)
        slot = at[QUARTERS]
        for j in range(QUARTERS):
            slot = jnp.where(kind == j, at[j], slot)
        out[slot] = code
        return tuple(n + jnp.where(kind == j, 1, 0) for j, n in enumerate(at))

    lax.fori_loop(0, count, place, tuple(starts))
    for u in range(UNROLL):
        out[count + u] = SPARE
    for j in range(QUARTERS):
        out[PARTS_AT + j] = starts[j + 1] // UNROLL
    out[STEPS_AT] = (count + UNROLL - 1) // UNROLL


def own_kernel(piece, own_weights, own_base):
    row = lax.broadcasted_iota(jnp.int32, (FRAMES, FRAMES), 0)
    col = lax.broadcasted_iota(jnp.int32, (FRAMES, FRAMES), 1)
    for b in range(PART):
        block = piece[b * FRAMES:(b + 1) * FRAMES, :]
        units = block[:, :FEAT]
        affinity = lax.dot_general(
            units, units, (((1,), (1,)), ((), ())), preferred_element_type=jnp.float32
        )
        weights = jnp.where(row == col, 0.0, jnp.exp(sharpness * affinity)).astype(jnp.bfloat16)
        own_weights[b] = weights
        own_base[b] = jnp.dot(weights, values_of(block[:, FEAT:]), preferred_element_type=jnp.float32)


def values_of(scores):
    floats = scores.astype(jnp.float32)
    real = floats < UNREAL
    return jnp.concatenate(
        [jnp.where(real, floats, 0.0), jnp.where(real, 1.0, 0.0)], axis=1
    ).astype(jnp.bfloat16)


def pairs_copy(source, target, sem, i):
    group = pl.ds(i * (UNROLL // 2), UNROLL // 2)
    return pltpu.make_async_copy(source.at[group], target.at[group], sem)


def join_kernel(*refs):
    parts, out, sems = refs[:3], refs[3], refs[4]
    rows = TURN * FRAMES
    copies = [
        pltpu.make_async_copy(part, out.at[pl.ds(d * rows, rows)], sems.at[d]) for d, part in enumerate(parts)
    ]
    for copy in copies:
        copy.start()
    for copy in copies:
        copy.wait()


def first_kernel(lst_in, keys, *refs):
    queries = refs[:10]
    send_out, w_out, q, k, acc, send, w, lst, sems, w_sem, send_sem, lst_sem = refs[10:]
    lst_copy = pltpu.make_async_copy(lst_in, lst, lst_sem)
    lst_copy.start()
    quarter = k.shape[0] // QUARTERS
    q_copies = []
    at = 0
    for part in queries:
        rows = part.shape[0]
        q_copies.append(pltpu.make_async_copy(part, q.at[pl.ds(at, rows)], sems.at[len(q_copies)]))
        at += rows
    k_copies = [
        pltpu.make_async_copy(
            keys.at[pl.ds(i * quarter, quarter)], k.at[pl.ds(i * quarter, quarter)], sems.at[10 + i]
        )
        for i in range(QUARTERS)
    ]
    straight, turned = q_copies[:5], q_copies[5:]
    for copy in straight + k_copies + turned:
        copy.start()
    acc[...] = jnp.zeros_like(acc)
    lst_copy.wait()
    for copy in straight:
        copy.wait()
    steps = lst[STEPS_AT]

    def step(i, carry):
        codes = [lst[i * UNROLL + u] for u in range(UNROLL)]
        key_rows = [pl.multiple_of(((code >> 7) & 63) * FRAMES, FRAMES) for code in codes]
        query_rows = [pl.multiple_of(((code >> 13) & 63) * FRAMES, FRAMES) for code in codes]
        weights = []
        for query_row, key_row in zip(query_rows, key_rows):
            affinity = lax.dot_general(
                q[pl.ds(query_row, FRAMES), :],
                k[pl.ds(key_row, FRAMES), pl.ds(0, FEAT)],
                (((1,), (1,)), ((), ())),
                preferred_element_type=jnp.float32,
            )
            weights.append(jnp.exp(sharpness * affinity).astype(jnp.bfloat16))
        for u in range(UNROLL // 2):
            w[i * (UNROLL // 2) + u] = jnp.concatenate(weights[2 * u:2 * u + 2], axis=1)
        sums = []
        for u, key_row in enumerate(key_rows):
            values = values_of(k[pl.ds(key_row, FRAMES), pl.ds(FEAT, CH)])
            sums.append(jnp.dot(weights[u], values, preferred_element_type=jnp.float32))
        for u, code in enumerate(codes):
            acc[code & 127] += sums[u]
        pairs_copy(w, w_out, w_sem, i).start()
        return carry

    done = 0
    for j in range(QUARTERS):
        k_copies[j].wait()
        lax.fori_loop(done, lst[PARTS_AT + j], step, 0)
        done = lst[PARTS_AT + j]
    for copy in turned:
        copy.wait()
    lax.fori_loop(done, steps, step, 0)
    row = lax.broadcasted_iota(jnp.int32, (FRAMES, CH), 0)
    lane = lax.broadcasted_iota(jnp.int32, (FRAMES, CH), 1)
    pick = row == lane % FRAMES
    low = lax.broadcasted_iota(jnp.int32, (1, CH), 1) < FRAMES

    def finish(d, carry):
        rows = []
        for b in range(PART):
            block = acc[d * PART + b]
            send[d, b * FRAMES:(b + 1) * FRAMES, :] = block[:, :CH].astype(jnp.bfloat16)
            mass = jnp.sum(jnp.where(pick, block[:, CH:], 0.0), axis=0, keepdims=True)
            coarse = mass.astype(jnp.bfloat16).astype(jnp.float32)
            rows.append(jnp.where(low, coarse, mass - coarse))
        rows.append(jnp.zeros((16 - PART, CH), jnp.float32))
        send[d, PIECE:SEND, :] = jnp.concatenate(rows, axis=0).astype(jnp.bfloat16)
        pltpu.make_async_copy(send.at[d], send_out.at[d], send_sem).start()
        return carry

    lax.fori_loop(0, NY * NX, finish, 0)

    def drain_send(d, carry):
        pltpu.make_async_copy(send.at[d], send_out.at[d], send_sem).wait()
        return carry

    lax.fori_loop(0, NY * NX, drain_send, 0)

    def drain(i, carry):
        pairs_copy(w, w_out, w_sem, i).wait()
        return carry

    lax.fori_loop(0, steps, drain, 0)


def second_kernel(lst, w_in, near, far, send, acc, w, w_sem):
    steps = lst[STEPS_AT]

    def fetch(i, carry):
        pairs_copy(w_in, w, w_sem, i).start()
        return carry

    lax.fori_loop(0, steps, fetch, 0)
    acc[...] = jnp.zeros_like(acc)

    def drain(i, carry):
        pairs_copy(w_in, w, w_sem, i).wait()
        return carry

    lax.fori_loop(0, steps, drain, 0)

    def step(i, carry):
        codes = [lst[i * UNROLL + u] for u in range(UNROLL)]
        sums = []
        for u, code in enumerate(codes):
            weights = w[i * (UNROLL // 2) + u // 2][:, (u % 2) * FRAMES:(u % 2 + 1) * FRAMES]
            block = (code >> 21) & 31
            scores = jnp.where(((code >> 20) & 1) == 0, near[block], far[block])
            sums.append(jnp.dot(weights, scores, preferred_element_type=jnp.float32))
        for u, code in enumerate(codes):
            acc[code & 127] += sums[u]
        return carry

    lax.fori_loop(0, steps, step, 0)
    for b in range(QBLOCKS):
        send[b] = acc[b].astype(jnp.bfloat16)


def mix_kernel(got, base, weights, prior, marks, masked, denominator, own_second):
    row = lax.broadcasted_iota(jnp.int32, (FRAMES, CH), 0)
    lane = lax.broadcasted_iota(jnp.int32, (FRAMES, CH), 1)
    pick = (row == lane % FRAMES).astype(jnp.float32)
    for b in range(PART):
        total = base[b, :, :CH]
        for d in range(NY * NX):
            total = total + got[d, b * FRAMES:(b + 1) * FRAMES, :].astype(jnp.float32)
        mass = jnp.sum(got[:, PIECE:SEND, :].astype(jnp.float32), axis=0)[b:b + 1, :]
        column = jnp.sum(pick * mass, axis=1, keepdims=True)
        full = 1.0 + column + base[b, :, CH:]
        denominator[b] = full
        mixed = keep_share * total / full + (1.0 - keep_share) * prior[b].astype(jnp.float32)
        keep = (mixed.astype(jnp.bfloat16).astype(jnp.float32) * marks[b].astype(jnp.float32)).astype(jnp.bfloat16)
        for d in range(NZ):
            masked[d, b] = keep
        own_second[b] = jnp.dot(weights[b], keep, preferred_element_type=jnp.float32)


def last_kernel(got, own_second, denominator, prior, out):
    for b in range(PART):
        total = own_second[b]
        for d in range(NY * NX):
            total = total + got[d, b].astype(jnp.float32)
        mixed = keep_share * total / denominator[b]
        out[b] = (mixed + (1.0 - keep_share) * prior[b].astype(jnp.float32)).astype(jnp.bfloat16)


smem = pl.BlockSpec(memory_space=pltpu.SMEM)
vmem = pl.BlockSpec(memory_space=pltpu.VMEM)
hbm = pl.BlockSpec(memory_space=pl.ANY)
far_memory = pl.BlockSpec(memory_space=pltpu.HBM)


def limit(mebibytes):
    return pltpu.CompilerParams(vmem_limit_bytes=mebibytes * 1024 * 1024)


def body(embeddings, prior_scores, frame_valid, neighbour_ids, neighbour_count, block_home):
    per_list = neighbour_ids.shape[1]
    y, z, c, x = (lax.axis_index(a) for a in ("y", "z", "c", "x"))
    first = x * PART
    piece, turn = pl.pallas_call(
        prep_kernel,
        out_shape=(
            jax.ShapeDtypeStruct((PIECE, WIDE), jnp.bfloat16),
            jax.ShapeDtypeStruct((TURN * FRAMES, FEAT), jnp.bfloat16),
        ),
        in_specs=[hbm, hbm, hbm],
        out_specs=(far_memory, far_memory),
        scratch_shapes=[
            pltpu.VMEM((PART, FRAMES, FEAT), jnp.bfloat16),
            pltpu.VMEM((PART, FRAMES, CH), jnp.bfloat16),
            pltpu.VMEM((ROWS, FRAMES), jnp.int32),
            pltpu.VMEM((PIECE, WIDE), jnp.bfloat16),
            pltpu.SemaphoreType.DMA((PART + 2,)),
            pltpu.SemaphoreType.DMA((PART + TURN,)),
        ],
        compiler_params=limit(59),
    )(embeddings, prior_scores, frame_valid)

    keys = lax.all_gather(piece, ("z", "c"), axis=0, tiled=True)

    embeddings, prior_scores, ids, block_home, piece = lax.optimization_barrier(
        (embeddings, prior_scores, neighbour_ids, block_home, piece)
    )
    prior = lax.dynamic_slice_in_dim(prior_scores, first, PART, 0)
    valid = lax.dynamic_slice_in_dim(frame_valid, first, PART, 0)
    marks = jnp.broadcast_to(valid[:, :, None], prior.shape).astype(jnp.bfloat16)
    target = jnp.take(block_home, ids.reshape(-1), axis=0)
    column = x * per_list + jnp.arange(per_list, dtype=jnp.int32)
    in_list = (column[None, :] < neighbour_count[:, None]).reshape(-1)
    target = jnp.where(in_list, target, -1)
    target = jnp.broadcast_to(target[None, :], (NY * NX, ROWS * per_list))
    target = lax.all_to_all(target, ("y", "x"), split_axis=0, concat_axis=0, tiled=True)

    one, two, three = shift(turn, "y", -1), shift(turn, "y", 2), shift(turn, "y", 1)
    all_units = normalize(embeddings)
    straight = all_units.reshape(NX, PART, FRAMES, FEAT)[:, TURN:].reshape(STRAIGHT * FRAMES, FEAT)
    one, three, straight, target = lax.optimization_barrier((one, three, straight, target))
    behind, ahead = shift(straight, "y", 1), shift(straight, "y", -1)
    rows = (NY - 1) * TURN * FRAMES
    turned = pl.pallas_call(
        join_kernel,
        out_shape=jax.ShapeDtypeStruct((rows, FEAT), jnp.bfloat16),
        in_specs=[hbm] * 3,
        out_specs=hbm,
        scratch_shapes=[pltpu.SemaphoreType.DMA((3,))],
        compiler_params=limit(1),
    )(one, two, three)
    following, leading = shift(turned, "x", -1), shift(turned, "x", 1)
    over = [shift(leading[:rows // 2], "x", 1), shift(following[rows // 2:], "x", -1)]
    turned = [turned, following, *over, leading]

    target = target.reshape(NY, NX, ROWS, per_list)
    source_y = jnp.arange(NY, dtype=jnp.int32)[:, None, None, None]
    source_row = jnp.arange(ROWS, dtype=jnp.int32)[None, None, :, None]
    distance = (source_y - y) % NY
    source = source_y * ROWS + source_row
    wanted = (target >= 0) & (target // 256 == y) & ((target % 16) // PART == x)
    place = (target // 16) % 16
    inner = target % PART
    side = (place % 2) ^ c
    quarter, within = source_row // PART, source_row % PART
    taken = jnp.where(
        distance == 0,
        source_row,
        jnp.where(
            within < TURN,
            Q_TURN + (((quarter - x) % NX) * (NY - 1) + distance - 1) * TURN + within,
            ROWS + (distance - 1) * STRAIGHT + quarter * (PART - TURN) + within - TURN,
        ),
    )
    codes = source | ((place * PART + inner) << 7) | (taken << 13) | (side << 20) | (((place // 2) * PART + inner) << 21)
    codes = jnp.where(wanted, codes, -1).reshape(-1)
    lst = pl.pallas_call(
        list_kernel,
        out_shape=jax.ShapeDtypeStruct((LIST,), jnp.int32),
        in_specs=[smem],
        out_specs=smem,
        scratch_shapes=[pltpu.SMEM((LIST,), jnp.int32)],
        compiler_params=limit(1),
    )(codes)
    half = STRAIGHT * FRAMES // 2
    own_weights, own_base = pl.pallas_call(
        own_kernel,
        out_shape=(
            jax.ShapeDtypeStruct((PART, FRAMES, FRAMES), jnp.bfloat16),
            jax.ShapeDtypeStruct((PART, FRAMES, 2 * CH), jnp.float32),
        ),
        in_specs=[vmem],
        out_specs=(vmem, vmem),
        compiler_params=limit(4),
    )(piece)
    behind, ahead, lst, own_weights, own_base, prior, marks = lax.optimization_barrier(
        (behind, ahead, lst, own_weights, own_base, prior, marks)
    )
    across = [shift(behind[:half], "y", 1), shift(ahead[half:], "y", -1)]

    send, weights = pl.pallas_call(
        first_kernel,
        out_shape=(
            jax.ShapeDtypeStruct((NY * NX, SEND, CH), jnp.bfloat16),
            jax.ShapeDtypeStruct((HELD, FRAMES, 2 * FRAMES), jnp.bfloat16),
        ),
        in_specs=[hbm] * 12,
        out_specs=(far_memory, far_memory),
        scratch_shapes=[
            pltpu.VMEM((QBLOCKS * FRAMES, FEAT), jnp.bfloat16),
            pltpu.VMEM((NZ * NC * PIECE, WIDE), jnp.bfloat16),
            pltpu.VMEM((QBLOCKS + 1, FRAMES, 2 * CH), jnp.float32),
            pltpu.VMEM((NY * NX, SEND, CH), jnp.bfloat16),
            pltpu.VMEM((SLOTS // 2, FRAMES, 2 * FRAMES), jnp.bfloat16),
            pltpu.SMEM((LIST,), jnp.int32),
            pltpu.SemaphoreType.DMA((14,)),
            pltpu.SemaphoreType.DMA,
            pltpu.SemaphoreType.DMA,
            pltpu.SemaphoreType.DMA,
        ],
        compiler_params=limit(58),
    )(lst, keys, all_units.reshape(ROWS * FRAMES, FEAT), ahead, *across, behind, *turned)
    got = lax.all_to_all(send, ("y", "x"), split_axis=0, concat_axis=0, tiled=True)

    masked, denominator, own_second = pl.pallas_call(
        mix_kernel,
        out_shape=(
            jax.ShapeDtypeStruct((NZ, PART, FRAMES, CH), jnp.bfloat16),
            jax.ShapeDtypeStruct((PART, FRAMES, CH), jnp.float32),
            jax.ShapeDtypeStruct((PART, FRAMES, CH), jnp.float32),
        ),
        in_specs=[vmem] * 5,
        out_specs=(vmem,) * 3,
        compiler_params=limit(8),
    )(got, own_base, own_weights, prior, marks)
    near_scores = lax.all_to_all(masked, "z", split_axis=0, concat_axis=0, tiled=True)
    near_scores = near_scores.reshape(NZ * PART, FRAMES, CH)
    far_scores = shift(near_scores, "c", 1)

    send = pl.pallas_call(
        second_kernel,
        out_shape=jax.ShapeDtypeStruct((QBLOCKS, FRAMES, CH), jnp.bfloat16),
        in_specs=[smem, far_memory, vmem, vmem],
        out_specs=vmem,
        scratch_shapes=[
            pltpu.VMEM((QBLOCKS + 1, FRAMES, CH), jnp.float32),
            pltpu.VMEM((SLOTS // 2, FRAMES, 2 * FRAMES), jnp.bfloat16),
            pltpu.SemaphoreType.DMA,
        ],
        compiler_params=limit(16),
    )(lst, weights, near_scores, far_scores)
    got = lax.all_to_all(send, ("y", "x"), split_axis=0, concat_axis=0, tiled=True)
    return pl.pallas_call(
        last_kernel,
        out_shape=jax.ShapeDtypeStruct((PART, FRAMES, CH), jnp.bfloat16),
        in_specs=[vmem] * 4,
        out_specs=vmem,
        compiler_params=limit(8),
    )(got.reshape(NY * NX, PART, FRAMES, CH), own_second, denominator, prior)


def solution(mesh):
    fine = Mesh(mesh.devices.reshape(NY, NZ, NC, NX), ("y", "z", "c", "x"))
    bucket = ("y", "z", "c")
    in_specs = (P(bucket, None, None), P(bucket, None, None), P(bucket, None), P(bucket, "x"), P(bucket), P())
    out_specs = P(("y", "z", "c", "x"), None, None)
    return jax.shard_map(body, mesh=fine, in_specs=in_specs, out_specs=out_specs, check_vma=False)
```
